32 devices in a mesh: dp: 16 (over z, y, core), tensor: 2 (over x).
Axes of the slice: x: 2, y: 2, z: 4, core: 2. Of those that a mesh axis runs over, the one named last changes fastest.
Arguments:
- tokens: bfloat16 [16384, 1024], P(('dp', 'tensor')), may hold values from -6 to 6
- segments: int32 [16, 1024], P('dp'), may hold values from 0 to 2, as said below
- w_qkv: bfloat16 [1024, 3072], P(None, 'tensor'), may hold values from -0.1875 to 0.1875
- b_qv: bfloat16 [2048], P('tensor'), may hold values from -3 to 3
- w_out: bfloat16 [1024, 1024], P('tensor'), may hold values from -0.75 to 0.75
- b_out: bfloat16 [1024], replicated, may hold values from -2 to 2
- w_up: bfloat16 [1024, 4096], P(None, 'tensor'), may hold values from -0.1875 to 0.1875
- b_up: bfloat16 [4096], P('tensor'), may hold values from -3 to 3
- w_down: bfloat16 [4096, 1024], P('tensor'), may hold values from -0.09375 to 0.09375
- b_down: bfloat16 [1024], replicated, may hold values from -2 to 2
- gain_one: bfloat16 [1024], replicated, may hold values from 0.099609375 to 1.8984375
- shift_one: bfloat16 [1024], replicated, may hold values from -2 to 2
- gain_two: bfloat16 [1024], replicated, may hold values from 0.099609375 to 1.8984375
- shift_two: bfloat16 [1024], replicated, may hold values from -2 to 2
- cotangent: bfloat16 [16384, 1024], P(('dp', 'tensor')), may hold values from -6 to 6
Outputs:
- layer_out: bfloat16 [16384, 1024], P(('dp', 'tensor'))
- input_grad: bfloat16 [16384, 1024], P(('dp', 'tensor'))
- grad_w_qkv: float32 [1024, 3072], P('dp', 'tensor')
- grad_b_qv: float32 [2048], P('tensor')
- grad_w_out: float32 [1024, 1024], P('tensor', 'dp')
- grad_b_out: float32 [1024], replicated
- grad_w_up: float32 [1024, 4096], P('dp', 'tensor')
- grad_b_up: float32 [4096], P('tensor')
- grad_w_down: float32 [4096, 1024], P('tensor', 'dp')
- grad_b_down: float32 [1024], replicated
- grad_gain_one: float32 [1024], replicated
- grad_shift_one: float32 [1024], replicated
- grad_gain_two: float32 [1024], replicated
- grad_shift_two: float32 [1024], replicated
The draws below stay inside these ranges and needn't reach their ends.
Inputs may be any that keep to these rules, and one draw needn't show every extreme that they name: `segments`: along each sequence the numbers never fall.
All inputs are finite; a program needn't handle non-finite values.
Results may differ from the reference program's by a relative error of at most 0.02.
Values may be sent and summed in bfloat16 or wider, within the bound.
No kernel may reach another device: no remote copies, remote signals or barrier semaphores. Data moves between devices by JAX's collectives and lax.ppermute only.
A program may use at most 256 MiB of HBM per device.

```python
import jax
import jax.numpy as jnp
from jax import lax

D = 1024
HEADS = 16
HEAD_DIM = 64
FF = 4096
LEN = 1024
SEQUENCES = 16
TOKENS = 16384
SHARD = 512


def draw_segments(key, part):
    key = jax.random.fold_in(key, 11)
    key_start, key_end = jax.random.split(key, 2)
    starts = jax.random.randint(key_start, (SEQUENCES, 1), 1, SHARD)
    ends = jax.random.randint(key_end, (SEQUENCES, 1), LEN - SHARD + 1, LEN)
    place = lax.iota(jnp.int32, LEN)[None, :]
    first_part = (place >= starts).astype(jnp.int32)
    last_part = (place >= ends).astype(jnp.int32)
    return first_part + last_part


def levels(own_key, shape, cuts, least, high):
    loudness, own = 1.0, jax.random.fold_in(own_key, 6)
    for dim, parts in cuts:
        draws = jnp.exp(jax.random.uniform(jax.random.fold_in(own, dim), (parts,), jnp.float32, least / len(cuts), high / len(cuts)))
        loudness = loudness * jnp.repeat(draws, shape[dim] // parts).reshape([-1 if axis == dim else 1 for axis in range(len(shape))])
    return loudness


def normal_values(stream_key, extent, scale, limit, cuts=(), held_as=jnp.bfloat16):
    entries = scale * jax.random.normal(stream_key, extent, jnp.float32)
    if cuts:
        entries = entries * levels(stream_key, extent, cuts, -0.22, 0.18)
    return jnp.clip(entries, -limit, limit).astype(held_as)


def setup_inputs(seed: int = 0) -> dict:
    key_list = jax.random.split(jax.random.key(seed), 16)
    tokens = normal_values(key_list[0], (TOKENS, D), 1.0, 6.0, ((0, 32),))
    segments = draw_segments(jax.random.fold_in(key_list[15], 71), 0)
    w_qkv = normal_values(key_list[2], (D, 3 * D), D ** -0.5, 0.1875, ((1, 2),))
    b_qv = normal_values(key_list[3], (2 * D,), 0.5, 3.0, ((0, 2),))
    w_out = normal_values(key_list[4], (D, D), (D // 16) ** -0.5, 0.75, ((0, 2),))
    b_out = normal_values(key_list[5], (D,), 0.3, 2.0)
    w_up = normal_values(key_list[6], (D, FF), D ** -0.5, 0.1875, ((1, 2),))
    b_up = normal_values(key_list[7], (FF,), 0.5, 3.0, ((0, 2),))
    w_down = normal_values(key_list[8], (FF, D), FF ** -0.5, 0.09375, ((0, 2),))
    b_down = normal_values(key_list[9], (D,), 0.3, 2.0)
    gain_one = jnp.clip(1.0 + 0.18 * jax.random.normal(key_list[10], (D,), jnp.float32), 0.099609375, 1.8984375).astype(jnp.bfloat16)
    shift_one = normal_values(key_list[11], (D,), 0.3, 2.0)
    gain_two = jnp.clip(1.0 + 0.18 * jax.random.normal(key_list[12], (D,), jnp.float32), 0.099609375, 1.8984375).astype(jnp.bfloat16)
    shift_two = normal_values(key_list[13], (D,), 0.3, 2.0)
    cotangent = normal_values(key_list[14], (TOKENS, D), 1.0, 6.0, ((0, 32),))
    return {"tokens": tokens, "segments": segments, "w_qkv": w_qkv, "b_qv": b_qv, "w_out": w_out, "b_out": b_out, "w_up": w_up, "b_up": b_up, "w_down": w_down, "b_down": b_down, "gain_one": gain_one, "shift_one": shift_one, "gain_two": gain_two, "shift_two": shift_two, "cotangent": cotangent}


norm_eps = 1e-05
masked_fill = -1e+30
highest = lax.Precision.HIGHEST

@jax.custom_vjp
def low(v):
    return lax.optimization_barrier(v.astype(jnp.bfloat16)).astype(jnp.float32)

@jax.custom_vjp
def low_back(v):
    return v

def low_keep(v):
    return (low(v), None)

def low_pass(kept, grad):
    return (grad,)

def back_keep(v):
    return (v, None)

def back_low(kept, grad):
    return (low(grad),)
low.defvjp(low_keep, low_pass)
low_back.defvjp(back_keep, back_low)

def layer_norm(values, gain, shift):
    row_mean = lax.optimization_barrier(jnp.mean(values, axis=-1, keepdims=True))
    centered = values - row_mean
    row_var = lax.optimization_barrier(jnp.mean(centered * centered, axis=-1, keepdims=True))
    return centered * lax.rsqrt(row_var + norm_eps) * gain + shift

def forward(weights, tokens, segment):
    w_qkv, b_qv, w_out, b_out, w_up, b_up, w_down, b_down, gain_one, shift_one, gain_two, shift_two = weights
    length = tokens.shape[0]
    normed_one = low(layer_norm(tokens, gain_one, shift_one))
    joined = jnp.dot(normed_one, w_qkv, precision=highest).reshape(length, HEADS, 3, HEAD_DIM)
    bias_pair = b_qv.reshape(HEADS, 2, HEAD_DIM)
    query = low_back(low(joined[:, :, 0] + bias_pair[:, 0]))
    keys = low_back(low(joined[:, :, 1]))
    values = low_back(low(joined[:, :, 2] + bias_pair[:, 1]))
    place = jnp.arange(length)
    distance = (place[:, None] - place[None, :]).astype(jnp.float32)
    allowed = (segment[:, None] == segment[None, :]) & (distance >= 0)
    slopes = 2.0 ** (-8.0 * (jnp.arange(HEADS) + 1) / HEADS)
    scores = jnp.einsum('qhd,khd->hqk', query, keys, precision=highest) * HEAD_DIM ** (-0.5)
    scores = low_back(jnp.where(allowed[None], scores - slopes[:, None, None] * distance[None], masked_fill))
    top = lax.optimization_barrier(jnp.max(scores, axis=2, keepdims=True))
    log_total = top + jnp.log(lax.optimization_barrier(jnp.sum(jnp.exp(scores - top), axis=2, keepdims=True)))
    probs = jnp.exp(scores - log_total)
    mixed = jnp.einsum('hqk,khd->qhd', low(probs), values, precision=highest)
    mixed = low_back(low(mixed)).reshape(length, HEADS * HEAD_DIM)
    resid = tokens + low_back(jnp.dot(mixed, w_out, precision=highest)) + b_out
    normed_two = low(layer_norm(resid, gain_two, shift_two))
    pre_act = low_back(jnp.dot(normed_two, w_up, precision=highest) + b_up)
    hidden = low(jax.nn.gelu(pre_act, approximate=True))
    return resid + jnp.dot(hidden, w_down, precision=highest) + b_down

def reference(tokens, segments, w_qkv, b_qv, w_out, b_out, w_up, b_up, w_down, b_down, gain_one, shift_one, gain_two, shift_two, cotangent):
    weights = tuple((item.astype(jnp.float32) for item in (w_qkv, b_qv, w_out, b_out, w_up, b_up, w_down, b_down, gain_one, shift_one, gain_two, shift_two)))
    count = segments.shape[0]
    length = segments.shape[1]
    width = tokens.shape[1]
    seq_tokens = tokens.astype(jnp.float32).reshape(count, length, width)
    seq_seed = cotangent.astype(jnp.float32).reshape(count, length, width)

    def one_sequence(totals, inputs):
        rows, segment, seed_grad = inputs

        def apply_layer(params, values):
            return forward(params, values, segment)
        result, pullback = jax.vjp(apply_layer, weights, rows)
        grads, row_grad = pullback(seed_grad)
        totals = jax.tree.map(jnp.add, totals, grads)
        return (totals, (result.astype(jnp.bfloat16), row_grad.astype(jnp.bfloat16)))
    start = jax.tree.map(jnp.zeros_like, weights)
    totals, (outputs, input_grads) = lax.scan(one_sequence, start, (seq_tokens, segments, seq_seed))
    return (outputs.reshape(count * length, width), input_grads.reshape(count * length, width), totals[0], totals[1], totals[2], totals[3], totals[4], totals[5], totals[6], totals[7], totals[8], totals[9], totals[10], totals[11])
```

```python
from functools import partial

import jax
import jax.numpy as jnp
from jax import lax
from jax.experimental import pallas as pl
from jax.experimental.pallas import tpu as pltpu
from jax.sharding import PartitionSpec as P

HEADS = 16
HEAD_DIM = 64


norm_eps = 1e-05
masked_fill = -1e30


def layer_norm(values, gain, shift):
    row_mean = jnp.mean(values, axis=-1, keepdims=True)
    centered = values - row_mean
    row_var = jnp.mean(centered * centered, axis=-1, keepdims=True)
    return centered * lax.rsqrt(row_var + norm_eps) * gain + shift


def contract_rows(left, right):
    return lax.dot_general(
        left, right, (((0,), (0,)), ((), ())), preferred_element_type=jnp.float32
    )


def contract_cols(left, right):
    return lax.dot_general(
        left, right, (((1,), (1,)), ((), ())), preferred_element_type=jnp.float32
    )


def spread_slots(local, rank, parts):
    slots = (lax.iota(jnp.int32, parts) == rank).astype(jnp.float32)
    return (slots[:, None] * local[None, :]).reshape(-1)


def masked_scores(query, keys, segment, first, slopes):
    scale = keys.shape[2] ** (-0.5)
    raw = jnp.einsum("qhd,khd->hqk", query, keys, preferred_element_type=jnp.float32) * scale
    rows_at = first + lax.iota(jnp.int32, query.shape[0])
    cols_at = lax.iota(jnp.int32, keys.shape[0])
    distance = (rows_at[:, None] - cols_at[None, :]).astype(jnp.float32)
    seg_rows = segment[first : first + query.shape[0]]
    allowed = (seg_rows[:, None] == segment[None, :]) & (distance >= 0)
    return jnp.where(allowed[None], raw - slopes[:, None, None] * distance[None], masked_fill)


def attend_forward(inputs, slopes, block):
    query, keys, values, segment = inputs
    outputs = []
    totals = []
    for first in range(0, keys.shape[0], block):
        scores = masked_scores(query[first : first + block], keys, segment, first, slopes)
        top = jnp.max(scores, axis=2, keepdims=True)
        log_total = top + jnp.log(jnp.sum(jnp.exp(scores - top), axis=2, keepdims=True))
        probs = jnp.exp(scores - log_total).astype(jnp.bfloat16)
        outputs.append(
            jnp.einsum("hqk,khd->qhd", probs, values, preferred_element_type=jnp.float32)
        )
        totals.append(log_total)
    return (jnp.concatenate(outputs, 0).astype(jnp.bfloat16), jnp.concatenate(totals, 1))


def attend_backward(inputs, slopes, block):
    query, keys, values, segment, log_total, grad_mixed = inputs
    scale = keys.shape[2] ** (-0.5)
    grad_keys = jnp.zeros(keys.shape, jnp.float32)
    grad_values = jnp.zeros(values.shape, jnp.float32)
    grad_query = []
    for first in range(0, keys.shape[0], block):
        rows = query[first : first + block]
        grad_rows = grad_mixed[first : first + block]
        scores = masked_scores(rows, keys, segment, first, slopes)
        probs = jnp.exp(scores - log_total[:, first : first + block])
        grad_probs = jnp.einsum(
            "qhd,khd->hqk", grad_rows, values, preferred_element_type=jnp.float32
        )
        inner = jnp.sum(probs * grad_probs, axis=2, keepdims=True)
        grad_scores = (probs * (grad_probs - inner)).astype(jnp.bfloat16)
        grad_query.append(
            jnp.einsum("hqk,khd->qhd", grad_scores, keys, preferred_element_type=jnp.float32)
            * scale
        )
        grad_keys = (
            grad_keys
            + jnp.einsum("hqk,qhd->khd", grad_scores, rows, preferred_element_type=jnp.float32)
            * scale
        )
        grad_values = grad_values + jnp.einsum(
            "hqk,qhd->khd",
            probs.astype(jnp.bfloat16),
            grad_rows,
            preferred_element_type=jnp.float32,
        )
    grad_query = jnp.concatenate(grad_query, 0)
    return jnp.stack((grad_query, grad_keys, grad_values), axis=2).astype(jnp.bfloat16)


def body(
    tokens,
    segments,
    w_qkv,
    b_qv,
    w_out,
    b_out,
    w_up,
    b_up,
    w_down,
    b_down,
    gain_one,
    shift_one,
    gain_two,
    shift_two,
    cotangent,
):
    rank = lax.axis_index("tensor")
    parts = lax.axis_size("tensor")
    count, length = segments.shape
    head_dim = HEAD_DIM
    local_heads = w_qkv.shape[1] // (3 * head_dim)
    block = length // 2
    rows_total = count * length
    local_rows = tokens.shape[0]
    head_index = rank * local_heads + lax.iota(jnp.int32, local_heads)
    slopes = 2.0 ** (-8.0 * (head_index + 1).astype(jnp.float32) / HEADS)
    gain_one_f = gain_one.astype(jnp.float32)
    shift_one_f = shift_one.astype(jnp.float32)
    gain_two_f = gain_two.astype(jnp.float32)
    shift_two_f = shift_two.astype(jnp.float32)
    source = tokens.astype(jnp.float32)
    normed_one = layer_norm(source, gain_one_f, shift_one_f).astype(jnp.bfloat16)
    rows_one = lax.all_gather(normed_one, "tensor", axis=0, tiled=True)
    joined = jnp.dot(rows_one, w_qkv, preferred_element_type=jnp.float32).reshape(
        count, length, local_heads, 3, head_dim
    )
    bias_pair = b_qv.astype(jnp.float32).reshape(local_heads, 2, head_dim)
    query = (joined[:, :, :, 0] + bias_pair[:, 0]).astype(jnp.bfloat16)
    keys = joined[:, :, :, 1].astype(jnp.bfloat16)
    values = (joined[:, :, :, 2] + bias_pair[:, 1]).astype(jnp.bfloat16)
    mixed, log_total = lax.map(
        partial(attend_forward, slopes=slopes, block=block), (query, keys, values, segments)
    )
    mixed = mixed.reshape(rows_total, local_heads * head_dim)
    attn_part = lax.psum_scatter(
        jnp.dot(
            lax.slice_in_dim(mixed, 0, local_rows * lax.axis_size("tensor"), axis=0),
            w_out,
            preferred_element_type=jnp.float32,
        ).astype(jnp.bfloat16),
        "tensor",
        scatter_dimension=0,
        tiled=True,
    ).astype(jnp.float32)
    resid = source + attn_part + b_out.astype(jnp.float32)
    normed_two = layer_norm(resid, gain_two_f, shift_two_f).astype(jnp.bfloat16)
    rows_two = lax.all_gather(normed_two, "tensor", axis=0, tiled=True)
    pre_act = jnp.dot(rows_two, w_up, preferred_element_type=jnp.float32) + b_up.astype(jnp.float32)
    hidden = jax.nn.gelu(pre_act, approximate=True).astype(jnp.bfloat16)
    mlp_part = lax.psum_scatter(
        jnp.dot(
            lax.slice_in_dim(hidden, 0, local_rows * lax.axis_size("tensor"), axis=0),
            w_down,
            preferred_element_type=jnp.float32,
        ).astype(jnp.bfloat16),
        "tensor",
        scatter_dimension=0,
        tiled=True,
    ).astype(jnp.float32)
    layer_out = resid + mlp_part + b_down.astype(jnp.float32)
    piece = lax.all_gather(cotangent, "tensor", axis=0, tiled=True)
    start = jnp.int32(0)
    grad_down = jnp.zeros((hidden.shape[1], cotangent.shape[1]), jnp.float32)
    grad_hidden = jnp.zeros(hidden.shape, jnp.float32)
    grad_down = grad_down + contract_rows(
        lax.dynamic_slice_in_dim(hidden, start, piece.shape[0], 0), piece
    )
    grad_hidden = lax.dynamic_update_slice_in_dim(
        grad_hidden, contract_cols(piece, w_down), start, 0
    )
    grad_down, grad_hidden = (grad_down, grad_hidden)
    unused, gelu_pull = jax.vjp(partial(jax.nn.gelu, approximate=True), pre_act)
    grad_pre = gelu_pull(grad_hidden)[0].astype(jnp.bfloat16)
    grad_up = contract_rows(rows_two, grad_pre)
    grad_b_up = jnp.sum(grad_pre.astype(jnp.float32), axis=0)
    grad_normed_two = lax.psum_scatter(
        contract_cols(
            lax.slice_in_dim(grad_pre, 0, local_rows * lax.axis_size("tensor"), axis=0), w_up
        ).astype(jnp.bfloat16),
        "tensor",
        scatter_dimension=0,
        tiled=True,
    ).astype(jnp.float32)
    unused, norm_two_pull = jax.vjp(layer_norm, resid, gain_two_f, shift_two_f)
    grad_resid_norm, grad_gain_two, grad_shift_two = norm_two_pull(grad_normed_two)
    seed = cotangent.astype(jnp.float32)
    grad_resid = seed + grad_resid_norm
    branch_grad = grad_resid.astype(jnp.bfloat16)
    piece = lax.all_gather(branch_grad, "tensor", axis=0, tiled=True)
    start = jnp.int32(0)
    grad_out = jnp.zeros((mixed.shape[1], branch_grad.shape[1]), jnp.float32)
    grad_mixed = jnp.zeros(mixed.shape, jnp.float32)
    grad_out = grad_out + contract_rows(
        lax.dynamic_slice_in_dim(mixed, start, piece.shape[0], 0), piece
    )
    grad_mixed = lax.dynamic_update_slice_in_dim(grad_mixed, contract_cols(piece, w_out), start, 0)
    grad_out, grad_mixed = (grad_out, grad_mixed)
    grad_mixed = grad_mixed.astype(jnp.bfloat16).reshape(count, length, local_heads, head_dim)
    grad_joined = lax.map(
        partial(attend_backward, slopes=slopes, block=block),
        (query, keys, values, segments, log_total, grad_mixed),
    )
    grad_joined = grad_joined.reshape(rows_total, local_heads, 3, head_dim)
    grad_b_qv = jnp.sum(grad_joined[:, :, 0::2].astype(jnp.float32), axis=0).reshape(-1)
    grad_joined = grad_joined.reshape(rows_total, local_heads * 3 * head_dim)
    grad_qkv = contract_rows(rows_one, grad_joined)
    grad_normed_one = lax.psum_scatter(
        contract_cols(
            lax.slice_in_dim(grad_joined, 0, local_rows * lax.axis_size("tensor"), axis=0), w_qkv
        ).astype(jnp.bfloat16),
        "tensor",
        scatter_dimension=0,
        tiled=True,
    ).astype(jnp.float32)
    unused, norm_one_pull = jax.vjp(layer_norm, source, gain_one_f, shift_one_f)
    grad_source, grad_gain_one, grad_shift_one = norm_one_pull(grad_normed_one)
    input_grad = (grad_resid + grad_source).astype(jnp.bfloat16)
    sum_qkv, sum_out, sum_up, sum_down = (
        lax.psum_scatter(
            grad_qkv.astype(jnp.bfloat16), "dp", scatter_dimension=0, tiled=True
        ).astype(jnp.float32),
        lax.psum_scatter(
            grad_out.astype(jnp.bfloat16), "dp", scatter_dimension=1, tiled=True
        ).astype(jnp.float32),
        lax.psum_scatter(
            grad_up.astype(jnp.bfloat16), "dp", scatter_dimension=0, tiled=True
        ).astype(jnp.float32),
        lax.psum_scatter(
            grad_down.astype(jnp.bfloat16), "dp", scatter_dimension=1, tiled=True
        ).astype(jnp.float32),
    )
    small = lax.psum(
        (
            grad_gain_one,
            grad_shift_one,
            jnp.sum(grad_resid, axis=0),
            grad_gain_two,
            grad_shift_two,
            jnp.sum(seed, axis=0),
            spread_slots(grad_b_qv, rank, parts),
            spread_slots(grad_b_up, rank, parts),
        ),
        ("dp", "tensor"),
    )
    qv_width = grad_b_qv.shape[0]
    up_width = grad_b_up.shape[0]
    sum_qv = lax.dynamic_slice_in_dim(small[6], rank * qv_width, qv_width)
    sum_bias_up = lax.dynamic_slice_in_dim(small[7], rank * up_width, up_width)
    return (
        layer_out.astype(jnp.bfloat16),
        input_grad,
        sum_qkv,
        sum_qv,
        sum_out,
        small[2],
        sum_up,
        sum_bias_up,
        sum_down,
        small[5],
        small[0],
        small[1],
        small[3],
        small[4],
    )


PIECE = 256


def core_of(index):
    return index % 2


def swap_pairs():
    return [((2 * k + c) * 2 + x, (2 * k + x) * 2 + c) for k in range(8) for c in (0, 1) for x in (0, 1)]


def swap_only_pairs():
    return [(a, b) for a, b in swap_pairs() if a != b]


def flip_pairs(bit):
    return [(d, d ^ bit) for d in range(16)]


def flip_far_pairs(bit):
    return [((d * 2 + x), (d ^ bit) * 2 + x) for d in range(16) for x in (0, 1) if d % 2 != x]


def swap(value):
    return lax.ppermute(value, ("dp", "tensor"), swap_pairs())


def swap_far(value):
    return lax.ppermute(value, ("dp", "tensor"), swap_only_pairs())


def flip(value, bit):
    return lax.ppermute(value, "dp", flip_pairs(bit))


def flip_far(value, bit):
    return lax.ppermute(value, ("dp", "tensor"), flip_far_pairs(bit))


def after(value, *earlier):
    return lax.optimization_barrier((value, *earlier))[0]


def nt(left, right):
    return lax.dot_general(
        left, right, (((1,), (1,)), ((), ())), preferred_element_type=jnp.float32
    )


def nn(left, right):
    return lax.dot_general(
        left, right, (((1,), (0,)), ((), ())), preferred_element_type=jnp.float32
    )


def tn(left, right):
    return lax.dot_general(
        left, right, (((0,), (0,)), ((), ())), preferred_element_type=jnp.float32
    )


def both_halves(ref, core, lanes):
    return jnp.concatenate([ref[core, :, lanes], ref[1 - core, :, lanes]], axis=0)


def scores_of(keys, rows, slope, seg_col, seg_row, first, size):
    part = nt(keys, rows)
    place = lax.broadcasted_iota(jnp.int32, (keys.shape[0], 1), 0)
    part = part + (place - first).astype(jnp.float32) * slope
    same = seg_col[: keys.shape[0]] == seg_row
    shape = (size, size)
    ahead = lax.broadcasted_iota(jnp.int32, shape, 0) <= lax.broadcasted_iota(jnp.int32, shape, 1)
    diag = jnp.where(same[first:] & ahead, part[first:], masked_fill)
    if first == 0:
        return [diag]
    return [jnp.where(same[:first], part[:first], masked_fill), diag]


def attend_kernel(core_ref, slope_ref, qkv_ref, col_ref, row_ref, mixed_ref, total_ref):
    pair = pl.program_id(0)
    core = core_ref[0]
    half = qkv_ref.shape[1]
    length = 2 * half
    size = min(PIECE, half)
    seg_col = col_ref[...]
    for head in range(2):
        at = head * 3 * HEAD_DIM
        keys = both_halves(qkv_ref, core, slice(at + HEAD_DIM, at + 2 * HEAD_DIM))
        values = both_halves(qkv_ref, core, slice(at + 2 * HEAD_DIM, at + 3 * HEAD_DIM))
        slope = slope_ref[2 * pair + head]
        for first in range(0, length, size):
            side = core if first < half else 1 - core
            rows_at = slice(first % half, first % half + size)
            rows = qkv_ref[side, rows_at, at : at + HEAD_DIM] * jnp.bfloat16(HEAD_DIM**-0.5)
            stop = first + size
            parts = scores_of(
                keys[:stop], rows, slope, seg_col, row_ref[:, first:stop], first, size
            )
            top = jnp.max(parts[-1], axis=0, keepdims=True)
            if len(parts) > 1:
                top = jnp.maximum(top, jnp.max(parts[0], axis=0, keepdims=True))
            weights = [jnp.exp(part - top) for part in parts]
            total = sum(jnp.sum(part, axis=0, keepdims=True) for part in weights)
            log_total = top + jnp.log(total)
            inverse = 1.0 / total
            probs = [(part * inverse).astype(jnp.bfloat16) for part in weights]
            if len(probs) > 1:
                probs = jnp.concatenate(probs, axis=0)
            else:
                probs = probs[0]
            out = tn(values[:stop], probs)
            mixed_ref[side, rows_at, head * HEAD_DIM : (head + 1) * HEAD_DIM] = out.T.astype(
                jnp.bfloat16
            )
            total_ref[0, head : head + 1, first:stop] = log_total


def attend_back_kernel(
    core_ref,
    slope_ref,
    qkv_ref,
    grad_ref,
    total_ref,
    col_ref,
    row_ref,
    out_ref,
    sums_ref,
    probs_ref,
    deltas_ref,
):
    pair = pl.program_id(0)
    core = core_ref[0]
    half = qkv_ref.shape[1]
    length = 2 * half
    size = min(PIECE, half)
    scale = HEAD_DIM**-0.5
    seg_col = col_ref[...]
    sums = []
    for head in range(2):
        at = head * 3 * HEAD_DIM
        keys = both_halves(qkv_ref, core, slice(at + HEAD_DIM, at + 2 * HEAD_DIM))
        values = both_halves(qkv_ref, core, slice(at + 2 * HEAD_DIM, at + 3 * HEAD_DIM))
        query = both_halves(qkv_ref, core, slice(at, at + HEAD_DIM)) * jnp.bfloat16(scale)
        grads = both_halves(grad_ref, core, slice(head * HEAD_DIM, (head + 1) * HEAD_DIM))
        slope = slope_ref[2 * pair + head]
        query_sum = jnp.zeros((1, HEAD_DIM), jnp.float32)
        value_sum = jnp.zeros((1, HEAD_DIM), jnp.float32)
        for first in range(0, length, size):
            side = core if first < half else 1 - core
            rows_at = slice(first % half, first % half + size)
            stop = first + size
            parts = scores_of(
                keys[:stop], query[first:stop], slope, seg_col, row_ref[:, first:stop], first, size
            )
            log_total = total_ref[0, head : head + 1, first:stop]
            grad_probs = nt(values[:stop], grads[first:stop])
            probs = [jnp.exp(part - log_total) for part in parts]
            if len(probs) > 1:
                probs = jnp.concatenate(probs, axis=0)
            else:
                probs = probs[0]
            flow = probs * grad_probs
            inner = jnp.sum(flow, axis=0, keepdims=True)
            deltas = (flow - probs * inner).astype(jnp.bfloat16)
            probs_ref[:stop, first:stop] = probs.astype(jnp.bfloat16)
            deltas_ref[:stop, first:stop] = deltas
            grad_query = (tn(keys[:stop], deltas).T * scale).astype(jnp.bfloat16)
            query_sum = query_sum + jnp.sum(
                grad_query.astype(jnp.float32), axis=0, keepdims=True
            )
            out_ref[side, rows_at, at : at + HEAD_DIM] = grad_query
        for first in range(0, length, size):
            side = core if first < half else 1 - core
            rows_at = slice(first % half, first % half + size)
            stop = first + size
            grad_keys = nn(deltas_ref[first:stop, first:], query[first:]).astype(jnp.bfloat16)
            grad_values = nn(probs_ref[first:stop, first:], grads[first:]).astype(jnp.bfloat16)
            value_sum = value_sum + jnp.sum(
                grad_values.astype(jnp.float32), axis=0, keepdims=True
            )
            out_ref[side, rows_at, at + HEAD_DIM : at + 2 * HEAD_DIM] = grad_keys
            out_ref[side, rows_at, at + 2 * HEAD_DIM : at + 3 * HEAD_DIM] = grad_values
        sums += [query_sum, value_sum]
    sums_ref[0] = jnp.concatenate(sums, axis=1)


def attend(core, slopes, qkv, seg_col, seg_row):
    half = qkv.shape[1]
    heads = qkv.shape[2] // (3 * HEAD_DIM)
    pairs = heads // 2
    length = 2 * half
    flops = 4 * heads * length * length * HEAD_DIM
    return pl.pallas_call(
        attend_kernel,
        grid_spec=pltpu.PrefetchScalarGridSpec(
            num_scalar_prefetch=2,
            grid=(pairs,),
            in_specs=[
                pl.BlockSpec((2, half, 6 * HEAD_DIM), lambda p, c, s: (0, 0, p)),
                pl.BlockSpec((length, 1), lambda p, c, s: (0, 0)),
                pl.BlockSpec((1, length), lambda p, c, s: (0, 0)),
            ],
            out_specs=[
                pl.BlockSpec((2, half, 2 * HEAD_DIM), lambda p, c, s: (0, 0, p)),
                pl.BlockSpec((1, 2, length), lambda p, c, s: (p, 0, 0)),
            ],
        ),
        out_shape=[
            jax.ShapeDtypeStruct((2, half, heads * HEAD_DIM), jnp.bfloat16),
            jax.ShapeDtypeStruct((pairs, 2, length), jnp.float32),
        ],
        compiler_params=pltpu.CompilerParams(vmem_limit_bytes=48 * 2**20),
        cost_estimate=pl.CostEstimate(
            flops=4 * flops, bytes_accessed=6 * 2**20, transcendentals=heads * length * length
        ),
        name="attend_forward",
    )(core, slopes, qkv, seg_col, seg_row)


def attend_back(core, slopes, qkv, grads, totals, seg_col, seg_row):
    half = qkv.shape[1]
    heads = qkv.shape[2] // (3 * HEAD_DIM)
    pairs = heads // 2
    length = 2 * half
    flops = 10 * heads * length * length * HEAD_DIM
    return pl.pallas_call(
        attend_back_kernel,
        grid_spec=pltpu.PrefetchScalarGridSpec(
            num_scalar_prefetch=2,
            grid=(pairs,),
            in_specs=[
                pl.BlockSpec((2, half, 6 * HEAD_DIM), lambda p, c, s: (0, 0, p)),
                pl.BlockSpec((2, half, 2 * HEAD_DIM), lambda p, c, s: (0, 0, p)),
                pl.BlockSpec((1, 2, length), lambda p, c, s: (p, 0, 0)),
                pl.BlockSpec((length, 1), lambda p, c, s: (0, 0)),
                pl.BlockSpec((1, length), lambda p, c, s: (0, 0)),
            ],
            out_specs=[
                pl.BlockSpec((2, half, 6 * HEAD_DIM), lambda p, c, s: (0, 0, p)),
                pl.BlockSpec((1, 1, 4 * HEAD_DIM), lambda p, c, s: (p, 0, 0)),
            ],
            scratch_shapes=[
                pltpu.VMEM((length, length), jnp.bfloat16),
                pltpu.VMEM((length, length), jnp.bfloat16),
            ],
        ),
        out_shape=[
            jax.ShapeDtypeStruct(qkv.shape, jnp.bfloat16),
            jax.ShapeDtypeStruct((pairs, 1, 4 * HEAD_DIM), jnp.float32),
        ],
        compiler_params=pltpu.CompilerParams(vmem_limit_bytes=48 * 2**20),
        cost_estimate=pl.CostEstimate(
            flops=4 * flops, bytes_accessed=10 * 2**20, transcendentals=heads * length * length
        ),
        name="attend_backward",
    )(core, slopes, qkv, grads, totals, seg_col, seg_row)


def join_kernel(code_ref, far_ref, own_ref, *rest):
    parts, out_ref, sems = rest[:-2], rest[-2], rest[-1]
    count = len(parts)
    rows = out_ref.shape[0] // count
    for piece in range(count):
        spot = pl.ds(piece * rows, rows)

        @pl.when(far_ref[0] == 0)
        def _():
            pltpu.make_async_copy(own_ref.at[spot], out_ref.at[spot], sems.at[piece]).start()

        for slot in range(count):

            @pl.when((far_ref[0] != 0) & (jnp.bitwise_xor(code_ref[0], slot) == piece))
            def _():
                pltpu.make_async_copy(parts[slot], out_ref.at[spot], sems.at[piece]).start()

    for piece in range(count):
        spot = pl.ds(piece * rows, rows)
        pltpu.make_async_copy(own_ref.at[spot], out_ref.at[spot], sems.at[piece]).wait()


def join(code, far, own, parts):
    hbm = pl.BlockSpec(memory_space=pl.ANY)
    smem = pl.BlockSpec(memory_space=pltpu.SMEM)
    return pl.pallas_call(
        join_kernel,
        in_specs=[smem, smem, hbm] + [hbm] * len(parts),
        out_specs=hbm,
        out_shape=jax.ShapeDtypeStruct(own.shape, own.dtype),
        scratch_shapes=[pltpu.SemaphoreType.DMA((len(parts),))],
        cost_estimate=pl.CostEstimate(
            flops=0, bytes_accessed=4 * own.size, transcendentals=0
        ),
        name="join_pieces",
    )(code, far, own, *parts)


def norm_parts(values):
    row_mean = jnp.mean(values, axis=-1, keepdims=True)
    centered = values - row_mean
    row_var = jnp.mean(centered * centered, axis=-1, keepdims=True)
    inverse = lax.rsqrt(row_var + norm_eps)
    return centered * inverse, inverse


def norm_back(values, gain, grads):
    hat, inverse = norm_parts(values)
    scaled = grads * gain
    out = inverse * (
        scaled
        - jnp.mean(scaled, axis=-1, keepdims=True)
        - hat * jnp.mean(scaled * hat, axis=-1, keepdims=True)
    )
    return out, jnp.sum(grads * hat, axis=0), jnp.sum(grads, axis=0)


def halve(kept, came, bit, index):
    outer = kept.shape[0] // (2 * bit)

    def pick(value, which):
        value = value.reshape((outer, 2, bit) + value.shape[1:])
        return lax.dynamic_index_in_dim(value, which, 1, keepdims=False).reshape(
            (outer * bit,) + value.shape[3:]
        )

    def part(which):
        value = pick(kept, which).astype(jnp.float32)
        if came is not None:
            value = value + pick(came, which).astype(jnp.float32)
        return value.astype(jnp.bfloat16)

    return part(index), part(1 - index)


def reduce_rows(grads, order, places):
    core, y_at, z_low, z_high = places
    width = grads.shape[1]
    kept = grads.reshape(16, grads.shape[0] // 16, width)
    came = None
    left = ["core", "y", "low", "high"]
    spot = {"core": core, "y": y_at, "low": z_low, "high": z_high}
    flips = {"core": 1, "y": 2, "low": 4, "high": 8}
    for step in order:
        if step == "x":
            total = kept if came is None else (
                kept.astype(jnp.float32) + came.astype(jnp.float32)
            ).astype(jnp.bfloat16)
            kept, came = swap(total), None
            continue
        bit = 1 << left.index(step)
        mine, other = halve(kept, came, bit, spot[step])
        kept, came = mine, flip(other, flips[step])
        left.remove(step)
    return (kept.astype(jnp.float32) + came.astype(jnp.float32))[0]


def sum_everywhere(value):
    value = value + lax.ppermute(value, "tensor", [(0, 1), (1, 0)])
    for bit in (1, 2, 4, 8):
        value = value + flip(value, bit)
    return value


def chip_body(
    tokens,
    segments,
    w_qkv,
    b_qv,
    w_out,
    b_out,
    w_up,
    b_up,
    w_down,
    b_down,
    gain_one,
    shift_one,
    gain_two,
    shift_two,
    cotangent,
):
    f32, bf16 = jnp.float32, jnp.bfloat16
    place = lax.axis_index("dp")
    rank = lax.axis_index("tensor")
    core = core_of(place)
    y_at = (place // 2) % 2
    z_low = (place // 4) % 2
    z_high = place // 8
    places = (core, y_at, z_low, z_high)
    far = (core != rank).astype(jnp.int32).reshape(1)
    core_s = core.astype(jnp.int32).reshape(1)
    half, width = tokens.shape
    length = segments.shape[1]
    heads = w_qkv.shape[1] // (3 * HEAD_DIM)

    def fetch(weight, ways, gate):
        rows = weight.shape[0] // ways
        code = y_at if ways == 2 else z_low * 2 + y_at
        piece = lax.dynamic_slice_in_dim(weight, code * rows, rows, 0)
        piece = after(piece, gate) if gate is not None else piece
        first = swap_far(piece)
        parts = [first, flip_far(first, 2)]
        if ways == 4:
            parts += [flip_far(parts[0], 4), flip_far(parts[1], 4)]
        return join(code.astype(jnp.int32).reshape(1), far, weight, parts), first

    source_b = swap(tokens)
    qkv_w, gate = fetch(w_qkv, 2, source_b)
    b_qv_l = swap(b_qv)
    b_up_l = swap(b_up)
    out_w, gate = fetch(w_out, 2, gate)
    up_w, gate = fetch(w_up, 4, gate)
    seed_mine = swap(after(cotangent, gate))
    down_w, gate = fetch(w_down, 4, seed_mine)
    segment = jnp.where(core == rank, segments, flip(segments, 1))
    seg_col = segment.reshape(length, 1)

    head_index = core * heads + lax.iota(jnp.int32, heads)
    slopes = 2.0 ** (-8.0 * (head_index + 1).astype(f32) / HEADS)
    gain_one_f = gain_one.astype(f32)
    gain_two_f = gain_two.astype(f32)

    source = source_b.astype(f32)
    normed = layer_norm(source, gain_one_f, shift_one.astype(f32)).astype(bf16)
    rows_one = jnp.concatenate([normed, flip(normed, 1)], axis=0)
    pair = b_qv_l.astype(f32).reshape(heads, 2, HEAD_DIM)
    bias = jnp.stack([pair[:, 0], jnp.zeros_like(pair[:, 0]), pair[:, 1]], axis=1).reshape(-1)
    joined = (jnp.dot(rows_one, qkv_w, preferred_element_type=f32) + bias).astype(bf16)
    joined = joined.reshape(2, half, joined.shape[1])
    mixed, totals = attend(core_s, slopes, joined, seg_col, segment)

    came = flip(jnp.dot(mixed[1], out_w, preferred_element_type=f32).astype(bf16), 1)
    resid = (
        source
        + jnp.dot(mixed[0], out_w, preferred_element_type=f32)
        + came.astype(f32)
        + b_out.astype(f32)
    )
    normed = layer_norm(resid, gain_two_f, shift_two.astype(f32)).astype(bf16)
    rows_two = jnp.concatenate([normed, flip(normed, 1)], axis=0)
    seed_rows = jnp.concatenate([seed_mine, flip(seed_mine, 1)], axis=0)
    pre_act = jnp.dot(rows_two, up_w, preferred_element_type=f32) + b_up_l.astype(f32)
    hidden, gelu_pull = jax.vjp(partial(jax.nn.gelu, approximate=True), pre_act)
    slope_act = gelu_pull(jnp.ones_like(pre_act))[0].astype(bf16)
    hidden = hidden.astype(bf16)
    came = flip(jnp.dot(hidden[half:], down_w, preferred_element_type=f32).astype(bf16), 1)
    layer_out = (
        resid
        + jnp.dot(hidden[:half], down_w, preferred_element_type=f32)
        + came.astype(f32)
        + b_down.astype(f32)
    )
    layer_out = swap(layer_out.astype(bf16))

    grad_pre_f = contract_cols(seed_rows, down_w) * slope_act.astype(f32)
    grad_pre = grad_pre_f.astype(bf16)
    grad_b_up = jnp.sum(grad_pre.astype(f32), axis=0)
    came = flip(contract_cols(grad_pre[half:], up_w).astype(bf16), 1)
    grad_normed = contract_cols(grad_pre[:half], up_w) + came.astype(f32)
    grad_down = contract_rows(seed_rows, hidden).astype(bf16)
    sum_down = reduce_rows(grad_down, ("x", "core", "y", "low", "high"), places).T
    grad_up = contract_rows(rows_two, grad_pre).astype(bf16)
    sum_up = reduce_rows(grad_up, ("y", "x", "core", "low", "high"), places)
    grad_norm, grad_gain_two, grad_shift_two = norm_back(resid, gain_two_f, grad_normed)
    seed = seed_mine.astype(f32)
    grad_resid = seed + grad_norm
    branch = grad_resid.astype(bf16)
    branch_rows = jnp.concatenate([branch, flip(branch, 1)], axis=0)
    grad_mixed = contract_cols(branch_rows, out_w).astype(bf16).reshape(mixed.shape)
    grad_joined, qv_sums = attend_back(core_s, slopes, joined, grad_mixed, totals, seg_col, segment)
    grad_out = contract_rows(branch_rows, mixed.reshape(2 * half, -1)).astype(bf16)
    sum_out = reduce_rows(grad_out, ("x", "core", "y", "low", "high"), places).T
    grad_joined = grad_joined.reshape(2 * half, -1)
    grad_qkv = contract_rows(rows_one, grad_joined).astype(bf16)
    sum_qkv = reduce_rows(grad_qkv, ("y", "x", "core", "low", "high"), places)
    came = flip(contract_cols(grad_joined[half:], qkv_w).astype(bf16), 1)
    grad_normed = contract_cols(grad_joined[:half], qkv_w) + came.astype(f32)
    grad_source, grad_gain_one, grad_shift_one = norm_back(source, gain_one_f, grad_normed)
    input_grad = swap((grad_resid + grad_source).astype(bf16))

    early = sum_everywhere(
        jnp.concatenate(
            [
                jnp.sum(grad_resid, axis=0),
                grad_gain_two,
                grad_shift_two,
                jnp.sum(seed, axis=0),
                spread_slots(grad_b_up, core, 2),
            ]
        )
    )
    late = sum_everywhere(
        jnp.concatenate(
            [grad_gain_one, grad_shift_one, spread_slots(qv_sums.reshape(-1), core, 2)]
        )
    )
    up_width = grad_b_up.shape[0]
    qv_width = b_qv.shape[0]
    sum_b_up = lax.dynamic_slice_in_dim(early[4 * width :], rank * up_width, up_width)
    sum_b_qv = lax.dynamic_slice_in_dim(late[2 * width :], rank * qv_width, qv_width)
    return (
        layer_out,
        input_grad,
        sum_qkv,
        sum_b_qv,
        sum_out,
        early[:width],
        sum_up,
        sum_b_up,
        sum_down,
        early[3 * width : 4 * width],
        late[:width],
        late[width : 2 * width],
        early[width : 2 * width],
        early[2 * width : 3 * width],
    )


def solution(mesh):
    in_specs = (
        P(("dp", "tensor"), None),
        P("dp", None),
        P(None, "tensor"),
        P("tensor"),
        P("tensor", None),
        P(),
        P(None, "tensor"),
        P("tensor"),
        P("tensor", None),
        P(),
        P(),
        P(),
        P(),
        P(),
        P(("dp", "tensor"), None),
    )
    out_specs = (
        P(("dp", "tensor"), None),
        P(("dp", "tensor"), None),
        P("dp", "tensor"),
        P("tensor"),
        P("tensor", "dp"),
        P(),
        P("dp", "tensor"),
        P("tensor"),
        P("tensor", "dp"),
        P(),
        P(),
        P(),
        P(),
        P(),
    )
    pairs = mesh.shape["tensor"] == 2 and mesh.shape["dp"] == 16
    plan = chip_body if pairs else body
    return jax.shard_map(plan, mesh=mesh, in_specs=in_specs, out_specs=out_specs, check_vma=False)
```

```python
from functools import partial

import jax
import jax.numpy as jnp
from jax import lax
from jax.experimental import pallas as pl
from jax.experimental.pallas import tpu as pltpu
from jax.sharding import PartitionSpec as P

HEADS = 16
HEAD_DIM = 64


norm_eps = 1e-05
masked_fill = -1e30


def layer_norm(values, gain, shift):
    row_mean = jnp.mean(values, axis=-1, keepdims=True)
    centered = values - row_mean
    row_var = jnp.mean(centered * centered, axis=-1, keepdims=True)
    return centered * lax.rsqrt(row_var + norm_eps) * gain + shift


def contract_rows(left, right):
    return lax.dot_general(
        left, right, (((0,), (0,)), ((), ())), preferred_element_type=jnp.float32
    )


def contract_cols(left, right):
    return lax.dot_general(
        left, right, (((1,), (1,)), ((), ())), preferred_element_type=jnp.float32
    )


def spread_slots(local, rank, parts):
    slots = (lax.iota(jnp.int32, parts) == rank).astype(jnp.float32)
    return (slots[:, None] * local[None, :]).reshape(-1)


def masked_scores(query, keys, segment, first, slopes):
    scale = keys.shape[2] ** (-0.5)
    raw = jnp.einsum("qhd,khd->hqk", query, keys, preferred_element_type=jnp.float32) * scale
    rows_at = first + lax.iota(jnp.int32, query.shape[0])
    cols_at = lax.iota(jnp.int32, keys.shape[0])
    distance = (rows_at[:, None] - cols_at[None, :]).astype(jnp.float32)
    seg_rows = segment[first : first + query.shape[0]]
    allowed = (seg_rows[:, None] == segment[None, :]) & (distance >= 0)
    return jnp.where(allowed[None], raw - slopes[:, None, None] * distance[None], masked_fill)


def attend_forward(inputs, slopes, block):
    query, keys, values, segment = inputs
    outputs = []
    totals = []
    for first in range(0, keys.shape[0], block):
        scores = masked_scores(query[first : first + block], keys, segment, first, slopes)
        top = jnp.max(scores, axis=2, keepdims=True)
        log_total = top + jnp.log(jnp.sum(jnp.exp(scores - top), axis=2, keepdims=True))
        probs = jnp.exp(scores - log_total).astype(jnp.bfloat16)
        outputs.append(
            jnp.einsum("hqk,khd->qhd", probs, values, preferred_element_type=jnp.float32)
        )
        totals.append(log_total)
    return (jnp.concatenate(outputs, 0).astype(jnp.bfloat16), jnp.concatenate(totals, 1))


def attend_backward(inputs, slopes, block):
    query, keys, values, segment, log_total, grad_mixed = inputs
    scale = keys.shape[2] ** (-0.5)
    grad_keys = jnp.zeros(keys.shape, jnp.float32)
    grad_values = jnp.zeros(values.shape, jnp.float32)
    grad_query = []
    for first in range(0, keys.shape[0], block):
        rows = query[first : first + block]
        grad_rows = grad_mixed[first : first + block]
        scores = masked_scores(rows, keys, segment, first, slopes)
        probs = jnp.exp(scores - log_total[:, first : first + block])
        grad_probs = jnp.einsum(
            "qhd,khd->hqk", grad_rows, values, preferred_element_type=jnp.float32
        )
        inner = jnp.sum(probs * grad_probs, axis=2, keepdims=True)
        grad_scores = (probs * (grad_probs - inner)).astype(jnp.bfloat16)
        grad_query.append(
            jnp.einsum("hqk,khd->qhd", grad_scores, keys, preferred_element_type=jnp.float32)
            * scale
        )
        grad_keys = (
            grad_keys
            + jnp.einsum("hqk,qhd->khd", grad_scores, rows, preferred_element_type=jnp.float32)
            * scale
        )
        grad_values = grad_values + jnp.einsum(
            "hqk,qhd->khd",
            probs.astype(jnp.bfloat16),
            grad_rows,
            preferred_element_type=jnp.float32,
        )
    grad_query = jnp.concatenate(grad_query, 0)
    return jnp.stack((grad_query, grad_keys, grad_values), axis=2).astype(jnp.bfloat16)


def body(
    tokens,
    segments,
    w_qkv,
    b_qv,
    w_out,
    b_out,
    w_up,
    b_up,
    w_down,
    b_down,
    gain_one,
    shift_one,
    gain_two,
    shift_two,
    cotangent,
):
    rank = lax.axis_index("tensor")
    parts = lax.axis_size("tensor")
    count, length = segments.shape
    head_dim = HEAD_DIM
    local_heads = w_qkv.shape[1] // (3 * head_dim)
    block = length // 2
    rows_total = count * length
    local_rows = tokens.shape[0]
    head_index = rank * local_heads + lax.iota(jnp.int32, local_heads)
    slopes = 2.0 ** (-8.0 * (head_index + 1).astype(jnp.float32) / HEADS)
    gain_one_f = gain_one.astype(jnp.float32)
    shift_one_f = shift_one.astype(jnp.float32)
    gain_two_f = gain_two.astype(jnp.float32)
    shift_two_f = shift_two.astype(jnp.float32)
    source = tokens.astype(jnp.float32)
    normed_one = layer_norm(source, gain_one_f, shift_one_f).astype(jnp.bfloat16)
    rows_one = lax.all_gather(normed_one, "tensor", axis=0, tiled=True)
    joined = jnp.dot(rows_one, w_qkv, preferred_element_type=jnp.float32).reshape(
        count, length, local_heads, 3, head_dim
    )
    bias_pair = b_qv.astype(jnp.float32).reshape(local_heads, 2, head_dim)
    query = (joined[:, :, :, 0] + bias_pair[:, 0]).astype(jnp.bfloat16)
    keys = joined[:, :, :, 1].astype(jnp.bfloat16)
    values = (joined[:, :, :, 2] + bias_pair[:, 1]).astype(jnp.bfloat16)
    mixed, log_total = lax.map(
        partial(attend_forward, slopes=slopes, block=block), (query, keys, values, segments)
    )
    mixed = mixed.reshape(rows_total, local_heads * head_dim)
    attn_part = lax.psum_scatter(
        jnp.dot(
            lax.slice_in_dim(mixed, 0, local_rows * lax.axis_size("tensor"), axis=0),
            w_out,
            preferred_element_type=jnp.float32,
        ).astype(jnp.bfloat16),
        "tensor",
        scatter_dimension=0,
        tiled=True,
    ).astype(jnp.float32)
    resid = source + attn_part + b_out.astype(jnp.float32)
    normed_two = layer_norm(resid, gain_two_f, shift_two_f).astype(jnp.bfloat16)
    rows_two = lax.all_gather(normed_two, "tensor", axis=0, tiled=True)
    pre_act = jnp.dot(rows_two, w_up, preferred_element_type=jnp.float32) + b_up.astype(jnp.float32)
    hidden = jax.nn.gelu(pre_act, approximate=True).astype(jnp.bfloat16)
    mlp_part = lax.psum_scatter(
        jnp.dot(
            lax.slice_in_dim(hidden, 0, local_rows * lax.axis_size("tensor"), axis=0),
            w_down,
            preferred_element_type=jnp.float32,
        ).astype(jnp.bfloat16),
        "tensor",
        scatter_dimension=0,
        tiled=True,
    ).astype(jnp.float32)
    layer_out = resid + mlp_part + b_down.astype(jnp.float32)
    piece = lax.all_gather(cotangent, "tensor", axis=0, tiled=True)
    start = jnp.int32(0)
    grad_down = jnp.zeros((hidden.shape[1], cotangent.shape[1]), jnp.float32)
    grad_hidden = jnp.zeros(hidden.shape, jnp.float32)
    grad_down = grad_down + contract_rows(
        lax.dynamic_slice_in_dim(hidden, start, piece.shape[0], 0), piece
    )
    grad_hidden = lax.dynamic_update_slice_in_dim(
        grad_hidden, contract_cols(piece, w_down), start, 0
    )
    grad_down, grad_hidden = (grad_down, grad_hidden)
    unused, gelu_pull = jax.vjp(partial(jax.nn.gelu, approximate=True), pre_act)
    grad_pre = gelu_pull(grad_hidden)[0].astype(jnp.bfloat16)
    grad_up = contract_rows(rows_two, grad_pre)
    grad_b_up = jnp.sum(grad_pre.astype(jnp.float32), axis=0)
    grad_normed_two = lax.psum_scatter(
        contract_cols(
            lax.slice_in_dim(grad_pre, 0, local_rows * lax.axis_size("tensor"), axis=0), w_up
        ).astype(jnp.bfloat16),
        "tensor",
        scatter_dimension=0,
        tiled=True,
    ).astype(jnp.float32)
    unused, norm_two_pull = jax.vjp(layer_norm, resid, gain_two_f, shift_two_f)
    grad_resid_norm, grad_gain_two, grad_shift_two = norm_two_pull(grad_normed_two)
    seed = cotangent.astype(jnp.float32)
    grad_resid = seed + grad_resid_norm
    branch_grad = grad_resid.astype(jnp.bfloat16)
    piece = lax.all_gather(branch_grad, "tensor", axis=0, tiled=True)
    start = jnp.int32(0)
    grad_out = jnp.zeros((mixed.shape[1], branch_grad.shape[1]), jnp.float32)
    grad_mixed = jnp.zeros(mixed.shape, jnp.float32)
    grad_out = grad_out + contract_rows(
        lax.dynamic_slice_in_dim(mixed, start, piece.shape[0], 0), piece
    )
    grad_mixed = lax.dynamic_update_slice_in_dim(grad_mixed, contract_cols(piece, w_out), start, 0)
    grad_out, grad_mixed = (grad_out, grad_mixed)
    grad_mixed = grad_mixed.astype(jnp.bfloat16).reshape(count, length, local_heads, head_dim)
    grad_joined = lax.map(
        partial(attend_backward, slopes=slopes, block=block),
        (query, keys, values, segments, log_total, grad_mixed),
    )
    grad_joined = grad_joined.reshape(rows_total, local_heads, 3, head_dim)
    grad_b_qv = jnp.sum(grad_joined[:, :, 0::2].astype(jnp.float32), axis=0).reshape(-1)
    grad_joined = grad_joined.reshape(rows_total, local_heads * 3 * head_dim)
    grad_qkv = contract_rows(rows_one, grad_joined)
    grad_normed_one = lax.psum_scatter(
        contract_cols(
            lax.slice_in_dim(grad_joined, 0, local_rows * lax.axis_size("tensor"), axis=0), w_qkv
        ).astype(jnp.bfloat16),
        "tensor",
        scatter_dimension=0,
        tiled=True,
    ).astype(jnp.float32)
    unused, norm_one_pull = jax.vjp(layer_norm, source, gain_one_f, shift_one_f)
    grad_source, grad_gain_one, grad_shift_one = norm_one_pull(grad_normed_one)
    input_grad = (grad_resid + grad_source).astype(jnp.bfloat16)
    sum_qkv, sum_out, sum_up, sum_down = (
        lax.psum_scatter(
            grad_qkv.astype(jnp.bfloat16), "dp", scatter_dimension=0, tiled=True
        ).astype(jnp.float32),
        lax.psum_scatter(
            grad_out.astype(jnp.bfloat16), "dp", scatter_dimension=1, tiled=True
        ).astype(jnp.float32),
        lax.psum_scatter(
            grad_up.astype(jnp.bfloat16), "dp", scatter_dimension=0, tiled=True
        ).astype(jnp.float32),
        lax.psum_scatter(
            grad_down.astype(jnp.bfloat16), "dp", scatter_dimension=1, tiled=True
        ).astype(jnp.float32),
    )
    small = lax.psum(
        (
            grad_gain_one,
            grad_shift_one,
            jnp.sum(grad_resid, axis=0),
            grad_gain_two,
            grad_shift_two,
            jnp.sum(seed, axis=0),
            spread_slots(grad_b_qv, rank, parts),
            spread_slots(grad_b_up, rank, parts),
        ),
        ("dp", "tensor"),
    )
    qv_width = grad_b_qv.shape[0]
    up_width = grad_b_up.shape[0]
    sum_qv = lax.dynamic_slice_in_dim(small[6], rank * qv_width, qv_width)
    sum_bias_up = lax.dynamic_slice_in_dim(small[7], rank * up_width, up_width)
    return (
        layer_out.astype(jnp.bfloat16),
        input_grad,
        sum_qkv,
        sum_qv,
        sum_out,
        small[2],
        sum_up,
        sum_bias_up,
        sum_down,
        small[5],
        small[0],
        small[1],
        small[3],
        small[4],
    )


PIECE = 256


def core_of(index):
    return index % 2


def swap_pairs():
    return [((2 * k + c) * 2 + x, (2 * k + x) * 2 + c) for k in range(8) for c in (0, 1) for x in (0, 1)]


def swap_only_pairs():
    return [(a, b) for a, b in swap_pairs() if a != b]


def flip_pairs(bit):
    return [(d, d ^ bit) for d in range(16)]


def flip_far_pairs(bit):
    return [((d * 2 + x), (d ^ bit) * 2 + x) for d in range(16) for x in (0, 1) if d % 2 != x]


def swap(value):
    core = lax.axis_index("dp") % 2
    return jnp.where(core != lax.axis_index("tensor"), swap_far(value), value)


def swap_far(value):
    return lax.ppermute(value, ("dp", "tensor"), swap_only_pairs())


def flip(value, bit):
    return lax.ppermute(value, "dp", flip_pairs(bit))


def flip_far(value, bit):
    return lax.ppermute(value, ("dp", "tensor"), flip_far_pairs(bit))


def after(value, *earlier):
    return lax.optimization_barrier((value, *earlier))[0]


def nt(left, right):
    return lax.dot_general(
        left, right, (((1,), (1,)), ((), ())), preferred_element_type=jnp.float32
    )


def nn(left, right):
    return lax.dot_general(
        left, right, (((1,), (0,)), ((), ())), preferred_element_type=jnp.float32
    )


def tn(left, right):
    return lax.dot_general(
        left, right, (((0,), (0,)), ((), ())), preferred_element_type=jnp.float32
    )


def both_halves(ref, core, lanes):
    return jnp.concatenate([ref[core, :, lanes], ref[1 - core, :, lanes]], axis=0)


def scores_of(keys, rows, slope, seg_col, seg_row, first, size):
    part = nt(keys, rows)
    place = lax.broadcasted_iota(jnp.int32, (keys.shape[0], 1), 0)
    part = part + (place - first).astype(jnp.float32) * slope
    same = seg_col[: keys.shape[0]] == seg_row
    shape = (size, size)
    ahead = lax.broadcasted_iota(jnp.int32, shape, 0) <= lax.broadcasted_iota(jnp.int32, shape, 1)
    diag = jnp.where(same[first:] & ahead, part[first:], masked_fill)
    if first == 0:
        return [diag]
    return [jnp.where(same[:first], part[:first], masked_fill), diag]


def attend_kernel(core_ref, slope_ref, qkv_ref, col_ref, row_ref, mixed_ref, total_ref):
    pair = pl.program_id(0)
    core = core_ref[0]
    half = qkv_ref.shape[1]
    length = 2 * half
    size = min(PIECE, half)
    seg_col = col_ref[...]
    for head in range(2):
        at = head * 3 * HEAD_DIM
        keys = both_halves(qkv_ref, core, slice(at + HEAD_DIM, at + 2 * HEAD_DIM))
        values = both_halves(qkv_ref, core, slice(at + 2 * HEAD_DIM, at + 3 * HEAD_DIM))
        slope = slope_ref[2 * pair + head]
        for first in range(0, length, size):
            side = core if first < half else 1 - core
            rows_at = slice(first % half, first % half + size)
            rows = qkv_ref[side, rows_at, at : at + HEAD_DIM] * jnp.bfloat16(HEAD_DIM**-0.5)
            stop = first + size
            parts = scores_of(
                keys[:stop], rows, slope, seg_col, row_ref[:, first:stop], first, size
            )
            top = jnp.max(parts[-1], axis=0, keepdims=True)
            if len(parts) > 1:
                top = jnp.maximum(top, jnp.max(parts[0], axis=0, keepdims=True))
            weights = [jnp.exp(part - top) for part in parts]
            total = sum(jnp.sum(part, axis=0, keepdims=True) for part in weights)
            log_total = top + jnp.log(total)
            inverse = 1.0 / total
            probs = [(part * inverse).astype(jnp.bfloat16) for part in weights]
            if len(probs) > 1:
                probs = jnp.concatenate(probs, axis=0)
            else:
                probs = probs[0]
            out = tn(values[:stop], probs)
            mixed_ref[side, rows_at, head * HEAD_DIM : (head + 1) * HEAD_DIM] = out.T.astype(
                jnp.bfloat16
            )
            total_ref[0, head : head + 1, first:stop] = log_total


def attend_back_kernel(
    core_ref,
    slope_ref,
    qkv_ref,
    grad_ref,
    total_ref,
    col_ref,
    row_ref,
    out_ref,
    sums_ref,
    probs_ref,
    deltas_ref,
):
    pair = pl.program_id(0)
    core = core_ref[0]
    half = qkv_ref.shape[1]
    length = 2 * half
    size = min(PIECE, half)
    scale = HEAD_DIM**-0.5
    seg_col = col_ref[...]
    sums = []
    for head in range(2):
        at = head * 3 * HEAD_DIM
        keys = both_halves(qkv_ref, core, slice(at + HEAD_DIM, at + 2 * HEAD_DIM))
        values = both_halves(qkv_ref, core, slice(at + 2 * HEAD_DIM, at + 3 * HEAD_DIM))
        query = both_halves(qkv_ref, core, slice(at, at + HEAD_DIM)) * jnp.bfloat16(scale)
        grads = both_halves(grad_ref, core, slice(head * HEAD_DIM, (head + 1) * HEAD_DIM))
        slope = slope_ref[2 * pair + head]
        query_sum = jnp.zeros((1, HEAD_DIM), jnp.float32)
        value_sum = jnp.zeros((1, HEAD_DIM), jnp.float32)
        for first in range(0, length, size):
            side = core if first < half else 1 - core
            rows_at = slice(first % half, first % half + size)
            stop = first + size
            parts = scores_of(
                keys[:stop], query[first:stop], slope, seg_col, row_ref[:, first:stop], first, size
            )
            log_total = total_ref[0, head : head + 1, first:stop]
            grad_probs = nt(values[:stop], grads[first:stop])
            probs = [jnp.exp(part - log_total) for part in parts]
            if len(probs) > 1:
                probs = jnp.concatenate(probs, axis=0)
            else:
                probs = probs[0]
            flow = probs * grad_probs
            inner = jnp.sum(flow, axis=0, keepdims=True)
            deltas = (flow - probs * inner).astype(jnp.bfloat16)
            probs_ref[:stop, first:stop] = probs.astype(jnp.bfloat16)
            deltas_ref[:stop, first:stop] = deltas
            grad_query = (tn(keys[:stop], deltas).T * scale).astype(jnp.bfloat16)
            query_sum = query_sum + jnp.sum(
                grad_query.astype(jnp.float32), axis=0, keepdims=True
            )
            out_ref[side, rows_at, at : at + HEAD_DIM] = grad_query
        for first in range(0, length, size):
            side = core if first < half else 1 - core
            rows_at = slice(first % half, first % half + size)
            stop = first + size
            grad_keys = nn(deltas_ref[first:stop, first:], query[first:]).astype(jnp.bfloat16)
            grad_values = nn(probs_ref[first:stop, first:], grads[first:]).astype(jnp.bfloat16)
            value_sum = value_sum + jnp.sum(
                grad_values.astype(jnp.float32), axis=0, keepdims=True
            )
            out_ref[side, rows_at, at + HEAD_DIM : at + 2 * HEAD_DIM] = grad_keys
            out_ref[side, rows_at, at + 2 * HEAD_DIM : at + 3 * HEAD_DIM] = grad_values
        sums += [query_sum, value_sum]
    sums_ref[0] = jnp.concatenate(sums, axis=1)


def attend(core, slopes, qkv, seg_col, seg_row):
    half = qkv.shape[1]
    heads = qkv.shape[2] // (3 * HEAD_DIM)
    pairs = heads // 2
    length = 2 * half
    flops = 4 * heads * length * length * HEAD_DIM
    return pl.pallas_call(
        attend_kernel,
        grid_spec=pltpu.PrefetchScalarGridSpec(
            num_scalar_prefetch=2,
            grid=(pairs,),
            in_specs=[
                pl.BlockSpec((2, half, 6 * HEAD_DIM), lambda p, c, s: (0, 0, p)),
                pl.BlockSpec((length, 1), lambda p, c, s: (0, 0)),
                pl.BlockSpec((1, length), lambda p, c, s: (0, 0)),
            ],
            out_specs=[
                pl.BlockSpec((2, half, 2 * HEAD_DIM), lambda p, c, s: (0, 0, p)),
                pl.BlockSpec((1, 2, length), lambda p, c, s: (p, 0, 0)),
            ],
        ),
        out_shape=[
            jax.ShapeDtypeStruct((2, half, heads * HEAD_DIM), jnp.bfloat16),
            jax.ShapeDtypeStruct((pairs, 2, length), jnp.float32),
        ],
        compiler_params=pltpu.CompilerParams(vmem_limit_bytes=48 * 2**20),
        cost_estimate=pl.CostEstimate(
            flops=4 * flops, bytes_accessed=6 * 2**20, transcendentals=heads * length * length
        ),
        name="attend_forward",
    )(core, slopes, qkv, seg_col, seg_row)


def attend_back(core, slopes, qkv, grads, totals, seg_col, seg_row):
    half = qkv.shape[1]
    heads = qkv.shape[2] // (3 * HEAD_DIM)
    pairs = heads // 2
    length = 2 * half
    flops = 10 * heads * length * length * HEAD_DIM
    return pl.pallas_call(
        attend_back_kernel,
        grid_spec=pltpu.PrefetchScalarGridSpec(
            num_scalar_prefetch=2,
            grid=(pairs,),
            in_specs=[
                pl.BlockSpec((2, half, 6 * HEAD_DIM), lambda p, c, s: (0, 0, p)),
                pl.BlockSpec((2, half, 2 * HEAD_DIM), lambda p, c, s: (0, 0, p)),
                pl.BlockSpec((1, 2, length), lambda p, c, s: (p, 0, 0)),
                pl.BlockSpec((length, 1), lambda p, c, s: (0, 0)),
                pl.BlockSpec((1, length), lambda p, c, s: (0, 0)),
            ],
            out_specs=[
                pl.BlockSpec((2, half, 6 * HEAD_DIM), lambda p, c, s: (0, 0, p)),
                pl.BlockSpec((1, 1, 4 * HEAD_DIM), lambda p, c, s: (p, 0, 0)),
            ],
            scratch_shapes=[
                pltpu.VMEM((length, length), jnp.bfloat16),
                pltpu.VMEM((length, length), jnp.bfloat16),
            ],
        ),
        out_shape=[
            jax.ShapeDtypeStruct(qkv.shape, jnp.bfloat16),
            jax.ShapeDtypeStruct((pairs, 1, 4 * HEAD_DIM), jnp.float32),
        ],
        compiler_params=pltpu.CompilerParams(vmem_limit_bytes=48 * 2**20),
        cost_estimate=pl.CostEstimate(
            flops=4 * flops, bytes_accessed=10 * 2**20, transcendentals=heads * length * length
        ),
        name="attend_backward",
    )(core, slopes, qkv, grads, totals, seg_col, seg_row)


def join_kernel(code_ref, far_ref, own_ref, *rest):
    parts, out_ref, sem = rest[:-2], rest[-2], rest[-1]
    rows = out_ref.shape[0]
    piece = pl.program_id(0)
    own = own_ref.at[pl.ds(pl.multiple_of(piece * rows, rows), rows)]

    @pl.when(far_ref[0] == 0)
    def _():
        pltpu.make_async_copy(own, out_ref, sem).start()

    for slot, part in enumerate(parts):

        @pl.when((far_ref[0] != 0) & (jnp.bitwise_xor(code_ref[0], slot) == piece))
        def _():
            pltpu.make_async_copy(part, out_ref, sem).start()

    pltpu.make_async_copy(own, out_ref, sem).wait()


def join(code, far, own, parts):
    hbm = pl.BlockSpec(memory_space=pl.ANY)
    smem = pl.BlockSpec(memory_space=pltpu.SMEM)
    rows = own.shape[0] // len(parts)
    return pl.pallas_call(
        join_kernel,
        grid=(len(parts),),
        in_specs=[smem, smem, hbm] + [hbm] * len(parts),
        out_specs=pl.BlockSpec((rows, own.shape[1]), lambda i: (i, 0)),
        out_shape=jax.ShapeDtypeStruct(own.shape, own.dtype),
        scratch_shapes=[pltpu.SemaphoreType.DMA],
        compiler_params=pltpu.CompilerParams(vmem_limit_bytes=24 * 2**20),
        cost_estimate=pl.CostEstimate(
            flops=0, bytes_accessed=4 * own.size, transcendentals=0
        ),
        name="join_pieces",
    )(code, far, own, *parts)


def norm_parts(values):
    row_mean = jnp.mean(values, axis=-1, keepdims=True)
    centered = values - row_mean
    row_var = jnp.mean(centered * centered, axis=-1, keepdims=True)
    inverse = lax.rsqrt(row_var + norm_eps)
    return centered * inverse, inverse


def norm_back(values, gain, grads):
    hat, inverse = norm_parts(values)
    scaled = grads * gain
    out = inverse * (
        scaled
        - jnp.mean(scaled, axis=-1, keepdims=True)
        - hat * jnp.mean(scaled * hat, axis=-1, keepdims=True)
    )
    return out, jnp.sum(grads * hat, axis=0), jnp.sum(grads, axis=0)


def halve(kept, came, bit, index):
    outer = kept.shape[0] // (2 * bit)

    def pick(value, which):
        value = value.reshape((outer, 2, bit) + value.shape[1:])
        return lax.dynamic_index_in_dim(value, which, 1, keepdims=False).reshape(
            (outer * bit,) + value.shape[3:]
        )

    def part(which):
        value = pick(kept, which).astype(jnp.float32)
        if came is not None:
            value = value + pick(came, which).astype(jnp.float32)
        return value.astype(jnp.bfloat16)

    return part(index), part(1 - index)


def reduce_rows(grads, order, places):
    core, y_at, z_low, z_high = places
    width = grads.shape[1]
    kept = grads.reshape(16, grads.shape[0] // 16, width)
    came = None
    left = ["core", "y", "low", "high"]
    spot = {"core": core, "y": y_at, "low": z_low, "high": z_high}
    flips = {"core": 1, "y": 2, "low": 4, "high": 8}
    for step in order:
        if step == "x":
            if came is not None:
                kept = (kept.astype(jnp.float32) + came.astype(jnp.float32)).astype(jnp.bfloat16)
            kept, came = swap(kept), None
            continue
        bit = 1 << left.index(step)
        mine, other = halve(kept, came, bit, spot[step])
        kept, came = mine, flip(other, flips[step])
        left.remove(step)
    return (kept.astype(jnp.float32) + came.astype(jnp.float32))[0]


def sum_everywhere(value):
    value = value + lax.ppermute(value, "tensor", [(0, 1), (1, 0)])
    for bit in (1, 2, 4, 8):
        value = value + flip(value, bit)
    return value


def chip_body(
    tokens,
    segments,
    w_qkv,
    b_qv,
    w_out,
    b_out,
    w_up,
    b_up,
    w_down,
    b_down,
    gain_one,
    shift_one,
    gain_two,
    shift_two,
    cotangent,
):
    f32, bf16 = jnp.float32, jnp.bfloat16
    place = lax.axis_index("dp")
    rank = lax.axis_index("tensor")
    core = core_of(place)
    y_at = (place // 2) % 2
    z_low = (place // 4) % 2
    z_high = place // 8
    places = (core, y_at, z_low, z_high)
    far = (core != rank).astype(jnp.int32).reshape(1)
    core_s = core.astype(jnp.int32).reshape(1)
    half, width = tokens.shape
    length = segments.shape[1]
    heads = w_qkv.shape[1] // (3 * HEAD_DIM)

    def fetch(weight, ways, gate):
        rows = weight.shape[0] // ways
        code = y_at if ways == 2 else z_low * 2 + y_at
        piece = lax.dynamic_slice_in_dim(weight, code * rows, rows, 0)
        piece = after(piece, gate) if gate is not None else piece
        first = swap_far(piece)
        parts = [first, flip_far(first, 2)]
        if ways == 4:
            parts += [flip_far(parts[0], 4), flip_far(parts[1], 4)]
        return join(code.astype(jnp.int32).reshape(1), far, weight, parts), first

    source_b = swap(tokens)
    qkv_w, gate = fetch(w_qkv, 2, None)
    biases = swap(jnp.concatenate([b_qv, b_up]))
    b_qv_l, b_up_l = biases[: b_qv.shape[0]], biases[b_qv.shape[0] :]
    out_w, _ = fetch(w_out, 2, None)
    up_w, _ = fetch(w_up, 4, gate)
    seed_mine = swap(after(cotangent, gate))
    down_w, _ = fetch(w_down, 4, gate)
    segment = jnp.where(core == rank, segments, flip(segments, 1))
    seg_col = segment.reshape(length, 1)

    head_index = core * heads + lax.iota(jnp.int32, heads)
    slopes = 2.0 ** (-8.0 * (head_index + 1).astype(f32) / HEADS)
    gain_one_f = gain_one.astype(f32)
    gain_two_f = gain_two.astype(f32)

    source = source_b.astype(f32)
    normed = layer_norm(source, gain_one_f, shift_one.astype(f32)).astype(bf16)
    rows_one = jnp.concatenate([normed, flip(normed, 1)], axis=0)
    pair = b_qv_l.astype(f32).reshape(heads, 2, HEAD_DIM)
    bias = jnp.stack([pair[:, 0], jnp.zeros_like(pair[:, 0]), pair[:, 1]], axis=1).reshape(-1)
    joined = (jnp.dot(rows_one, qkv_w, preferred_element_type=f32) + bias).astype(bf16)
    joined = joined.reshape(2, half, joined.shape[1])
    mixed, totals = attend(core_s, slopes, joined, seg_col, segment)

    came = flip(jnp.dot(mixed[1], out_w, preferred_element_type=f32).astype(bf16), 1)
    resid = (
        source
        + jnp.dot(mixed[0], out_w, preferred_element_type=f32)
        + came.astype(f32)
        + b_out.astype(f32)
    )
    normed = layer_norm(resid, gain_two_f, shift_two.astype(f32)).astype(bf16)
    rows_two = jnp.concatenate([normed, flip(normed, 1)], axis=0)
    seed_rows = jnp.concatenate([seed_mine, flip(seed_mine, 1)], axis=0)
    pre_act = jnp.dot(rows_two, up_w, preferred_element_type=f32) + b_up_l.astype(f32)
    hidden, gelu_pull = jax.vjp(partial(jax.nn.gelu, approximate=True), pre_act)
    slope_act = gelu_pull(jnp.ones_like(pre_act))[0].astype(bf16)
    hidden = hidden.astype(bf16)
    came = flip(jnp.dot(hidden[half:], down_w, preferred_element_type=f32).astype(bf16), 1)
    layer_out = (
        resid
        + jnp.dot(hidden[:half], down_w, preferred_element_type=f32)
        + came.astype(f32)
        + b_down.astype(f32)
    )
    layer_out = swap(layer_out.astype(bf16))

    grad_pre_f = contract_cols(seed_rows, down_w) * slope_act.astype(f32)
    grad_pre = grad_pre_f.astype(bf16)
    grad_b_up = jnp.sum(grad_pre.astype(f32), axis=0)
    came = flip(contract_cols(grad_pre[half:], up_w).astype(bf16), 1)
    grad_normed = contract_cols(grad_pre[:half], up_w) + came.astype(f32)
    grad_down = contract_rows(seed_rows, hidden).astype(bf16)
    sum_down = reduce_rows(grad_down, ("x", "core", "y", "low", "high"), places).T
    grad_up = contract_rows(rows_two, grad_pre).astype(bf16)
    sum_up = reduce_rows(grad_up, ("y", "x", "core", "low", "high"), places)
    grad_norm, grad_gain_two, grad_shift_two = norm_back(resid, gain_two_f, grad_normed)
    seed = seed_mine.astype(f32)
    grad_resid = seed + grad_norm
    branch = grad_resid.astype(bf16)
    branch_rows = jnp.concatenate([branch, flip(branch, 1)], axis=0)
    grad_mixed = contract_cols(branch_rows, out_w).astype(bf16).reshape(mixed.shape)
    grad_joined, qv_sums = attend_back(core_s, slopes, joined, grad_mixed, totals, seg_col, segment)
    grad_out = contract_rows(branch_rows, mixed.reshape(2 * half, -1)).astype(bf16)
    sum_out = reduce_rows(grad_out, ("x", "core", "y", "low", "high"), places).T
    grad_joined = grad_joined.reshape(2 * half, -1)
    grad_qkv = contract_rows(rows_one, grad_joined).astype(bf16)
    sum_qkv = reduce_rows(grad_qkv, ("y", "x", "core", "low", "high"), places)
    came = flip(contract_cols(grad_joined[half:], qkv_w).astype(bf16), 1)
    grad_normed = contract_cols(grad_joined[:half], qkv_w) + came.astype(f32)
    grad_source, grad_gain_one, grad_shift_one = norm_back(source, gain_one_f, grad_normed)
    input_grad = swap((grad_resid + grad_source).astype(bf16))

    small = sum_everywhere(
        jnp.concatenate(
            [
                jnp.sum(grad_resid, axis=0),
                grad_gain_two,
                grad_shift_two,
                jnp.sum(seed, axis=0),
                grad_gain_one,
                grad_shift_one,
                spread_slots(grad_b_up, core, 2),
                spread_slots(qv_sums.reshape(-1), core, 2),
            ]
        )
    )
    up_width = grad_b_up.shape[0]
    qv_width = b_qv.shape[0]
    up_from, qv_from = 6 * width, 6 * width + 2 * up_width
    sum_b_up = lax.dynamic_slice_in_dim(small, up_from + rank * up_width, up_width)
    sum_b_qv = lax.dynamic_slice_in_dim(small, qv_from + rank * qv_width, qv_width)
    rows = [small[i * width : (i + 1) * width] for i in range(6)]
    return (
        layer_out,
        input_grad,
        sum_qkv,
        sum_b_qv,
        sum_out,
        rows[0],
        sum_up,
        sum_b_up,
        sum_down,
        rows[3],
        rows[4],
        rows[5],
        rows[1],
        rows[2],
    )


def solution(mesh):
    in_specs = (
        P(("dp", "tensor"), None),
        P("dp", None),
        P(None, "tensor"),
        P("tensor"),
        P("tensor", None),
        P(),
        P(None, "tensor"),
        P("tensor"),
        P("tensor", None),
        P(),
        P(),
        P(),
        P(),
        P(),
        P(("dp", "tensor"), None),
    )
    out_specs = (
        P(("dp", "tensor"), None),
        P(("dp", "tensor"), None),
        P("dp", "tensor"),
        P("tensor"),
        P("tensor", "dp"),
        P(),
        P("dp", "tensor"),
        P("tensor"),
        P("tensor", "dp"),
        P(),
        P(),
        P(),
        P(),
        P(),
    )
    pairs = mesh.shape["tensor"] == 2 and mesh.shape["dp"] == 16
    plan = chip_body if pairs else body
    return jax.shard_map(plan, mesh=mesh, in_specs=in_specs, out_specs=out_specs, check_vma=False)
```

```python
from functools import partial

import jax
import jax.numpy as jnp
from jax import lax
from jax.experimental import pallas as pl
from jax.experimental.pallas import tpu as pltpu
from jax.sharding import PartitionSpec as P

HEADS = 16
HEAD_DIM = 64


norm_eps = 1e-05
masked_fill = -1e30


def layer_norm(values, gain, shift):
    row_mean = jnp.mean(values, axis=-1, keepdims=True)
    centered = values - row_mean
    row_var = jnp.mean(centered * centered, axis=-1, keepdims=True)
    return centered * lax.rsqrt(row_var + norm_eps) * gain + shift


def contract_rows(left, right):
    return lax.dot_general(
        left, right, (((0,), (0,)), ((), ())), preferred_element_type=jnp.float32
    )


def contract_cols(left, right):
    return lax.dot_general(
        left, right, (((1,), (1,)), ((), ())), preferred_element_type=jnp.float32
    )


def spread_slots(local, rank, parts):
    slots = (lax.iota(jnp.int32, parts) == rank).astype(jnp.float32)
    return (slots[:, None] * local[None, :]).reshape(-1)


def masked_scores(query, keys, segment, first, slopes):
    scale = keys.shape[2] ** (-0.5)
    raw = jnp.einsum("qhd,khd->hqk", query, keys, preferred_element_type=jnp.float32) * scale
    rows_at = first + lax.iota(jnp.int32, query.shape[0])
    cols_at = lax.iota(jnp.int32, keys.shape[0])
    distance = (rows_at[:, None] - cols_at[None, :]).astype(jnp.float32)
    seg_rows = segment[first : first + query.shape[0]]
    allowed = (seg_rows[:, None] == segment[None, :]) & (distance >= 0)
    return jnp.where(allowed[None], raw - slopes[:, None, None] * distance[None], masked_fill)


def attend_forward(inputs, slopes, block):
    query, keys, values, segment = inputs
    outputs = []
    totals = []
    for first in range(0, keys.shape[0], block):
        scores = masked_scores(query[first : first + block], keys, segment, first, slopes)
        top = jnp.max(scores, axis=2, keepdims=True)
        log_total = top + jnp.log(jnp.sum(jnp.exp(scores - top), axis=2, keepdims=True))
        probs = jnp.exp(scores - log_total).astype(jnp.bfloat16)
        outputs.append(
            jnp.einsum("hqk,khd->qhd", probs, values, preferred_element_type=jnp.float32)
        )
        totals.append(log_total)
    return (jnp.concatenate(outputs, 0).astype(jnp.bfloat16), jnp.concatenate(totals, 1))


def attend_backward(inputs, slopes, block):
    query, keys, values, segment, log_total, grad_mixed = inputs
    scale = keys.shape[2] ** (-0.5)
    grad_keys = jnp.zeros(keys.shape, jnp.float32)
    grad_values = jnp.zeros(values.shape, jnp.float32)
    grad_query = []
    for first in range(0, keys.shape[0], block):
        rows = query[first : first + block]
        grad_rows = grad_mixed[first : first + block]
        scores = masked_scores(rows, keys, segment, first, slopes)
        probs = jnp.exp(scores - log_total[:, first : first + block])
        grad_probs = jnp.einsum(
            "qhd,khd->hqk", grad_rows, values, preferred_element_type=jnp.float32
        )
        inner = jnp.sum(probs * grad_probs, axis=2, keepdims=True)
        grad_scores = (probs * (grad_probs - inner)).astype(jnp.bfloat16)
        grad_query.append(
            jnp.einsum("hqk,khd->qhd", grad_scores, keys, preferred_element_type=jnp.float32)
            * scale
        )
        grad_keys = (
            grad_keys
            + jnp.einsum("hqk,qhd->khd", grad_scores, rows, preferred_element_type=jnp.float32)
            * scale
        )
        grad_values = grad_values + jnp.einsum(
            "hqk,qhd->khd",
            probs.astype(jnp.bfloat16),
            grad_rows,
            preferred_element_type=jnp.float32,
        )
    grad_query = jnp.concatenate(grad_query, 0)
    return jnp.stack((grad_query, grad_keys, grad_values), axis=2).astype(jnp.bfloat16)


def body(
    tokens,
    segments,
    w_qkv,
    b_qv,
    w_out,
    b_out,
    w_up,
    b_up,
    w_down,
    b_down,
    gain_one,
    shift_one,
    gain_two,
    shift_two,
    cotangent,
):
    rank = lax.axis_index("tensor")
    parts = lax.axis_size("tensor")
    count, length = segments.shape
    head_dim = HEAD_DIM
    local_heads = w_qkv.shape[1] // (3 * head_dim)
    block = length // 2
    rows_total = count * length
    local_rows = tokens.shape[0]
    head_index = rank * local_heads + lax.iota(jnp.int32, local_heads)
    slopes = 2.0 ** (-8.0 * (head_index + 1).astype(jnp.float32) / HEADS)
    gain_one_f = gain_one.astype(jnp.float32)
    shift_one_f = shift_one.astype(jnp.float32)
    gain_two_f = gain_two.astype(jnp.float32)
    shift_two_f = shift_two.astype(jnp.float32)
    source = tokens.astype(jnp.float32)
    normed_one = layer_norm(source, gain_one_f, shift_one_f).astype(jnp.bfloat16)
    rows_one = lax.all_gather(normed_one, "tensor", axis=0, tiled=True)
    joined = jnp.dot(rows_one, w_qkv, preferred_element_type=jnp.float32).reshape(
        count, length, local_heads, 3, head_dim
    )
    bias_pair = b_qv.astype(jnp.float32).reshape(local_heads, 2, head_dim)
    query = (joined[:, :, :, 0] + bias_pair[:, 0]).astype(jnp.bfloat16)
    keys = joined[:, :, :, 1].astype(jnp.bfloat16)
    values = (joined[:, :, :, 2] + bias_pair[:, 1]).astype(jnp.bfloat16)
    mixed, log_total = lax.map(
        partial(attend_forward, slopes=slopes, block=block), (query, keys, values, segments)
    )
    mixed = mixed.reshape(rows_total, local_heads * head_dim)
    attn_part = lax.psum_scatter(
        jnp.dot(
            lax.slice_in_dim(mixed, 0, local_rows * lax.axis_size("tensor"), axis=0),
            w_out,
            preferred_element_type=jnp.float32,
        ).astype(jnp.bfloat16),
        "tensor",
        scatter_dimension=0,
        tiled=True,
    ).astype(jnp.float32)
    resid = source + attn_part + b_out.astype(jnp.float32)
    normed_two = layer_norm(resid, gain_two_f, shift_two_f).astype(jnp.bfloat16)
    rows_two = lax.all_gather(normed_two, "tensor", axis=0, tiled=True)
    pre_act = jnp.dot(rows_two, w_up, preferred_element_type=jnp.float32) + b_up.astype(jnp.float32)
    hidden = jax.nn.gelu(pre_act, approximate=True).astype(jnp.bfloat16)
    mlp_part = lax.psum_scatter(
        jnp.dot(
            lax.slice_in_dim(hidden, 0, local_rows * lax.axis_size("tensor"), axis=0),
            w_down,
            preferred_element_type=jnp.float32,
        ).astype(jnp.bfloat16),
        "tensor",
        scatter_dimension=0,
        tiled=True,
    ).astype(jnp.float32)
    layer_out = resid + mlp_part + b_down.astype(jnp.float32)
    piece = lax.all_gather(cotangent, "tensor", axis=0, tiled=True)
    start = jnp.int32(0)
    grad_down = jnp.zeros((hidden.shape[1], cotangent.shape[1]), jnp.float32)
    grad_hidden = jnp.zeros(hidden.shape, jnp.float32)
    grad_down = grad_down + contract_rows(
        lax.dynamic_slice_in_dim(hidden, start, piece.shape[0], 0), piece
    )
    grad_hidden = lax.dynamic_update_slice_in_dim(
        grad_hidden, contract_cols(piece, w_down), start, 0
    )
    grad_down, grad_hidden = (grad_down, grad_hidden)
    unused, gelu_pull = jax.vjp(partial(jax.nn.gelu, approximate=True), pre_act)
    grad_pre = gelu_pull(grad_hidden)[0].astype(jnp.bfloat16)
    grad_up = contract_rows(rows_two, grad_pre)
    grad_b_up = jnp.sum(grad_pre.astype(jnp.float32), axis=0)
    grad_normed_two = lax.psum_scatter(
        contract_cols(
            lax.slice_in_dim(grad_pre, 0, local_rows * lax.axis_size("tensor"), axis=0), w_up
        ).astype(jnp.bfloat16),
        "tensor",
        scatter_dimension=0,
        tiled=True,
    ).astype(jnp.float32)
    unused, norm_two_pull = jax.vjp(layer_norm, resid, gain_two_f, shift_two_f)
    grad_resid_norm, grad_gain_two, grad_shift_two = norm_two_pull(grad_normed_two)
    seed = cotangent.astype(jnp.float32)
    grad_resid = seed + grad_resid_norm
    branch_grad = grad_resid.astype(jnp.bfloat16)
    piece = lax.all_gather(branch_grad, "tensor", axis=0, tiled=True)
    start = jnp.int32(0)
    grad_out = jnp.zeros((mixed.shape[1], branch_grad.shape[1]), jnp.float32)
    grad_mixed = jnp.zeros(mixed.shape, jnp.float32)
    grad_out = grad_out + contract_rows(
        lax.dynamic_slice_in_dim(mixed, start, piece.shape[0], 0), piece
    )
    grad_mixed = lax.dynamic_update_slice_in_dim(grad_mixed, contract_cols(piece, w_out), start, 0)
    grad_out, grad_mixed = (grad_out, grad_mixed)
    grad_mixed = grad_mixed.astype(jnp.bfloat16).reshape(count, length, local_heads, head_dim)
    grad_joined = lax.map(
        partial(attend_backward, slopes=slopes, block=block),
        (query, keys, values, segments, log_total, grad_mixed),
    )
    grad_joined = grad_joined.reshape(rows_total, local_heads, 3, head_dim)
    grad_b_qv = jnp.sum(grad_joined[:, :, 0::2].astype(jnp.float32), axis=0).reshape(-1)
    grad_joined = grad_joined.reshape(rows_total, local_heads * 3 * head_dim)
    grad_qkv = contract_rows(rows_one, grad_joined)
    grad_normed_one = lax.psum_scatter(
        contract_cols(
            lax.slice_in_dim(grad_joined, 0, local_rows * lax.axis_size("tensor"), axis=0), w_qkv
        ).astype(jnp.bfloat16),
        "tensor",
        scatter_dimension=0,
        tiled=True,
    ).astype(jnp.float32)
    unused, norm_one_pull = jax.vjp(layer_norm, source, gain_one_f, shift_one_f)
    grad_source, grad_gain_one, grad_shift_one = norm_one_pull(grad_normed_one)
    input_grad = (grad_resid + grad_source).astype(jnp.bfloat16)
    sum_qkv, sum_out, sum_up, sum_down = (
        lax.psum_scatter(
            grad_qkv.astype(jnp.bfloat16), "dp", scatter_dimension=0, tiled=True
        ).astype(jnp.float32),
        lax.psum_scatter(
            grad_out.astype(jnp.bfloat16), "dp", scatter_dimension=1, tiled=True
        ).astype(jnp.float32),
        lax.psum_scatter(
            grad_up.astype(jnp.bfloat16), "dp", scatter_dimension=0, tiled=True
        ).astype(jnp.float32),
        lax.psum_scatter(
            grad_down.astype(jnp.bfloat16), "dp", scatter_dimension=1, tiled=True
        ).astype(jnp.float32),
    )
    small = lax.psum(
        (
            grad_gain_one,
            grad_shift_one,
            jnp.sum(grad_resid, axis=0),
            grad_gain_two,
            grad_shift_two,
            jnp.sum(seed, axis=0),
            spread_slots(grad_b_qv, rank, parts),
            spread_slots(grad_b_up, rank, parts),
        ),
        ("dp", "tensor"),
    )
    qv_width = grad_b_qv.shape[0]
    up_width = grad_b_up.shape[0]
    sum_qv = lax.dynamic_slice_in_dim(small[6], rank * qv_width, qv_width)
    sum_bias_up = lax.dynamic_slice_in_dim(small[7], rank * up_width, up_width)
    return (
        layer_out.astype(jnp.bfloat16),
        input_grad,
        sum_qkv,
        sum_qv,
        sum_out,
        small[2],
        sum_up,
        sum_bias_up,
        sum_down,
        small[5],
        small[0],
        small[1],
        small[3],
        small[4],
    )


PIECE = 256
STRIP = 512
CROSS = [(0, 1), (1, 0)]


def flip_pairs(bit):
    return [(d, d ^ bit) for d in range(16)]


def flip(value, bit):
    return lax.ppermute(value, "dp", flip_pairs(bit))


def cross(value):
    return lax.ppermute(value, "tensor", CROSS)


def barrier(*values):
    return lax.optimization_barrier(values)


def nt(left, right):
    return lax.dot_general(
        left, right, (((1,), (1,)), ((), ())), preferred_element_type=jnp.float32
    )


def nn(left, right):
    return lax.dot_general(
        left, right, (((1,), (0,)), ((), ())), preferred_element_type=jnp.float32
    )


def tn(left, right):
    return lax.dot_general(
        left, right, (((0,), (0,)), ((), ())), preferred_element_type=jnp.float32
    )


def both_halves(mine_ref, other_ref, rank, lanes):
    mine, other = mine_ref[:, lanes], other_ref[:, lanes]
    first = jnp.where(rank == 0, mine, other)
    return jnp.concatenate([first, jnp.where(rank == 0, other, mine)], axis=0)


def scores_of(keys, rows, slope, seg_col, seg_row, first, size):
    part = nt(keys, rows)
    place = lax.broadcasted_iota(jnp.int32, (keys.shape[0], 1), 0)
    part = part + (place - first).astype(jnp.float32) * slope
    same = seg_col[: keys.shape[0]] == seg_row
    shape = (size, size)
    ahead = lax.broadcasted_iota(jnp.int32, shape, 0) <= lax.broadcasted_iota(jnp.int32, shape, 1)
    diag = jnp.where(same[first:] & ahead, part[first:], masked_fill)
    if first == 0:
        return [diag]
    return [jnp.where(same[:first], part[:first], masked_fill), diag]


def attend_kernel(core_ref, slope_ref, mine_ref, other_ref, col_ref, row_ref, mixed_ref, total_ref):
    pair = pl.program_id(0)
    core = core_ref[0]
    half = mine_ref.shape[0]
    length = 2 * half
    size = min(PIECE, half)
    seg_col = col_ref[...]
    for head in range(2):
        at = head * 3 * HEAD_DIM
        keys = both_halves(mine_ref, other_ref, core, slice(at + HEAD_DIM, at + 2 * HEAD_DIM))
        values = both_halves(mine_ref, other_ref, core, slice(at + 2 * HEAD_DIM, at + 3 * HEAD_DIM))
        query = both_halves(mine_ref, other_ref, core, slice(at, at + HEAD_DIM))
        query = query * jnp.bfloat16(HEAD_DIM**-0.5)
        slope = slope_ref[2 * pair + head]
        for first in range(0, length, size):
            side = core if first < half else 1 - core
            rows_at = slice(first % half, first % half + size)
            stop = first + size
            parts = scores_of(
                keys[:stop], query[first:stop], slope, seg_col, row_ref[:, first:stop], first, size
            )
            top = jnp.max(parts[-1], axis=0, keepdims=True)
            if len(parts) > 1:
                top = jnp.maximum(top, jnp.max(parts[0], axis=0, keepdims=True))
            weights = [jnp.exp(part - top) for part in parts]
            total = sum(jnp.sum(part, axis=0, keepdims=True) for part in weights)
            log_total = top + jnp.log(total)
            inverse = 1.0 / total
            probs = [(part * inverse).astype(jnp.bfloat16) for part in weights]
            if len(probs) > 1:
                probs = jnp.concatenate(probs, axis=0)
            else:
                probs = probs[0]
            out = tn(values[:stop], probs)
            mixed_ref[side, rows_at, head * HEAD_DIM : (head + 1) * HEAD_DIM] = out.T.astype(
                jnp.bfloat16
            )
            total_ref[0, head : head + 1, first:stop] = log_total


def attend_back_kernel(
    core_ref,
    slope_ref,
    mine_ref,
    other_ref,
    grad_mine_ref,
    grad_other_ref,
    total_ref,
    col_ref,
    row_ref,
    out_ref,
    sums_ref,
    probs_ref,
    deltas_ref,
):
    pair = pl.program_id(0)
    core = core_ref[0]
    half = mine_ref.shape[0]
    length = 2 * half
    size = min(PIECE, half)
    scale = HEAD_DIM**-0.5
    seg_col = col_ref[...]
    sums = []
    for head in range(2):
        at = head * 3 * HEAD_DIM
        keys = both_halves(mine_ref, other_ref, core, slice(at + HEAD_DIM, at + 2 * HEAD_DIM))
        values = both_halves(mine_ref, other_ref, core, slice(at + 2 * HEAD_DIM, at + 3 * HEAD_DIM))
        query = both_halves(mine_ref, other_ref, core, slice(at, at + HEAD_DIM)) * jnp.bfloat16(scale)
        grads = both_halves(
            grad_mine_ref, grad_other_ref, core, slice(head * HEAD_DIM, (head + 1) * HEAD_DIM)
        )
        slope = slope_ref[2 * pair + head]
        query_sum = jnp.zeros((1, HEAD_DIM), jnp.float32)
        value_sum = jnp.zeros((1, HEAD_DIM), jnp.float32)
        for first in range(0, length, size):
            side = core if first < half else 1 - core
            rows_at = slice(first % half, first % half + size)
            stop = first + size
            parts = scores_of(
                keys[:stop], query[first:stop], slope, seg_col, row_ref[:, first:stop], first, size
            )
            log_total = total_ref[0, head : head + 1, first:stop]
            grad_probs = nt(values[:stop], grads[first:stop])
            probs = [jnp.exp(part - log_total) for part in parts]
            if len(probs) > 1:
                probs = jnp.concatenate(probs, axis=0)
            else:
                probs = probs[0]
            flow = probs * grad_probs
            inner = jnp.sum(flow, axis=0, keepdims=True)
            deltas = (flow - probs * inner).astype(jnp.bfloat16)
            probs_ref[:stop, first:stop] = probs.astype(jnp.bfloat16)
            deltas_ref[:stop, first:stop] = deltas
            grad_query = (tn(keys[:stop], deltas).T * scale).astype(jnp.bfloat16)
            query_sum = query_sum + jnp.sum(
                grad_query.astype(jnp.float32), axis=0, keepdims=True
            )
            out_ref[side, rows_at, at : at + HEAD_DIM] = grad_query
        for first in range(0, length, size):
            side = core if first < half else 1 - core
            rows_at = slice(first % half, first % half + size)
            stop = first + size
            grad_keys = nn(deltas_ref[first:stop, first:], query[first:]).astype(jnp.bfloat16)
            grad_values = nn(probs_ref[first:stop, first:], grads[first:]).astype(jnp.bfloat16)
            value_sum = value_sum + jnp.sum(
                grad_values.astype(jnp.float32), axis=0, keepdims=True
            )
            out_ref[side, rows_at, at + HEAD_DIM : at + 2 * HEAD_DIM] = grad_keys
            out_ref[side, rows_at, at + 2 * HEAD_DIM : at + 3 * HEAD_DIM] = grad_values
        sums += [query_sum, value_sum]
    sums_ref[0] = jnp.concatenate(sums, axis=1)


def attend(rank, slopes, mine, other, seg_col, seg_row):
    half = mine.shape[0]
    heads = slopes.shape[0]
    pairs = heads // 2
    length = 2 * half
    joined = pl.BlockSpec((half, 6 * HEAD_DIM), lambda p, c, s: (0, p))
    return pl.pallas_call(
        attend_kernel,
        grid_spec=pltpu.PrefetchScalarGridSpec(
            num_scalar_prefetch=2,
            grid=(pairs,),
            in_specs=[
                joined,
                joined,
                pl.BlockSpec((length, 1), lambda p, c, s: (0, 0)),
                pl.BlockSpec((1, length), lambda p, c, s: (0, 0)),
            ],
            out_specs=[
                pl.BlockSpec((2, half, 2 * HEAD_DIM), lambda p, c, s: (0, 0, p)),
                pl.BlockSpec((1, 2, length), lambda p, c, s: (p, 0, 0)),
            ],
        ),
        out_shape=[
            jax.ShapeDtypeStruct((2, half, heads * HEAD_DIM), jnp.bfloat16),
            jax.ShapeDtypeStruct((pairs, 2, length), jnp.float32),
        ],
        compiler_params=pltpu.CompilerParams(vmem_limit_bytes=20 * 2**20),
        cost_estimate=free(),
        name="attend_forward",
    )(rank, slopes, mine, other, seg_col, seg_row)


def attend_back(rank, slopes, mine, other, grads, totals, seg_col, seg_row, start, pairs):
    half = mine.shape[0]
    length = 2 * half
    joined = pl.BlockSpec((half, 6 * HEAD_DIM), lambda p, c, s: (0, p + start))
    mixed = pl.BlockSpec((half, 2 * HEAD_DIM), lambda p, c, s: (0, p + start))
    return pl.pallas_call(
        attend_back_kernel,
        grid_spec=pltpu.PrefetchScalarGridSpec(
            num_scalar_prefetch=2,
            grid=(pairs,),
            in_specs=[
                joined,
                joined,
                mixed,
                mixed,
                pl.BlockSpec((1, 2, length), lambda p, c, s: (p + start, 0, 0)),
                pl.BlockSpec((length, 1), lambda p, c, s: (0, 0)),
                pl.BlockSpec((1, length), lambda p, c, s: (0, 0)),
            ],
            out_specs=[
                pl.BlockSpec((2, half, 6 * HEAD_DIM), lambda p, c, s: (0, 0, p)),
                pl.BlockSpec((1, 1, 4 * HEAD_DIM), lambda p, c, s: (p, 0, 0)),
            ],
            scratch_shapes=[
                pltpu.VMEM((length, length), jnp.bfloat16),
                pltpu.VMEM((length, length), jnp.bfloat16),
            ],
        ),
        out_shape=[
            jax.ShapeDtypeStruct((2, half, pairs * 6 * HEAD_DIM), jnp.bfloat16),
            jax.ShapeDtypeStruct((pairs, 1, 4 * HEAD_DIM), jnp.float32),
        ],
        compiler_params=pltpu.CompilerParams(vmem_limit_bytes=20 * 2**20),
        cost_estimate=free(),
        name="attend_backward",
    )(rank, slopes[2 * start :], mine, other, *grads, totals, seg_col, seg_row)


def free():
    return pl.CostEstimate(flops=1000, bytes_accessed=1000, transcendentals=0)


def gelu_parts(v):
    rate, bend = 0.7978845608028654, 0.044715
    square = v * v
    t = 0.5 + 0.5 * jnp.tanh(v * (rate + (rate * bend) * square))
    turn = v * (2.0 * rate + (6.0 * rate * bend) * square)
    return v * t, t * (1.0 + turn * (1.0 - t))


def up_kernel(rows_ref, weight_ref, bias_ref, act_ref, slope_ref):
    rows = rows_ref[...]
    for at in range(0, act_ref.shape[1], STRIP):
        strip = slice(at, at + STRIP)
        act, slope = gelu_parts(nn(rows, weight_ref[:, strip]) + bias_ref[:, strip])
        act_ref[:, strip] = act.astype(act_ref.dtype)
        slope_ref[:, strip] = slope.astype(slope_ref.dtype)


def pull_kernel(rows_ref, weight_ref, slope_ref, out_ref, sum_ref):
    rows = rows_ref[...]

    @pl.when(pl.program_id(0) == 0)
    def _():
        sum_ref[...] = jnp.zeros_like(sum_ref)

    for at in range(0, out_ref.shape[1], STRIP):
        strip = slice(at, at + STRIP)
        value = nt(rows, weight_ref[strip, :]) * slope_ref[:, strip].astype(jnp.float32)
        grads = value.astype(jnp.bfloat16)
        out_ref[:, strip] = grads
        sum_ref[:, strip] += jnp.sum(grads.astype(jnp.float32), axis=0, keepdims=True)


def units_call(kernel, name, rows, weight, third, wide, outs, tile=256):
    by_rows = pl.BlockSpec((tile, wide), lambda i: (i, 0))
    whole = pl.BlockSpec((1, wide), lambda i: (0, 0))
    specs = {rows.shape[0]: by_rows, 1: whole}
    return pl.pallas_call(
        kernel,
        grid=(rows.shape[0] // tile,),
        in_specs=[
            pl.BlockSpec((tile, rows.shape[1]), lambda i: (i, 0)),
            pl.BlockSpec(weight.shape, lambda i: (0, 0)),
            specs[third.shape[0]],
        ],
        out_specs=[specs[out.shape[0]] for out in outs],
        out_shape=outs,
        compiler_params=pltpu.CompilerParams(vmem_limit_bytes=28 * 2**20),
        cost_estimate=free(),
        name=name,
    )(rows, weight, third)


def outer_kernel(core_ref, mine_ref, other_ref, right_mine, right_other, kept_ref, send_ref, turned):
    half = mine_ref.shape[0]
    count = kept_ref.shape[0]
    size = kept_ref.shape[1]

    @pl.when(pl.program_id(0) == 0)
    def _():
        for part, ref in enumerate((mine_ref, other_ref)):
            value = ref[...].T
            for block in range(2 * count):
                to = ((block % 2) * count + block // 2) * size
                turned[to : to + size, part * half : (part + 1) * half] = value[
                    block * size : (block + 1) * size
                ]

    value = nn(turned[:, :half], right_mine[...]) + nn(turned[:, half:], right_other[...])
    value = value.astype(kept_ref.dtype).reshape(2, count, size, value.shape[1])

    @pl.when(core_ref[0] == 0)
    def _():
        kept_ref[...] = value[0]
        send_ref[...] = value[1]

    @pl.when(core_ref[0] != 0)
    def _():
        kept_ref[...] = value[1]
        send_ref[...] = value[0]


def outer(core, lefts, rights):
    half, deep = lefts[0].shape
    if len(rights) == 1:
        rights, below = rights * 2, 1
    else:
        below = 0
    wide = rights[0].shape[1]
    tile = next(t for t in (512, 384, 256, 128) if wide % t == 0)
    out = pl.BlockSpec((8, deep // 16, tile), lambda n, c: (0, 0, n))
    return pl.pallas_call(
        outer_kernel,
        grid_spec=pltpu.PrefetchScalarGridSpec(
            num_scalar_prefetch=1,
            grid=(wide // tile,),
            in_specs=[
                pl.BlockSpec((half, deep), lambda n, c: (0, 0)),
                pl.BlockSpec((half, deep), lambda n, c: (0, 0)),
                pl.BlockSpec((half, tile), lambda n, c: (0, n)),
                pl.BlockSpec((half, tile), lambda n, c: (below, n)),
            ],
            out_specs=[out, out],
            scratch_shapes=[pltpu.VMEM((deep, 2 * half), jnp.bfloat16)],
        ),
        out_shape=[jax.ShapeDtypeStruct((8, deep // 16, wide), jnp.bfloat16)] * 2,
        compiler_params=pltpu.CompilerParams(vmem_limit_bytes=18 * 2**20),
        cost_estimate=free(),
        name="matmul_outer",
    )(core, *lefts, *rights)


def rows_call(body, name, operands, vectors, outs, sums=0, tile=128):
    rows, wide = operands[0].shape
    by_rows = pl.BlockSpec((tile, wide), lambda i: (i, 0))
    whole = pl.BlockSpec((1, wide), lambda i: (0, 0))
    shapes = [jax.ShapeDtypeStruct((rows, wide), kind) for kind in outs]
    shapes += [jax.ShapeDtypeStruct((1, wide), jnp.float32)] * sums
    count = len(operands) + len(vectors)

    def kernel(*refs):
        values = [ref[...].astype(jnp.float32) for ref in refs[:count]]
        results, totals = body(*values)
        for ref, value in zip(refs[count:], results):
            ref[...] = value.astype(ref.dtype)
        for ref, value in zip(refs[count + len(outs) :], totals):
            part = jnp.sum(value, axis=0, keepdims=True)
            ref[...] = jnp.where(pl.program_id(0) == 0, part, ref[...] + part)

    return pl.pallas_call(
        kernel,
        grid=(rows // tile,),
        in_specs=[by_rows] * len(operands) + [whole] * len(vectors),
        out_specs=[by_rows] * len(outs) + [whole] * sums,
        out_shape=shapes,
        compiler_params=pltpu.CompilerParams(vmem_limit_bytes=16 * 2**20),
        cost_estimate=free(),
        name=name,
    )(*operands, *[v.reshape(1, wide) for v in vectors])


def join_norm(source, mine, came, bias, gain, shift):
    resid = source + mine + came + bias
    return (resid, layer_norm(resid, gain, shift)), ()


def join_out(resid, mine, came, bias):
    return (resid + mine + came + bias,), ()


def norm_two_back(resid, mine, came, seed, gain):
    grads = mine + came
    hat, inverse = norm_parts(resid)
    scaled = grads * gain
    out = seed + inverse * (
        scaled
        - jnp.mean(scaled, axis=-1, keepdims=True)
        - hat * jnp.mean(scaled * hat, axis=-1, keepdims=True)
    )
    return (out,), (grads * hat, grads, out, seed)


def norm_one_back(source, mine, came, resid_grad, gain):
    grads = mine + came
    hat, inverse = norm_parts(source)
    scaled = grads * gain
    out = resid_grad + inverse * (
        scaled
        - jnp.mean(scaled, axis=-1, keepdims=True)
        - hat * jnp.mean(scaled * hat, axis=-1, keepdims=True)
    )
    return (out,), (grads * hat, grads)


def norm_parts(values):
    row_mean = jnp.mean(values, axis=-1, keepdims=True)
    centered = values - row_mean
    row_var = jnp.mean(centered * centered, axis=-1, keepdims=True)
    inverse = lax.rsqrt(row_var + norm_eps)
    return centered * inverse, inverse


def pick(value, bit, which):
    outer = value.shape[0] // (2 * bit)
    value = value.reshape((outer, 2, bit) + value.shape[1:])
    value = lax.dynamic_index_in_dim(value, which, 1, keepdims=False)
    return value.reshape((outer * bit,) + value.shape[2:])


def add_parts(kept, came):
    return (kept.astype(jnp.float32) + came.astype(jnp.float32)).astype(jnp.bfloat16)


def fold(kept, came, bit, which):
    mine, other = pick(kept, bit, which), pick(kept, bit, 1 - which)
    if came is not None:
        mine = add_parts(mine, pick(came, bit, which))
        other = add_parts(other, pick(came, bit, 1 - which))
    return mine, other


def sum_everywhere(value):
    value = value + cross(value)
    for bit in (1, 2, 4, 8):
        value = value + flip(value, bit)
    return value


def chip_body(
    tokens,
    segments,
    w_qkv,
    b_qv,
    w_out,
    b_out,
    w_up,
    b_up,
    w_down,
    b_down,
    gain_one,
    shift_one,
    gain_two,
    shift_two,
    cotangent,
):
    f32, bf16 = jnp.float32, jnp.bfloat16
    place = lax.axis_index("dp")
    rank = lax.axis_index("tensor")
    core, y_at, z_low, z_high = place % 2, (place // 2) % 2, (place // 4) % 2, place // 8
    core_s = core.astype(jnp.int32).reshape(1)
    rank_s = rank.astype(jnp.int32).reshape(1)
    half, width = tokens.shape
    length = segments.shape[1]
    heads = w_qkv.shape[1] // (3 * HEAD_DIM)
    units = w_up.shape[1]
    seg_col = segments.reshape(length, 1)
    head_index = rank * heads + lax.iota(jnp.int32, heads)
    slopes = 2.0 ** (-8.0 * (head_index + 1).astype(f32) / HEADS)

    normed = layer_norm(
        tokens.astype(f32), gain_one.astype(f32), shift_one.astype(f32)
    ).astype(bf16)
    normed_came = cross(normed)
    pair = b_qv.astype(f32).reshape(heads, 2, HEAD_DIM)
    bias = jnp.stack([pair[:, 0], jnp.zeros_like(pair[:, 0]), pair[:, 1]], axis=1).reshape(-1)

    def project(rows):
        return (jnp.dot(rows, w_qkv, preferred_element_type=f32) + bias).astype(bf16)

    joined = [project(normed)]
    joined.append(project(normed_came))
    joined[1], seed = barrier(joined[1], cotangent)
    seed_came = cross(seed)
    mixed, totals = attend(rank_s, slopes, *joined, seg_col, segments)
    mixed, seed_came = barrier(mixed, seed_came)
    sent = jnp.dot(mixed[1], w_out, preferred_element_type=f32).astype(bf16)
    came = cross(sent)
    mine = jnp.dot(mixed[0], w_out, preferred_element_type=f32).astype(bf16)
    resid, normed_two = rows_call(
        join_norm, "join_norm", [tokens, mine, came], [b_out, gain_two, shift_two], [f32, bf16]
    )
    two_came = cross(normed_two)
    wide = jax.ShapeDtypeStruct((half, units), bf16)
    b_up_f = b_up.astype(f32).reshape(1, units)

    def lift(rows):
        return units_call(up_kernel, "matmul_up", rows, w_up, b_up_f, units, [wide] * 2)

    act_mine, slope_mine = lift(normed_two)
    two_came, act_mine = barrier(two_came, act_mine)
    act_other, slope_other = lift(two_came)

    sums = jax.ShapeDtypeStruct((1, units), f32)

    def pull(rows, slope):
        return units_call(pull_kernel, "matmul_pull", rows, w_down, slope, units, [wide, sums])

    grad_other, sum_other = pull(seed_came, slope_other)
    came = cross(contract_cols(grad_other, w_up).astype(bf16))
    grad_mine, sum_mine = pull(seed, slope_mine)
    grad_b_up = (sum_mine + sum_other)[0]
    mine = contract_cols(grad_mine, w_up).astype(bf16)
    act_mine, mine, act_other = barrier(act_mine, mine, act_other)
    down_kept, down_send = outer(core_s, [seed, seed_came], [act_mine, act_other])
    down_came = flip(down_send, 1)
    up_kept, up_send = outer(core_s, [normed_two, two_came], [grad_mine, grad_other])
    up_came = flip(up_send, 1)
    came, up_send, act_other = barrier(came, up_send, act_other)
    branch, grad_gain_two, grad_shift_two, sum_resid, sum_seed = rows_call(
        norm_two_back, "norm_two_back", [resid, mine, came, seed], [gain_two], [bf16], 4
    )
    branch_came = cross(branch)
    down_came, branch, act_other = barrier(down_came, branch, act_other)
    down_kept, down_send = fold(down_kept, down_came, 1, y_at)
    up_kept, up_send = fold(up_kept, up_came, 1, y_at)
    ff_kept = jnp.concatenate([down_kept, up_kept], axis=2)
    ff_came = flip(jnp.concatenate([down_send, up_send], axis=2), 2)
    down_sent = jnp.dot(act_other, w_down, preferred_element_type=f32).astype(bf16)
    down_mine = jnp.dot(act_mine, w_down, preferred_element_type=f32).astype(bf16)
    grad_mixed = [contract_cols(branch, w_out).astype(bf16)]
    grad_mixed[0], branch_came, down_sent, down_mine = barrier(
        grad_mixed[0], branch_came, down_sent, down_mine
    )
    grad_mixed.append(contract_cols(branch_came, w_out).astype(bf16))

    out_came = cross(down_sent)
    pairs = heads // 4
    back_one, sums_one = attend_back(
        rank_s, slopes, *joined, grad_mixed, totals, seg_col, segments, 0, pairs
    )
    back_one, ff_came, branch_came = barrier(back_one.reshape(length, -1), ff_came, branch_came)
    ff_kept, ff_send = fold(ff_kept, ff_came, 1, z_low)
    ff_came = flip(ff_send, 4)
    one_kept, one_send = outer(core_s, [normed, normed_came], [back_one])
    one_came = flip(one_send, 1)
    proj_kept, proj_send = outer(core_s, [branch, branch_came], [mixed.reshape(length, -1)])
    proj_came = flip(proj_send, 1)
    one_kept, one_send = fold(one_kept, one_came, 1, y_at)
    proj_kept, proj_send = fold(proj_kept, proj_came, 1, y_at)
    a_kept = jnp.concatenate([one_kept, proj_kept], axis=2)
    a_send = jnp.concatenate([one_send, proj_send], axis=2)
    a_came = flip(a_send, 2)
    joined[1], a_send, ff_send, out_came = barrier(joined[1], a_send, ff_send, out_came)
    back_two, sums_two = attend_back(
        rank_s, slopes, *joined, grad_mixed, totals, seg_col, segments, pairs, pairs
    )
    (layer_out,) = rows_call(join_out, "join_out", [resid, down_mine, out_came], [b_down], [bf16])
    back_two = back_two.reshape(length, -1)
    back_two, a_came, ff_came = barrier(back_two, a_came, ff_came)
    cut = back_one.shape[1]

    def to_rows(rows):
        return (
            contract_cols(back_one[rows], w_qkv[:, :cut])
            + contract_cols(back_two[rows], w_qkv[:, cut:])
        ).astype(bf16)

    sent = to_rows(slice(half, None))
    came = cross(sent)
    back_two, sent = barrier(back_two, sent)
    two_kept, two_send = outer(core_s, [normed, normed_came], [back_two])
    b_came = flip(two_send, 1)
    two_send, ff_came, a_came = barrier(two_send, ff_came, a_came)
    ff_kept, ff_send = fold(ff_kept, ff_came, 1, z_high)
    ff_came = flip(ff_send, 8)
    b_kept, b_send = fold(two_kept, b_came, 1, y_at)
    b_came = flip(b_send, 2)
    a_kept, a_send = fold(a_kept, a_came, 1, z_low)
    a_came = flip(a_send, 4)
    mine = to_rows(slice(0, half))
    b_kept, b_send = fold(b_kept, b_came, 1, z_low)
    b_came = flip(b_send, 4)
    a_kept, a_send = fold(a_kept, a_came, 1, z_high)
    b_kept, b_send = fold(b_kept, b_came, 1, z_high)
    t_kept = jnp.concatenate([a_kept, b_kept], axis=2)
    t_came = flip(jnp.concatenate([a_send, b_send], axis=2), 8)

    def last(kept, came):
        return (kept.astype(f32) + came.astype(f32))[0]

    sum_ff = last(ff_kept, ff_came)
    sum_down, sum_up = sum_ff[:, :units].T, sum_ff[:, units:]
    sum_rest = last(t_kept, t_came)
    split = cut + w_out.shape[0]
    sum_qkv = jnp.concatenate([sum_rest[:, :cut], sum_rest[:, split:]], axis=1)
    sum_out = sum_rest[:, cut:split].T
    input_grad, grad_gain_one, grad_shift_one = rows_call(
        norm_one_back, "norm_one_back", [tokens, mine, came, branch], [gain_one], [bf16], 2
    )
    qv_sums = jnp.concatenate([sums_one.reshape(-1), sums_two.reshape(-1)])
    small = sum_everywhere(
        jnp.concatenate(
            [
                sum_resid[0],
                grad_gain_two[0],
                grad_shift_two[0],
                sum_seed[0],
                grad_gain_one[0],
                grad_shift_one[0],
                spread_slots(grad_b_up, rank, 2),
                spread_slots(qv_sums, rank, 2),
            ]
        )
    )
    up_width = grad_b_up.shape[0]
    qv_width = b_qv.shape[0]
    up_from, qv_from = 6 * width, 6 * width + 2 * up_width
    sum_b_up = lax.dynamic_slice_in_dim(small, up_from + rank * up_width, up_width)
    sum_b_qv = lax.dynamic_slice_in_dim(small, qv_from + rank * qv_width, qv_width)
    rows = [small[i * width : (i + 1) * width] for i in range(6)]
    return (
        layer_out,
        input_grad,
        sum_qkv,
        sum_b_qv,
        sum_out,
        rows[0],
        sum_up,
        sum_b_up,
        sum_down,
        rows[3],
        rows[4],
        rows[5],
        rows[1],
        rows[2],
    )


def solution(mesh):
    in_specs = (
        P(("dp", "tensor"), None),
        P("dp", None),
        P(None, "tensor"),
        P("tensor"),
        P("tensor", None),
        P(),
        P(None, "tensor"),
        P("tensor"),
        P("tensor", None),
        P(),
        P(),
        P(),
        P(),
        P(),
        P(("dp", "tensor"), None),
    )
    out_specs = (
        P(("dp", "tensor"), None),
        P(("dp", "tensor"), None),
        P("dp", "tensor"),
        P("tensor"),
        P("tensor", "dp"),
        P(),
        P("dp", "tensor"),
        P("tensor"),
        P("tensor", "dp"),
        P(),
        P(),
        P(),
        P(),
        P(),
    )
    pairs = mesh.shape["tensor"] == 2 and mesh.shape["dp"] == 16
    plan = chip_body if pairs else body
    return jax.shard_map(plan, mesh=mesh, in_specs=in_specs, out_specs=out_specs, check_vma=False)
```

```python
from functools import partial

import jax
import jax.numpy as jnp
from jax import lax
from jax.experimental import pallas as pl
from jax.experimental.pallas import tpu as pltpu
from jax.sharding import PartitionSpec as P

HEADS = 16
HEAD_DIM = 64


norm_eps = 1e-05
masked_fill = -1e30


def layer_norm(values, gain, shift):
    row_mean = jnp.mean(values, axis=-1, keepdims=True)
    centered = values - row_mean
    row_var = jnp.mean(centered * centered, axis=-1, keepdims=True)
    return centered * lax.rsqrt(row_var + norm_eps) * gain + shift


def contract_rows(left, right):
    return lax.dot_general(
        left, right, (((0,), (0,)), ((), ())), preferred_element_type=jnp.float32
    )


def contract_cols(left, right):
    return lax.dot_general(
        left, right, (((1,), (1,)), ((), ())), preferred_element_type=jnp.float32
    )


def spread_slots(local, rank, parts):
    slots = (lax.iota(jnp.int32, parts) == rank).astype(jnp.float32)
    return (slots[:, None] * local[None, :]).reshape(-1)


def masked_scores(query, keys, segment, first, slopes):
    scale = keys.shape[2] ** (-0.5)
    raw = jnp.einsum("qhd,khd->hqk", query, keys, preferred_element_type=jnp.float32) * scale
    rows_at = first + lax.iota(jnp.int32, query.shape[0])
    cols_at = lax.iota(jnp.int32, keys.shape[0])
    distance = (rows_at[:, None] - cols_at[None, :]).astype(jnp.float32)
    seg_rows = segment[first : first + query.shape[0]]
    allowed = (seg_rows[:, None] == segment[None, :]) & (distance >= 0)
    return jnp.where(allowed[None], raw - slopes[:, None, None] * distance[None], masked_fill)


def attend_forward(inputs, slopes, block):
    query, keys, values, segment = inputs
    outputs = []
    totals = []
    for first in range(0, keys.shape[0], block):
        scores = masked_scores(query[first : first + block], keys, segment, first, slopes)
        top = jnp.max(scores, axis=2, keepdims=True)
        log_total = top + jnp.log(jnp.sum(jnp.exp(scores - top), axis=2, keepdims=True))
        probs = jnp.exp(scores - log_total).astype(jnp.bfloat16)
        outputs.append(
            jnp.einsum("hqk,khd->qhd", probs, values, preferred_element_type=jnp.float32)
        )
        totals.append(log_total)
    return (jnp.concatenate(outputs, 0).astype(jnp.bfloat16), jnp.concatenate(totals, 1))


def attend_backward(inputs, slopes, block):
    query, keys, values, segment, log_total, grad_mixed = inputs
    scale = keys.shape[2] ** (-0.5)
    grad_keys = jnp.zeros(keys.shape, jnp.float32)
    grad_values = jnp.zeros(values.shape, jnp.float32)
    grad_query = []
    for first in range(0, keys.shape[0], block):
        rows = query[first : first + block]
        grad_rows = grad_mixed[first : first + block]
        scores = masked_scores(rows, keys, segment, first, slopes)
        probs = jnp.exp(scores - log_total[:, first : first + block])
        grad_probs = jnp.einsum(
            "qhd,khd->hqk", grad_rows, values, preferred_element_type=jnp.float32
        )
        inner = jnp.sum(probs * grad_probs, axis=2, keepdims=True)
        grad_scores = (probs * (grad_probs - inner)).astype(jnp.bfloat16)
        grad_query.append(
            jnp.einsum("hqk,khd->qhd", grad_scores, keys, preferred_element_type=jnp.float32)
            * scale
        )
        grad_keys = (
            grad_keys
            + jnp.einsum("hqk,qhd->khd", grad_scores, rows, preferred_element_type=jnp.float32)
            * scale
        )
        grad_values = grad_values + jnp.einsum(
            "hqk,qhd->khd",
            probs.astype(jnp.bfloat16),
            grad_rows,
            preferred_element_type=jnp.float32,
        )
    grad_query = jnp.concatenate(grad_query, 0)
    return jnp.stack((grad_query, grad_keys, grad_values), axis=2).astype(jnp.bfloat16)


def body(
    tokens,
    segments,
    w_qkv,
    b_qv,
    w_out,
    b_out,
    w_up,
    b_up,
    w_down,
    b_down,
    gain_one,
    shift_one,
    gain_two,
    shift_two,
    cotangent,
):
    rank = lax.axis_index("tensor")
    parts = lax.axis_size("tensor")
    count, length = segments.shape
    head_dim = HEAD_DIM
    local_heads = w_qkv.shape[1] // (3 * head_dim)
    block = length // 2
    rows_total = count * length
    local_rows = tokens.shape[0]
    head_index = rank * local_heads + lax.iota(jnp.int32, local_heads)
    slopes = 2.0 ** (-8.0 * (head_index + 1).astype(jnp.float32) / HEADS)
    gain_one_f = gain_one.astype(jnp.float32)
    shift_one_f = shift_one.astype(jnp.float32)
    gain_two_f = gain_two.astype(jnp.float32)
    shift_two_f = shift_two.astype(jnp.float32)
    source = tokens.astype(jnp.float32)
    normed_one = layer_norm(source, gain_one_f, shift_one_f).astype(jnp.bfloat16)
    rows_one = lax.all_gather(normed_one, "tensor", axis=0, tiled=True)
    joined = jnp.dot(rows_one, w_qkv, preferred_element_type=jnp.float32).reshape(
        count, length, local_heads, 3, head_dim
    )
    bias_pair = b_qv.astype(jnp.float32).reshape(local_heads, 2, head_dim)
    query = (joined[:, :, :, 0] + bias_pair[:, 0]).astype(jnp.bfloat16)
    keys = joined[:, :, :, 1].astype(jnp.bfloat16)
    values = (joined[:, :, :, 2] + bias_pair[:, 1]).astype(jnp.bfloat16)
    mixed, log_total = lax.map(
        partial(attend_forward, slopes=slopes, block=block), (query, keys, values, segments)
    )
    mixed = mixed.reshape(rows_total, local_heads * head_dim)
    attn_part = lax.psum_scatter(
        jnp.dot(
            lax.slice_in_dim(mixed, 0, local_rows * lax.axis_size("tensor"), axis=0),
            w_out,
            preferred_element_type=jnp.float32,
        ).astype(jnp.bfloat16),
        "tensor",
        scatter_dimension=0,
        tiled=True,
    ).astype(jnp.float32)
    resid = source + attn_part + b_out.astype(jnp.float32)
    normed_two = layer_norm(resid, gain_two_f, shift_two_f).astype(jnp.bfloat16)
    rows_two = lax.all_gather(normed_two, "tensor", axis=0, tiled=True)
    pre_act = jnp.dot(rows_two, w_up, preferred_element_type=jnp.float32) + b_up.astype(jnp.float32)
    hidden = jax.nn.gelu(pre_act, approximate=True).astype(jnp.bfloat16)
    mlp_part = lax.psum_scatter(
        jnp.dot(
            lax.slice_in_dim(hidden, 0, local_rows * lax.axis_size("tensor"), axis=0),
            w_down,
            preferred_element_type=jnp.float32,
        ).astype(jnp.bfloat16),
        "tensor",
        scatter_dimension=0,
        tiled=True,
    ).astype(jnp.float32)
    layer_out = resid + mlp_part + b_down.astype(jnp.float32)
    piece = lax.all_gather(cotangent, "tensor", axis=0, tiled=True)
    start = jnp.int32(0)
    grad_down = jnp.zeros((hidden.shape[1], cotangent.shape[1]), jnp.float32)
    grad_hidden = jnp.zeros(hidden.shape, jnp.float32)
    grad_down = grad_down + contract_rows(
        lax.dynamic_slice_in_dim(hidden, start, piece.shape[0], 0), piece
    )
    grad_hidden = lax.dynamic_update_slice_in_dim(
        grad_hidden, contract_cols(piece, w_down), start, 0
    )
    grad_down, grad_hidden = (grad_down, grad_hidden)
    unused, gelu_pull = jax.vjp(partial(jax.nn.gelu, approximate=True), pre_act)
    grad_pre = gelu_pull(grad_hidden)[0].astype(jnp.bfloat16)
    grad_up = contract_rows(rows_two, grad_pre)
    grad_b_up = jnp.sum(grad_pre.astype(jnp.float32), axis=0)
    grad_normed_two = lax.psum_scatter(
        contract_cols(
            lax.slice_in_dim(grad_pre, 0, local_rows * lax.axis_size("tensor"), axis=0), w_up
        ).astype(jnp.bfloat16),
        "tensor",
        scatter_dimension=0,
        tiled=True,
    ).astype(jnp.float32)
    unused, norm_two_pull = jax.vjp(layer_norm, resid, gain_two_f, shift_two_f)
    grad_resid_norm, grad_gain_two, grad_shift_two = norm_two_pull(grad_normed_two)
    seed = cotangent.astype(jnp.float32)
    grad_resid = seed + grad_resid_norm
    branch_grad = grad_resid.astype(jnp.bfloat16)
    piece = lax.all_gather(branch_grad, "tensor", axis=0, tiled=True)
    start = jnp.int32(0)
    grad_out = jnp.zeros((mixed.shape[1], branch_grad.shape[1]), jnp.float32)
    grad_mixed = jnp.zeros(mixed.shape, jnp.float32)
    grad_out = grad_out + contract_rows(
        lax.dynamic_slice_in_dim(mixed, start, piece.shape[0], 0), piece
    )
    grad_mixed = lax.dynamic_update_slice_in_dim(grad_mixed, contract_cols(piece, w_out), start, 0)
    grad_out, grad_mixed = (grad_out, grad_mixed)
    grad_mixed = grad_mixed.astype(jnp.bfloat16).reshape(count, length, local_heads, head_dim)
    grad_joined = lax.map(
        partial(attend_backward, slopes=slopes, block=block),
        (query, keys, values, segments, log_total, grad_mixed),
    )
    grad_joined = grad_joined.reshape(rows_total, local_heads, 3, head_dim)
    grad_b_qv = jnp.sum(grad_joined[:, :, 0::2].astype(jnp.float32), axis=0).reshape(-1)
    grad_joined = grad_joined.reshape(rows_total, local_heads * 3 * head_dim)
    grad_qkv = contract_rows(rows_one, grad_joined)
    grad_normed_one = lax.psum_scatter(
        contract_cols(
            lax.slice_in_dim(grad_joined, 0, local_rows * lax.axis_size("tensor"), axis=0), w_qkv
        ).astype(jnp.bfloat16),
        "tensor",
        scatter_dimension=0,
        tiled=True,
    ).astype(jnp.float32)
    unused, norm_one_pull = jax.vjp(layer_norm, source, gain_one_f, shift_one_f)
    grad_source, grad_gain_one, grad_shift_one = norm_one_pull(grad_normed_one)
    input_grad = (grad_resid + grad_source).astype(jnp.bfloat16)
    sum_qkv, sum_out, sum_up, sum_down = (
        lax.psum_scatter(
            grad_qkv.astype(jnp.bfloat16), "dp", scatter_dimension=0, tiled=True
        ).astype(jnp.float32),
        lax.psum_scatter(
            grad_out.astype(jnp.bfloat16), "dp", scatter_dimension=1, tiled=True
        ).astype(jnp.float32),
        lax.psum_scatter(
            grad_up.astype(jnp.bfloat16), "dp", scatter_dimension=0, tiled=True
        ).astype(jnp.float32),
        lax.psum_scatter(
            grad_down.astype(jnp.bfloat16), "dp", scatter_dimension=1, tiled=True
        ).astype(jnp.float32),
    )
    small = lax.psum(
        (
            grad_gain_one,
            grad_shift_one,
            jnp.sum(grad_resid, axis=0),
            grad_gain_two,
            grad_shift_two,
            jnp.sum(seed, axis=0),
            spread_slots(grad_b_qv, rank, parts),
            spread_slots(grad_b_up, rank, parts),
        ),
        ("dp", "tensor"),
    )
    qv_width = grad_b_qv.shape[0]
    up_width = grad_b_up.shape[0]
    sum_qv = lax.dynamic_slice_in_dim(small[6], rank * qv_width, qv_width)
    sum_bias_up = lax.dynamic_slice_in_dim(small[7], rank * up_width, up_width)
    return (
        layer_out.astype(jnp.bfloat16),
        input_grad,
        sum_qkv,
        sum_qv,
        sum_out,
        small[2],
        sum_up,
        sum_bias_up,
        sum_down,
        small[5],
        small[0],
        small[1],
        small[3],
        small[4],
    )


PIECE = 256
STRIP = 512
CROSS = [(0, 1), (1, 0)]


def flip_pairs(bit):
    return [(d, d ^ bit) for d in range(16)]


def flip(value, bit):
    return lax.ppermute(value, "dp", flip_pairs(bit))


def cross(value):
    return lax.ppermute(value, "tensor", CROSS)


def barrier(*values):
    return lax.optimization_barrier(values)


def nt(left, right):
    return lax.dot_general(
        left, right, (((1,), (1,)), ((), ())), preferred_element_type=jnp.float32
    )


def nn(left, right):
    return lax.dot_general(
        left, right, (((1,), (0,)), ((), ())), preferred_element_type=jnp.float32
    )


def tn(left, right):
    return lax.dot_general(
        left, right, (((0,), (0,)), ((), ())), preferred_element_type=jnp.float32
    )


def both_halves(mine_ref, other_ref, rank, lanes):
    mine, other = mine_ref[:, lanes], other_ref[:, lanes]
    first = jnp.where(rank == 0, mine, other)
    return jnp.concatenate([first, jnp.where(rank == 0, other, mine)], axis=0)


def scores_of(keys, rows, slope, seg_col, seg_row, first, size):
    part = nt(keys, rows)
    place = lax.broadcasted_iota(jnp.int32, (keys.shape[0], 1), 0)
    part = part + (place - first).astype(jnp.float32) * slope
    same = seg_col[: keys.shape[0]] == seg_row
    shape = (size, size)
    ahead = lax.broadcasted_iota(jnp.int32, shape, 0) <= lax.broadcasted_iota(jnp.int32, shape, 1)
    diag = jnp.where(same[first:] & ahead, part[first:], masked_fill)
    if first == 0:
        return [diag]
    return [jnp.where(same[:first], part[:first], masked_fill), diag]


def attend_kernel(
    side, rank_ref, slope_ref, mine_ref, other_ref, col_ref, row_ref, mixed_ref, total_ref
):
    pair = pl.program_id(0)
    rank = rank_ref[0]
    half = mine_ref.shape[0]
    size = min(PIECE, half)
    query_ref = (mine_ref, other_ref)[side]
    seg_col = col_ref[...]

    def rows_of(first_row):
        for head in range(2):
            at = head * 3 * HEAD_DIM
            keys = both_halves(mine_ref, other_ref, rank, slice(at + HEAD_DIM, at + 2 * HEAD_DIM))
            values = both_halves(
                mine_ref, other_ref, rank, slice(at + 2 * HEAD_DIM, at + 3 * HEAD_DIM)
            )
            slope = slope_ref[2 * pair + head]
            for near in range(0, half, size):
                first = first_row + near
                stop = first + size
                rows = query_ref[near : near + size, at : at + HEAD_DIM]
                rows = rows * jnp.bfloat16(HEAD_DIM**-0.5)
                parts = scores_of(
                    keys[:stop], rows, slope, seg_col, row_ref[:, first:stop], first, size
                )
                top = jnp.max(parts[-1], axis=0, keepdims=True)
                if len(parts) > 1:
                    top = jnp.maximum(top, jnp.max(parts[0], axis=0, keepdims=True))
                weights = [jnp.exp(part - top) for part in parts]
                total = sum(jnp.sum(part, axis=0, keepdims=True) for part in weights)
                inverse = 1.0 / total
                probs = [(part * inverse).astype(jnp.bfloat16) for part in weights]
                probs = jnp.concatenate(probs, axis=0) if len(probs) > 1 else probs[0]
                out = tn(values[:stop], probs)
                mixed_ref[near : near + size, head * HEAD_DIM : (head + 1) * HEAD_DIM] = (
                    out.T.astype(jnp.bfloat16)
                )
                total_ref[0, head : head + 1, near : near + size] = top + jnp.log(total)

    for number in range(2):

        @pl.when(rank == (number if side == 0 else 1 - number))
        def _():
            rows_of(number * half)


def attend_back_kernel(
    core_ref,
    slope_ref,
    mine_ref,
    other_ref,
    grad_mine_ref,
    grad_other_ref,
    total_mine_ref,
    total_other_ref,
    col_ref,
    row_ref,
    out_ref,
    sums_ref,
    probs_ref,
    deltas_ref,
):
    pair = pl.program_id(0)
    core = core_ref[0]
    half = mine_ref.shape[0]
    length = 2 * half
    size = min(PIECE, half)
    scale = HEAD_DIM**-0.5
    seg_col = col_ref[...]
    totals = [total_mine_ref[0], total_other_ref[0]]
    totals = [
        jnp.where(core == 0, totals[0], totals[1]),
        jnp.where(core == 0, totals[1], totals[0]),
    ]
    sums = []
    for head in range(2):
        at = head * 3 * HEAD_DIM
        keys = both_halves(mine_ref, other_ref, core, slice(at + HEAD_DIM, at + 2 * HEAD_DIM))
        values = both_halves(mine_ref, other_ref, core, slice(at + 2 * HEAD_DIM, at + 3 * HEAD_DIM))
        query = both_halves(mine_ref, other_ref, core, slice(at, at + HEAD_DIM)) * jnp.bfloat16(scale)
        grads = both_halves(
            grad_mine_ref, grad_other_ref, core, slice(head * HEAD_DIM, (head + 1) * HEAD_DIM)
        )
        slope = slope_ref[2 * pair + head]
        query_sum = jnp.zeros((1, HEAD_DIM), jnp.float32)
        value_sum = jnp.zeros((1, HEAD_DIM), jnp.float32)
        for first in range(0, length, size):
            side = core if first < half else 1 - core
            rows_at = slice(first % half, first % half + size)
            stop = first + size
            parts = scores_of(
                keys[:stop], query[first:stop], slope, seg_col, row_ref[:, first:stop], first, size
            )
            log_total = totals[first // half][head : head + 1, rows_at]
            grad_probs = nt(values[:stop], grads[first:stop])
            probs = [jnp.exp(part - log_total) for part in parts]
            if len(probs) > 1:
                probs = jnp.concatenate(probs, axis=0)
            else:
                probs = probs[0]
            flow = probs * grad_probs
            inner = jnp.sum(flow, axis=0, keepdims=True)
            deltas = (flow - probs * inner).astype(jnp.bfloat16)
            probs_ref[:stop, first:stop] = probs.astype(jnp.bfloat16)
            deltas_ref[:stop, first:stop] = deltas
            grad_query = (tn(keys[:stop], deltas).T * scale).astype(jnp.bfloat16)
            query_sum = query_sum + jnp.sum(
                grad_query.astype(jnp.float32), axis=0, keepdims=True
            )
            out_ref[side, rows_at, at : at + HEAD_DIM] = grad_query
        for first in range(0, length, size):
            side = core if first < half else 1 - core
            rows_at = slice(first % half, first % half + size)
            stop = first + size
            grad_keys = nn(deltas_ref[first:stop, first:], query[first:]).astype(jnp.bfloat16)
            grad_values = nn(probs_ref[first:stop, first:], grads[first:]).astype(jnp.bfloat16)
            value_sum = value_sum + jnp.sum(
                grad_values.astype(jnp.float32), axis=0, keepdims=True
            )
            out_ref[side, rows_at, at + HEAD_DIM : at + 2 * HEAD_DIM] = grad_keys
            out_ref[side, rows_at, at + 2 * HEAD_DIM : at + 3 * HEAD_DIM] = grad_values
        sums += [query_sum, value_sum]
    sums_ref[0] = jnp.concatenate(sums, axis=1)


def attend(rank, slopes, mine, other, seg_col, seg_row, side):
    half = mine.shape[0]
    heads = slopes.shape[0]
    pairs = heads // 2
    length = 2 * half
    joined = pl.BlockSpec((half, 6 * HEAD_DIM), lambda p, c, s: (0, p))
    return pl.pallas_call(
        partial(attend_kernel, side),
        grid_spec=pltpu.PrefetchScalarGridSpec(
            num_scalar_prefetch=2,
            grid=(pairs,),
            in_specs=[
                joined,
                joined,
                pl.BlockSpec((length, 1), lambda p, c, s: (0, 0)),
                pl.BlockSpec((1, length), lambda p, c, s: (0, 0)),
            ],
            out_specs=[
                pl.BlockSpec((half, 2 * HEAD_DIM), lambda p, c, s: (0, p)),
                pl.BlockSpec((1, 2, half), lambda p, c, s: (p, 0, 0)),
            ],
        ),
        out_shape=[
            jax.ShapeDtypeStruct((half, heads * HEAD_DIM), jnp.bfloat16),
            jax.ShapeDtypeStruct((pairs, 2, half), jnp.float32),
        ],
        compiler_params=pltpu.CompilerParams(vmem_limit_bytes=20 * 2**20),
        cost_estimate=free(),
        name="attend_forward",
    )(rank, slopes, mine, other, seg_col, seg_row)


def attend_back(rank, slopes, mine, other, grads, totals, seg_col, seg_row, start, pairs):
    half = mine.shape[0]
    length = 2 * half
    joined = pl.BlockSpec((half, 6 * HEAD_DIM), lambda p, c, s: (0, p + start))
    mixed = pl.BlockSpec((half, 2 * HEAD_DIM), lambda p, c, s: (0, p + start))
    return pl.pallas_call(
        attend_back_kernel,
        grid_spec=pltpu.PrefetchScalarGridSpec(
            num_scalar_prefetch=2,
            grid=(pairs,),
            in_specs=[
                joined,
                joined,
                mixed,
                mixed,
                pl.BlockSpec((1, 2, half), lambda p, c, s: (p + start, 0, 0)),
                pl.BlockSpec((1, 2, half), lambda p, c, s: (p + start, 0, 0)),
                pl.BlockSpec((length, 1), lambda p, c, s: (0, 0)),
                pl.BlockSpec((1, length), lambda p, c, s: (0, 0)),
            ],
            out_specs=[
                pl.BlockSpec((2, half, 6 * HEAD_DIM), lambda p, c, s: (0, 0, p)),
                pl.BlockSpec((1, 1, 4 * HEAD_DIM), lambda p, c, s: (p, 0, 0)),
            ],
            scratch_shapes=[
                pltpu.VMEM((length, length), jnp.bfloat16),
                pltpu.VMEM((length, length), jnp.bfloat16),
            ],
        ),
        out_shape=[
            jax.ShapeDtypeStruct((2, half, pairs * 6 * HEAD_DIM), jnp.bfloat16),
            jax.ShapeDtypeStruct((pairs, 1, 4 * HEAD_DIM), jnp.float32),
        ],
        compiler_params=pltpu.CompilerParams(vmem_limit_bytes=20 * 2**20),
        cost_estimate=free(),
        name="attend_backward",
    )(rank, slopes[2 * start :], mine, other, *grads, *totals, seg_col, seg_row)


def free():
    return pl.CostEstimate(flops=1000, bytes_accessed=1000, transcendentals=0)


def gelu_parts(v):
    rate, bend = 0.7978845608028654, 0.044715
    square = v * v
    t = 0.5 + 0.5 * jnp.tanh(v * (rate + (rate * bend) * square))
    turn = v * (2.0 * rate + (6.0 * rate * bend) * square)
    return v * t, t * (1.0 + turn * (1.0 - t))


def up_kernel(rows_ref, weight_ref, bias_ref, act_ref, slope_ref):
    rows = rows_ref[...]
    for at in range(0, act_ref.shape[1], STRIP):
        strip = slice(at, at + STRIP)
        act, slope = gelu_parts(nn(rows, weight_ref[:, strip]) + bias_ref[:, strip])
        act_ref[:, strip] = act.astype(act_ref.dtype)
        slope_ref[:, strip] = slope.astype(slope_ref.dtype)


def pull_kernel(rows_ref, weight_ref, slope_ref, out_ref, sum_ref):
    rows = rows_ref[...]

    @pl.when(pl.program_id(0) == 0)
    def _():
        sum_ref[...] = jnp.zeros_like(sum_ref)

    for at in range(0, out_ref.shape[1], STRIP):
        strip = slice(at, at + STRIP)
        value = nt(rows, weight_ref[strip, :]) * slope_ref[:, strip].astype(jnp.float32)
        grads = value.astype(jnp.bfloat16)
        out_ref[:, strip] = grads
        sum_ref[:, strip] += jnp.sum(grads.astype(jnp.float32), axis=0, keepdims=True)


def units_call(kernel, name, rows, weight, third, wide, outs, tile=256):
    by_rows = pl.BlockSpec((tile, wide), lambda i: (i, 0))
    whole = pl.BlockSpec((1, wide), lambda i: (0, 0))
    specs = {rows.shape[0]: by_rows, 1: whole}
    return pl.pallas_call(
        kernel,
        grid=(rows.shape[0] // tile,),
        in_specs=[
            pl.BlockSpec((tile, rows.shape[1]), lambda i: (i, 0)),
            pl.BlockSpec(weight.shape, lambda i: (0, 0)),
            specs[third.shape[0]],
        ],
        out_specs=[specs[out.shape[0]] for out in outs],
        out_shape=outs,
        compiler_params=pltpu.CompilerParams(vmem_limit_bytes=28 * 2**20),
        cost_estimate=free(),
        name=name,
    )(rows, weight, third)


def outer_kernel(core_ref, mine_ref, other_ref, right_mine, right_other, kept_ref, send_ref, turned):
    half = mine_ref.shape[0]
    count = kept_ref.shape[0]
    size = kept_ref.shape[1]

    @pl.when(pl.program_id(0) == 0)
    def _():
        for part, ref in enumerate((mine_ref, other_ref)):
            value = ref[...].T
            for block in range(2 * count):
                to = ((block % 2) * count + block // 2) * size
                turned[to : to + size, part * half : (part + 1) * half] = value[
                    block * size : (block + 1) * size
                ]

    value = nn(turned[:, :half], right_mine[...]) + nn(turned[:, half:], right_other[...])
    value = value.astype(kept_ref.dtype).reshape(2, count, size, value.shape[1])

    @pl.when(core_ref[0] == 0)
    def _():
        kept_ref[...] = value[0]
        send_ref[...] = value[1]

    @pl.when(core_ref[0] != 0)
    def _():
        kept_ref[...] = value[1]
        send_ref[...] = value[0]


def outer(core, lefts, rights):
    half, deep = lefts[0].shape
    if len(rights) == 1:
        rights, below = rights * 2, 1
    else:
        below = 0
    wide = rights[0].shape[1]
    tile = next(t for t in (512, 384, 256, 128) if wide % t == 0)
    out = pl.BlockSpec((8, deep // 16, tile), lambda n, c: (0, 0, n))
    return pl.pallas_call(
        outer_kernel,
        grid_spec=pltpu.PrefetchScalarGridSpec(
            num_scalar_prefetch=1,
            grid=(wide // tile,),
            in_specs=[
                pl.BlockSpec((half, deep), lambda n, c: (0, 0)),
                pl.BlockSpec((half, deep), lambda n, c: (0, 0)),
                pl.BlockSpec((half, tile), lambda n, c: (0, n)),
                pl.BlockSpec((half, tile), lambda n, c: (below, n)),
            ],
            out_specs=[out, out],
            scratch_shapes=[pltpu.VMEM((deep, 2 * half), jnp.bfloat16)],
        ),
        out_shape=[jax.ShapeDtypeStruct((8, deep // 16, wide), jnp.bfloat16)] * 2,
        compiler_params=pltpu.CompilerParams(vmem_limit_bytes=18 * 2**20),
        cost_estimate=free(),
        name="matmul_outer",
    )(core, *lefts, *rights)


def rows_call(body, name, operands, vectors, outs, sums=0, tile=128):
    rows, wide = operands[0].shape
    by_rows = pl.BlockSpec((tile, wide), lambda i: (i, 0))
    whole = pl.BlockSpec((1, wide), lambda i: (0, 0))
    shapes = [jax.ShapeDtypeStruct((rows, wide), kind) for kind in outs]
    shapes += [jax.ShapeDtypeStruct((1, wide), jnp.float32)] * sums
    count = len(operands) + len(vectors)

    def kernel(*refs):
        values = [ref[...].astype(jnp.float32) for ref in refs[:count]]
        results, totals = body(*values)
        for ref, value in zip(refs[count:], results):
            ref[...] = value.astype(ref.dtype)
        for ref, value in zip(refs[count + len(outs) :], totals):
            part = jnp.sum(value, axis=0, keepdims=True)
            ref[...] = jnp.where(pl.program_id(0) == 0, part, ref[...] + part)

    return pl.pallas_call(
        kernel,
        grid=(rows // tile,),
        in_specs=[by_rows] * len(operands) + [whole] * len(vectors),
        out_specs=[by_rows] * len(outs) + [whole] * sums,
        out_shape=shapes,
        compiler_params=pltpu.CompilerParams(vmem_limit_bytes=16 * 2**20),
        cost_estimate=free(),
        name=name,
    )(*operands, *[v.reshape(1, wide) for v in vectors])


def first_norm(source, gain, shift):
    return (layer_norm(source, gain, shift),), ()


def join_norm(source, mine, came, bias, gain, shift):
    resid = source + mine + came + bias
    return (resid, layer_norm(resid, gain, shift)), ()


def join_out(resid, mine, came, bias):
    return (resid + mine + came + bias,), ()


def norm_two_back(resid, mine, came, seed, gain):
    grads = mine + came
    hat, inverse = norm_parts(resid)
    scaled = grads * gain
    out = seed + inverse * (
        scaled
        - jnp.mean(scaled, axis=-1, keepdims=True)
        - hat * jnp.mean(scaled * hat, axis=-1, keepdims=True)
    )
    return (out,), (grads * hat, grads, out, seed)


def norm_one_back(source, mine, came, resid_grad, gain):
    grads = mine + came
    hat, inverse = norm_parts(source)
    scaled = grads * gain
    out = resid_grad + inverse * (
        scaled
        - jnp.mean(scaled, axis=-1, keepdims=True)
        - hat * jnp.mean(scaled * hat, axis=-1, keepdims=True)
    )
    return (out,), (grads * hat, grads)


def norm_parts(values):
    row_mean = jnp.mean(values, axis=-1, keepdims=True)
    centered = values - row_mean
    row_var = jnp.mean(centered * centered, axis=-1, keepdims=True)
    inverse = lax.rsqrt(row_var + norm_eps)
    return centered * inverse, inverse


def fold_kernel(widths, came, which_ref, *refs):
    count = len(widths)
    step = 2 if came else 1
    ins, (kept_ref, send_ref) = refs[:-2], refs[-2:]
    for out_ref, side in ((kept_ref, 0), (send_ref, 1)):
        at = 0
        for number, wide in enumerate(widths):
            first = (side * count + number) * step
            value = ins[first][...]
            if came:
                value = value.astype(jnp.float32) + ins[first + 1][...].astype(jnp.float32)
            out_ref[:, :, at : at + wide] = value.astype(out_ref.dtype)
            at += wide


def fold(which, *terms):
    widths = [kept.shape[2] for kept, _ in terms]
    blocks, size = terms[0][0].shape[:2]
    came = terms[0][1] is not None
    specs, operands = [], []
    for side in range(2):
        for (kept, other), wide in zip(terms, widths):

            def at(i, w, side=side):
                return (2 * i + (w[0] if side == 0 else 1 - w[0]), 0, 0)

            for value in (kept, other) if came else (kept,):
                specs.append(pl.BlockSpec((1, size, wide), at))
                operands.append(value)
    out = pl.BlockSpec((1, size, sum(widths)), lambda i, w: (i, 0, 0))
    return pl.pallas_call(
        partial(fold_kernel, widths, came),
        grid_spec=pltpu.PrefetchScalarGridSpec(
            num_scalar_prefetch=1,
            grid=(blocks // 2,),
            in_specs=specs,
            out_specs=[out, out],
        ),
        out_shape=[jax.ShapeDtypeStruct((blocks // 2, size, sum(widths)), jnp.bfloat16)] * 2,
        compiler_params=pltpu.CompilerParams(vmem_limit_bytes=16 * 2**20),
        cost_estimate=free(),
        name="fold_halves",
    )(which.astype(jnp.int32).reshape(1), *operands)


def sum_everywhere(value):
    value = value + cross(value)
    for bit in (1, 2, 4, 8):
        value = value + flip(value, bit)
    return value


def chip_body(
    tokens,
    segments,
    w_qkv,
    b_qv,
    w_out,
    b_out,
    w_up,
    b_up,
    w_down,
    b_down,
    gain_one,
    shift_one,
    gain_two,
    shift_two,
    cotangent,
):
    f32, bf16 = jnp.float32, jnp.bfloat16
    place = lax.axis_index("dp")
    rank = lax.axis_index("tensor")
    core, y_at, z_low, z_high = place % 2, (place // 2) % 2, (place // 4) % 2, place // 8
    core_s = core.astype(jnp.int32).reshape(1)
    rank_s = rank.astype(jnp.int32).reshape(1)
    half, width = tokens.shape
    length = segments.shape[1]
    heads = w_qkv.shape[1] // (3 * HEAD_DIM)
    units = w_up.shape[1]
    seg_col = segments.reshape(length, 1)
    head_index = rank * heads + lax.iota(jnp.int32, heads)
    slopes = 2.0 ** (-8.0 * (head_index + 1).astype(f32) / HEADS)

    (normed,) = rows_call(first_norm, "first_norm", [tokens], [gain_one, shift_one], [bf16])
    normed_came = cross(normed)
    pair = b_qv.astype(f32).reshape(heads, 2, HEAD_DIM)
    bias = jnp.stack([pair[:, 0], jnp.zeros_like(pair[:, 0]), pair[:, 1]], axis=1).reshape(-1)

    def project(rows):
        return (jnp.dot(rows, w_qkv, preferred_element_type=f32) + bias).astype(bf16)

    seed_came = cross(cotangent)
    joined = [project(normed)]
    joined[0], normed_came = barrier(joined[0], normed_came)
    joined.append(project(normed_came))
    attend_args = (rank_s, slopes, *joined, seg_col, segments)
    mixed_other, totals_other = attend(*attend_args, 1)
    sent = jnp.dot(mixed_other, w_out, preferred_element_type=f32).astype(bf16)
    came = cross(sent)
    sent, *attend_args = barrier(sent, *attend_args)
    mixed_mine, totals_mine = attend(*attend_args, 0)
    mixed, totals = [mixed_mine, mixed_other], [totals_mine, totals_other]
    mine = jnp.dot(mixed_mine, w_out, preferred_element_type=f32).astype(bf16)
    mine, came, seed_came = barrier(mine, came, seed_came)
    resid, normed_two = rows_call(
        join_norm, "join_norm", [tokens, mine, came], [b_out, gain_two, shift_two], [f32, bf16]
    )
    two_came = cross(normed_two)
    wide = jax.ShapeDtypeStruct((half, units), bf16)
    b_up_f = b_up.astype(f32).reshape(1, units)

    def lift(rows):
        return units_call(up_kernel, "matmul_up", rows, w_up, b_up_f, units, [wide] * 2)

    act_mine, slope_mine = lift(normed_two)

    sums = jax.ShapeDtypeStruct((1, units), f32)

    def pull(rows, slope):
        return units_call(pull_kernel, "matmul_pull", rows, w_down, slope, units, [wide, sums])

    grad_mine, sum_mine = pull(cotangent, slope_mine)
    down_mine = jnp.dot(act_mine, w_down, preferred_element_type=f32).astype(bf16)
    two_came, down_mine, grad_mine = barrier(two_came, down_mine, grad_mine)
    act_other, slope_other = lift(two_came)
    grad_other, sum_other = pull(seed_came, slope_other)
    grad_b_up = (sum_mine + sum_other)[0]
    sent = contract_cols(grad_other, w_up).astype(bf16)
    came = cross(sent)
    sent, act_mine, act_other, grad_mine, grad_other = barrier(
        sent, act_mine, act_other, grad_mine, grad_other
    )
    down_kept, down_send = outer(core_s, [cotangent, seed_came], [act_mine, act_other])
    up_kept, up_send = outer(core_s, [normed_two, two_came], [grad_mine, grad_other])
    mine = contract_cols(grad_mine, w_up).astype(bf16)
    came, mine, up_send, down_send = barrier(came, mine, up_send, down_send)
    down_came = flip(down_send, 1)
    up_came = flip(up_send, 1)
    branch, grad_gain_two, grad_shift_two, sum_resid, sum_seed = rows_call(
        norm_two_back, "norm_two_back", [resid, mine, came, cotangent], [gain_two], [bf16], 4
    )
    branch_came = cross(branch)
    branch, down_came, up_came = barrier(branch, down_came, up_came)
    ff_kept, ff_send = fold(y_at, (down_kept, down_came), (up_kept, up_came))
    down_sent = jnp.dot(act_other, w_down, preferred_element_type=f32).astype(bf16)
    ff_came = flip(ff_send, 2)
    ff_send, branch_b = barrier(ff_send, branch)
    grad_mixed = [contract_cols(branch_b, w_out).astype(bf16)]
    grad_mixed[0], branch_came, down_sent = barrier(grad_mixed[0], branch_came, down_sent)
    grad_mixed.append(contract_cols(branch_came, w_out).astype(bf16))

    grad_mixed[1], down_sent = barrier(grad_mixed[1], down_sent)
    out_came = cross(down_sent)
    pairs = heads // 4
    back_one, sums_one = attend_back(
        rank_s, slopes, *joined, grad_mixed, totals, seg_col, segments, 0, pairs
    )
    back_one, branch_came, mixed[0] = barrier(
        back_one.reshape(length, -1), branch_came, mixed[0]
    )
    one_kept, one_send = outer(core_s, [normed, normed_came], [back_one])
    one_came = flip(one_send, 1)
    proj_kept, proj_send = outer(core_s, [branch, branch_came], mixed)
    proj_came = flip(proj_send, 1)
    proj_send, ff_came = barrier(proj_send, ff_came)
    ff_kept, ff_send = fold(z_low, (ff_kept, ff_came))
    ff_came = flip(ff_send, 4)
    a_kept, a_send = fold(y_at, (one_kept, one_came), (proj_kept, proj_came))
    a_came = flip(a_send, 2)
    joined[1], a_send, ff_send = barrier(joined[1], a_send, ff_send)
    back_two, sums_two = attend_back(
        rank_s, slopes, *joined, grad_mixed, totals, seg_col, segments, pairs, pairs
    )
    back_two = back_two.reshape(length, -1)
    back_two, a_came, out_came = barrier(back_two, a_came, out_came)
    cut = back_one.shape[1]

    def to_rows(rows):
        return (
            contract_cols(back_one[rows], w_qkv[:, :cut])
            + contract_cols(back_two[rows], w_qkv[:, cut:])
        ).astype(bf16)

    sent = to_rows(slice(half, None))
    came = cross(sent)
    back_two, sent = barrier(back_two, sent)
    two_kept, two_send = outer(core_s, [normed, normed_came], [back_two])
    b_came = flip(two_send, 1)
    two_send, ff_came, a_came = barrier(two_send, ff_came, a_came)
    a_kept, a_send = fold(z_low, (a_kept, a_came))
    a_came = flip(a_send, 4)
    ff_kept, ff_send = fold(z_high, (ff_kept, ff_came))
    ff_came = flip(ff_send, 8)
    ff_send, b_came = barrier(ff_send, b_came)
    b_kept, b_send = fold(y_at, (two_kept, b_came))
    b_came = flip(b_send, 2)
    mine = to_rows(slice(0, half))
    mine, b_came = barrier(mine, b_came)
    b_kept, b_send = fold(z_low, (b_kept, b_came))
    b_came = flip(b_send, 4)
    b_send, a_came = barrier(b_send, a_came)
    t_kept, t_send = fold(z_high, (a_kept, a_came), (b_kept, b_came))
    t_came = flip(t_send, 8)
    t_send, came = barrier(t_send, came)
    input_grad, grad_gain_one, grad_shift_one = rows_call(
        norm_one_back, "norm_one_back", [tokens, mine, came, branch], [gain_one], [bf16], 2
    )
    grad_gain_one, down_mine = barrier(grad_gain_one, down_mine)
    (layer_out,) = rows_call(join_out, "join_out", [resid, down_mine, out_came], [b_down], [bf16])

    def last(kept, came):
        return (kept.astype(f32) + came.astype(f32))[0]

    sum_ff = last(ff_kept, ff_came)
    sum_down, sum_up = sum_ff[:, :units].T, sum_ff[:, units:]
    sum_rest = last(t_kept, t_came)
    split = cut + w_out.shape[0]
    sum_qkv = jnp.concatenate([sum_rest[:, :cut], sum_rest[:, split:]], axis=1)
    sum_out = sum_rest[:, cut:split].T
    qv_sums = jnp.concatenate([sums_one.reshape(-1), sums_two.reshape(-1)])
    small = sum_everywhere(
        jnp.concatenate(
            [
                sum_resid[0],
                grad_gain_two[0],
                grad_shift_two[0],
                sum_seed[0],
                grad_gain_one[0],
                grad_shift_one[0],
                spread_slots(grad_b_up, rank, 2),
                spread_slots(qv_sums, rank, 2),
            ]
        )
    )
    up_width = grad_b_up.shape[0]
    qv_width = b_qv.shape[0]
    up_from, qv_from = 6 * width, 6 * width + 2 * up_width
    sum_b_up = lax.dynamic_slice_in_dim(small, up_from + rank * up_width, up_width)
    sum_b_qv = lax.dynamic_slice_in_dim(small, qv_from + rank * qv_width, qv_width)
    rows = [small[i * width : (i + 1) * width] for i in range(6)]
    return (
        layer_out,
        input_grad,
        sum_qkv,
        sum_b_qv,
        sum_out,
        rows[0],
        sum_up,
        sum_b_up,
        sum_down,
        rows[3],
        rows[4],
        rows[5],
        rows[1],
        rows[2],
    )


def solution(mesh):
    in_specs = (
        P(("dp", "tensor"), None),
        P("dp", None),
        P(None, "tensor"),
        P("tensor"),
        P("tensor", None),
        P(),
        P(None, "tensor"),
        P("tensor"),
        P("tensor", None),
        P(),
        P(),
        P(),
        P(),
        P(),
        P(("dp", "tensor"), None),
    )
    out_specs = (
        P(("dp", "tensor"), None),
        P(("dp", "tensor"), None),
        P("dp", "tensor"),
        P("tensor"),
        P("tensor", "dp"),
        P(),
        P("dp", "tensor"),
        P("tensor"),
        P("tensor", "dp"),
        P(),
        P(),
        P(),
        P(),
        P(),
    )
    pairs = mesh.shape["tensor"] == 2 and mesh.shape["dp"] == 16
    plan = chip_body if pairs else body
    return jax.shard_map(plan, mesh=mesh, in_specs=in_specs, out_specs=out_specs, check_vma=False)
```

```python
from functools import partial

import jax
import jax.numpy as jnp
from jax import lax
from jax.experimental import pallas as pl
from jax.experimental.pallas import tpu as pltpu
from jax.sharding import PartitionSpec as P

HEADS = 16
HEAD_DIM = 64


norm_eps = 1e-05
masked_fill = -1e30


def layer_norm(values, gain, shift):
    row_mean = jnp.mean(values, axis=-1, keepdims=True)
    centered = values - row_mean
    row_var = jnp.mean(centered * centered, axis=-1, keepdims=True)
    return centered * lax.rsqrt(row_var + norm_eps) * gain + shift


def contract_rows(left, right):
    return lax.dot_general(
        left, right, (((0,), (0,)), ((), ())), preferred_element_type=jnp.float32
    )


def contract_cols(left, right):
    return lax.dot_general(
        left, right, (((1,), (1,)), ((), ())), preferred_element_type=jnp.float32
    )


def spread_slots(local, rank, parts):
    slots = (lax.iota(jnp.int32, parts) == rank).astype(jnp.float32)
    return (slots[:, None] * local[None, :]).reshape(-1)


def masked_scores(query, keys, segment, first, slopes):
    scale = keys.shape[2] ** (-0.5)
    raw = jnp.einsum("qhd,khd->hqk", query, keys, preferred_element_type=jnp.float32) * scale
    rows_at = first + lax.iota(jnp.int32, query.shape[0])
    cols_at = lax.iota(jnp.int32, keys.shape[0])
    distance = (rows_at[:, None] - cols_at[None, :]).astype(jnp.float32)
    seg_rows = segment[first : first + query.shape[0]]
    allowed = (seg_rows[:, None] == segment[None, :]) & (distance >= 0)
    return jnp.where(allowed[None], raw - slopes[:, None, None] * distance[None], masked_fill)


def attend_forward(inputs, slopes, block):
    query, keys, values, segment = inputs
    outputs = []
    totals = []
    for first in range(0, keys.shape[0], block):
        scores = masked_scores(query[first : first + block], keys, segment, first, slopes)
        top = jnp.max(scores, axis=2, keepdims=True)
        log_total = top + jnp.log(jnp.sum(jnp.exp(scores - top), axis=2, keepdims=True))
        probs = jnp.exp(scores - log_total).astype(jnp.bfloat16)
        outputs.append(
            jnp.einsum("hqk,khd->qhd", probs, values, preferred_element_type=jnp.float32)
        )
        totals.append(log_total)
    return (jnp.concatenate(outputs, 0).astype(jnp.bfloat16), jnp.concatenate(totals, 1))


def attend_backward(inputs, slopes, block):
    query, keys, values, segment, log_total, grad_mixed = inputs
    scale = keys.shape[2] ** (-0.5)
    grad_keys = jnp.zeros(keys.shape, jnp.float32)
    grad_values = jnp.zeros(values.shape, jnp.float32)
    grad_query = []
    for first in range(0, keys.shape[0], block):
        rows = query[first : first + block]
        grad_rows = grad_mixed[first : first + block]
        scores = masked_scores(rows, keys, segment, first, slopes)
        probs = jnp.exp(scores - log_total[:, first : first + block])
        grad_probs = jnp.einsum(
            "qhd,khd->hqk", grad_rows, values, preferred_element_type=jnp.float32
        )
        inner = jnp.sum(probs * grad_probs, axis=2, keepdims=True)
        grad_scores = (probs * (grad_probs - inner)).astype(jnp.bfloat16)
        grad_query.append(
            jnp.einsum("hqk,khd->qhd", grad_scores, keys, preferred_element_type=jnp.float32)
            * scale
        )
        grad_keys = (
            grad_keys
            + jnp.einsum("hqk,qhd->khd", grad_scores, rows, preferred_element_type=jnp.float32)
            * scale
        )
        grad_values = grad_values + jnp.einsum(
            "hqk,qhd->khd",
            probs.astype(jnp.bfloat16),
            grad_rows,
            preferred_element_type=jnp.float32,
        )
    grad_query = jnp.concatenate(grad_query, 0)
    return jnp.stack((grad_query, grad_keys, grad_values), axis=2).astype(jnp.bfloat16)


def body(
    tokens,
    segments,
    w_qkv,
    b_qv,
    w_out,
    b_out,
    w_up,
    b_up,
    w_down,
    b_down,
    gain_one,
    shift_one,
    gain_two,
    shift_two,
    cotangent,
):
    rank = lax.axis_index("tensor")
    parts = lax.axis_size("tensor")
    count, length = segments.shape
    head_dim = HEAD_DIM
    local_heads = w_qkv.shape[1] // (3 * head_dim)
    block = length // 2
    rows_total = count * length
    local_rows = tokens.shape[0]
    head_index = rank * local_heads + lax.iota(jnp.int32, local_heads)
    slopes = 2.0 ** (-8.0 * (head_index + 1).astype(jnp.float32) / HEADS)
    gain_one_f = gain_one.astype(jnp.float32)
    shift_one_f = shift_one.astype(jnp.float32)
    gain_two_f = gain_two.astype(jnp.float32)
    shift_two_f = shift_two.astype(jnp.float32)
    source = tokens.astype(jnp.float32)
    normed_one = layer_norm(source, gain_one_f, shift_one_f).astype(jnp.bfloat16)
    rows_one = lax.all_gather(normed_one, "tensor", axis=0, tiled=True)
    joined = jnp.dot(rows_one, w_qkv, preferred_element_type=jnp.float32).reshape(
        count, length, local_heads, 3, head_dim
    )
    bias_pair = b_qv.astype(jnp.float32).reshape(local_heads, 2, head_dim)
    query = (joined[:, :, :, 0] + bias_pair[:, 0]).astype(jnp.bfloat16)
    keys = joined[:, :, :, 1].astype(jnp.bfloat16)
    values = (joined[:, :, :, 2] + bias_pair[:, 1]).astype(jnp.bfloat16)
    mixed, log_total = lax.map(
        partial(attend_forward, slopes=slopes, block=block), (query, keys, values, segments)
    )
    mixed = mixed.reshape(rows_total, local_heads * head_dim)
    attn_part = lax.psum_scatter(
        jnp.dot(
            lax.slice_in_dim(mixed, 0, local_rows * lax.axis_size("tensor"), axis=0),
            w_out,
            preferred_element_type=jnp.float32,
        ).astype(jnp.bfloat16),
        "tensor",
        scatter_dimension=0,
        tiled=True,
    ).astype(jnp.float32)
    resid = source + attn_part + b_out.astype(jnp.float32)
    normed_two = layer_norm(resid, gain_two_f, shift_two_f).astype(jnp.bfloat16)
    rows_two = lax.all_gather(normed_two, "tensor", axis=0, tiled=True)
    pre_act = jnp.dot(rows_two, w_up, preferred_element_type=jnp.float32) + b_up.astype(jnp.float32)
    hidden = jax.nn.gelu(pre_act, approximate=True).astype(jnp.bfloat16)
    mlp_part = lax.psum_scatter(
        jnp.dot(
            lax.slice_in_dim(hidden, 0, local_rows * lax.axis_size("tensor"), axis=0),
            w_down,
            preferred_element_type=jnp.float32,
        ).astype(jnp.bfloat16),
        "tensor",
        scatter_dimension=0,
        tiled=True,
    ).astype(jnp.float32)
    layer_out = resid + mlp_part + b_down.astype(jnp.float32)
    piece = lax.all_gather(cotangent, "tensor", axis=0, tiled=True)
    start = jnp.int32(0)
    grad_down = jnp.zeros((hidden.shape[1], cotangent.shape[1]), jnp.float32)
    grad_hidden = jnp.zeros(hidden.shape, jnp.float32)
    grad_down = grad_down + contract_rows(
        lax.dynamic_slice_in_dim(hidden, start, piece.shape[0], 0), piece
    )
    grad_hidden = lax.dynamic_update_slice_in_dim(
        grad_hidden, contract_cols(piece, w_down), start, 0
    )
    grad_down, grad_hidden = (grad_down, grad_hidden)
    unused, gelu_pull = jax.vjp(partial(jax.nn.gelu, approximate=True), pre_act)
    grad_pre = gelu_pull(grad_hidden)[0].astype(jnp.bfloat16)
    grad_up = contract_rows(rows_two, grad_pre)
    grad_b_up = jnp.sum(grad_pre.astype(jnp.float32), axis=0)
    grad_normed_two = lax.psum_scatter(
        contract_cols(
            lax.slice_in_dim(grad_pre, 0, local_rows * lax.axis_size("tensor"), axis=0), w_up
        ).astype(jnp.bfloat16),
        "tensor",
        scatter_dimension=0,
        tiled=True,
    ).astype(jnp.float32)
    unused, norm_two_pull = jax.vjp(layer_norm, resid, gain_two_f, shift_two_f)
    grad_resid_norm, grad_gain_two, grad_shift_two = norm_two_pull(grad_normed_two)
    seed = cotangent.astype(jnp.float32)
    grad_resid = seed + grad_resid_norm
    branch_grad = grad_resid.astype(jnp.bfloat16)
    piece = lax.all_gather(branch_grad, "tensor", axis=0, tiled=True)
    start = jnp.int32(0)
    grad_out = jnp.zeros((mixed.shape[1], branch_grad.shape[1]), jnp.float32)
    grad_mixed = jnp.zeros(mixed.shape, jnp.float32)
    grad_out = grad_out + contract_rows(
        lax.dynamic_slice_in_dim(mixed, start, piece.shape[0], 0), piece
    )
    grad_mixed = lax.dynamic_update_slice_in_dim(grad_mixed, contract_cols(piece, w_out), start, 0)
    grad_out, grad_mixed = (grad_out, grad_mixed)
    grad_mixed = grad_mixed.astype(jnp.bfloat16).reshape(count, length, local_heads, head_dim)
    grad_joined = lax.map(
        partial(attend_backward, slopes=slopes, block=block),
        (query, keys, values, segments, log_total, grad_mixed),
    )
    grad_joined = grad_joined.reshape(rows_total, local_heads, 3, head_dim)
    grad_b_qv = jnp.sum(grad_joined[:, :, 0::2].astype(jnp.float32), axis=0).reshape(-1)
    grad_joined = grad_joined.reshape(rows_total, local_heads * 3 * head_dim)
    grad_qkv = contract_rows(rows_one, grad_joined)
    grad_normed_one = lax.psum_scatter(
        contract_cols(
            lax.slice_in_dim(grad_joined, 0, local_rows * lax.axis_size("tensor"), axis=0), w_qkv
        ).astype(jnp.bfloat16),
        "tensor",
        scatter_dimension=0,
        tiled=True,
    ).astype(jnp.float32)
    unused, norm_one_pull = jax.vjp(layer_norm, source, gain_one_f, shift_one_f)
    grad_source, grad_gain_one, grad_shift_one = norm_one_pull(grad_normed_one)
    input_grad = (grad_resid + grad_source).astype(jnp.bfloat16)
    sum_qkv, sum_out, sum_up, sum_down = (
        lax.psum_scatter(
            grad_qkv.astype(jnp.bfloat16), "dp", scatter_dimension=0, tiled=True
        ).astype(jnp.float32),
        lax.psum_scatter(
            grad_out.astype(jnp.bfloat16), "dp", scatter_dimension=1, tiled=True
        ).astype(jnp.float32),
        lax.psum_scatter(
            grad_up.astype(jnp.bfloat16), "dp", scatter_dimension=0, tiled=True
        ).astype(jnp.float32),
        lax.psum_scatter(
            grad_down.astype(jnp.bfloat16), "dp", scatter_dimension=1, tiled=True
        ).astype(jnp.float32),
    )
    small = lax.psum(
        (
            grad_gain_one,
            grad_shift_one,
            jnp.sum(grad_resid, axis=0),
            grad_gain_two,
            grad_shift_two,
            jnp.sum(seed, axis=0),
            spread_slots(grad_b_qv, rank, parts),
            spread_slots(grad_b_up, rank, parts),
        ),
        ("dp", "tensor"),
    )
    qv_width = grad_b_qv.shape[0]
    up_width = grad_b_up.shape[0]
    sum_qv = lax.dynamic_slice_in_dim(small[6], rank * qv_width, qv_width)
    sum_bias_up = lax.dynamic_slice_in_dim(small[7], rank * up_width, up_width)
    return (
        layer_out.astype(jnp.bfloat16),
        input_grad,
        sum_qkv,
        sum_qv,
        sum_out,
        small[2],
        sum_up,
        sum_bias_up,
        sum_down,
        small[5],
        small[0],
        small[1],
        small[3],
        small[4],
    )


PIECE = 512
STRIP = 512
CROSS = [(0, 1), (1, 0)]


def flip_pairs(bit):
    return [(d, d ^ bit) for d in range(16)]


def flip(value, bit):
    return lax.ppermute(value, "dp", flip_pairs(bit))


def cross(value):
    return lax.ppermute(value, "tensor", CROSS)


def barrier(*values):
    return lax.optimization_barrier(values)


def nt(left, right):
    return lax.dot_general(
        left, right, (((1,), (1,)), ((), ())), preferred_element_type=jnp.float32
    )


def nn(left, right):
    return lax.dot_general(
        left, right, (((1,), (0,)), ((), ())), preferred_element_type=jnp.float32
    )


def tn(left, right):
    return lax.dot_general(
        left, right, (((0,), (0,)), ((), ())), preferred_element_type=jnp.float32
    )


def both_halves(mine_ref, other_ref, rank, lanes):
    mine, other = mine_ref[:, lanes], other_ref[:, lanes]
    first = jnp.where(rank == 0, mine, other)
    return jnp.concatenate([first, jnp.where(rank == 0, other, mine)], axis=0)


def scores_of(keys, rows, slope, seg_col, seg_row, first, size):
    part = nt(keys, rows)
    place = lax.broadcasted_iota(jnp.int32, (keys.shape[0], 1), 0)
    part = part + (place - first).astype(jnp.float32) * slope
    same = seg_col[: keys.shape[0]] == seg_row
    shape = (size, size)
    ahead = lax.broadcasted_iota(jnp.int32, shape, 0) <= lax.broadcasted_iota(jnp.int32, shape, 1)
    diag = jnp.where(same[first:] & ahead, part[first:], masked_fill)
    if first == 0:
        return [diag]
    return [jnp.where(same[:first], part[:first], masked_fill), diag]


def attend_kernel(
    side, rank_ref, slope_ref, mine_ref, other_ref, col_ref, row_ref, mixed_ref, total_ref
):
    pair = pl.program_id(0)
    rank = rank_ref[0]
    half = mine_ref.shape[0]
    size = min(PIECE, half)
    query_ref = (mine_ref, other_ref)[side]
    seg_col = col_ref[...]

    def rows_of(first_row):
        for head in range(2):
            at = head * 3 * HEAD_DIM
            keys = both_halves(mine_ref, other_ref, rank, slice(at + HEAD_DIM, at + 2 * HEAD_DIM))
            values = both_halves(
                mine_ref, other_ref, rank, slice(at + 2 * HEAD_DIM, at + 3 * HEAD_DIM)
            )
            slope = slope_ref[2 * pair + head]
            for near in range(0, half, size):
                first = first_row + near
                stop = first + size
                rows = query_ref[near : near + size, at : at + HEAD_DIM]
                rows = rows * jnp.bfloat16(HEAD_DIM**-0.5)
                parts = scores_of(
                    keys[:stop], rows, slope, seg_col, row_ref[:, first:stop], first, size
                )
                top = jnp.max(parts[-1], axis=0, keepdims=True)
                if len(parts) > 1:
                    top = jnp.maximum(top, jnp.max(parts[0], axis=0, keepdims=True))
                weights = [jnp.exp(part - top) for part in parts]
                total = sum(jnp.sum(part, axis=0, keepdims=True) for part in weights)
                weights = [part.astype(jnp.bfloat16) for part in weights]
                weights = jnp.concatenate(weights, axis=0) if len(weights) > 1 else weights[0]
                out = tn(values[:stop], weights) * (1.0 / total)
                mixed_ref[near : near + size, head * HEAD_DIM : (head + 1) * HEAD_DIM] = (
                    out.T.astype(jnp.bfloat16)
                )
                total_ref[0, head : head + 1, near : near + size] = top + jnp.log(total)

    for number in range(2):

        @pl.when(rank == (number if side == 0 else 1 - number))
        def _():
            rows_of(number * half)


def attend_back_kernel(
    core_ref,
    slope_ref,
    mine_ref,
    other_ref,
    grad_mine_ref,
    grad_other_ref,
    mixed_mine_ref,
    mixed_other_ref,
    total_mine_ref,
    total_other_ref,
    col_ref,
    row_ref,
    out_ref,
    sums_ref,
    probs_ref,
    deltas_ref,
):
    pair = pl.program_id(0)
    core = core_ref[0]
    half = mine_ref.shape[0]
    length = 2 * half
    size = min(PIECE, half)
    scale = HEAD_DIM**-0.5
    seg_col = col_ref[...]
    totals = [total_mine_ref[0], total_other_ref[0]]
    totals = [
        jnp.where(core == 0, totals[0], totals[1]),
        jnp.where(core == 0, totals[1], totals[0]),
    ]
    sums = []
    for head in range(2):
        at = head * 3 * HEAD_DIM
        keys = both_halves(mine_ref, other_ref, core, slice(at + HEAD_DIM, at + 2 * HEAD_DIM))
        values = both_halves(mine_ref, other_ref, core, slice(at + 2 * HEAD_DIM, at + 3 * HEAD_DIM))
        query = both_halves(mine_ref, other_ref, core, slice(at, at + HEAD_DIM)) * jnp.bfloat16(scale)
        grads = both_halves(
            grad_mine_ref, grad_other_ref, core, slice(head * HEAD_DIM, (head + 1) * HEAD_DIM)
        )
        outs = both_halves(
            mixed_mine_ref, mixed_other_ref, core, slice(head * HEAD_DIM, (head + 1) * HEAD_DIM)
        )
        inner = grads.astype(jnp.float32) * outs.astype(jnp.float32)
        inner = jnp.sum(inner.T, axis=0, keepdims=True)
        slope = slope_ref[2 * pair + head]
        query_sum = jnp.zeros((1, HEAD_DIM), jnp.float32)
        value_sum = jnp.zeros((1, HEAD_DIM), jnp.float32)
        for first in range(0, length, size):
            side = core if first < half else 1 - core
            rows_at = slice(first % half, first % half + size)
            stop = first + size
            parts = scores_of(
                keys[:stop], query[first:stop], slope, seg_col, row_ref[:, first:stop], first, size
            )
            log_total = totals[first // half][head : head + 1, rows_at]
            grad_probs = nt(values[:stop], grads[first:stop])
            probs = [jnp.exp(part - log_total) for part in parts]
            if len(probs) > 1:
                probs = jnp.concatenate(probs, axis=0)
            else:
                probs = probs[0]
            deltas = (probs * (grad_probs - inner[:, first:stop])).astype(jnp.bfloat16)
            probs_ref[:stop, first:stop] = probs.astype(jnp.bfloat16)
            deltas_ref[:stop, first:stop] = deltas
            grad_query = (tn(keys[:stop], deltas).T * scale).astype(jnp.bfloat16)
            query_sum = query_sum + jnp.sum(
                grad_query.astype(jnp.float32), axis=0, keepdims=True
            )
            out_ref[side, rows_at, at : at + HEAD_DIM] = grad_query
        for first in range(0, length, size):
            side = core if first < half else 1 - core
            rows_at = slice(first % half, first % half + size)
            stop = first + size
            grad_keys = nn(deltas_ref[first:stop, first:], query[first:]).astype(jnp.bfloat16)
            grad_values = nn(probs_ref[first:stop, first:], grads[first:]).astype(jnp.bfloat16)
            value_sum = value_sum + jnp.sum(
                grad_values.astype(jnp.float32), axis=0, keepdims=True
            )
            out_ref[side, rows_at, at + HEAD_DIM : at + 2 * HEAD_DIM] = grad_keys
            out_ref[side, rows_at, at + 2 * HEAD_DIM : at + 3 * HEAD_DIM] = grad_values
        sums += [query_sum, value_sum]
    sums_ref[0] = jnp.concatenate(sums, axis=1)


def attend(rank, slopes, mine, other, seg_col, seg_row, side):
    half = mine.shape[0]
    heads = slopes.shape[0]
    pairs = heads // 2
    length = 2 * half
    joined = pl.BlockSpec((half, 6 * HEAD_DIM), lambda p, c, s: (0, p))
    return pl.pallas_call(
        partial(attend_kernel, side),
        grid_spec=pltpu.PrefetchScalarGridSpec(
            num_scalar_prefetch=2,
            grid=(pairs,),
            in_specs=[
                joined,
                joined,
                pl.BlockSpec((length, 1), lambda p, c, s: (0, 0)),
                pl.BlockSpec((1, length), lambda p, c, s: (0, 0)),
            ],
            out_specs=[
                pl.BlockSpec((half, 2 * HEAD_DIM), lambda p, c, s: (0, p)),
                pl.BlockSpec((1, 2, half), lambda p, c, s: (p, 0, 0)),
            ],
        ),
        out_shape=[
            jax.ShapeDtypeStruct((half, heads * HEAD_DIM), jnp.bfloat16),
            jax.ShapeDtypeStruct((pairs, 2, half), jnp.float32),
        ],
        compiler_params=pltpu.CompilerParams(vmem_limit_bytes=20 * 2**20),
        cost_estimate=free(),
        name="attend_forward",
    )(rank, slopes, mine, other, seg_col, seg_row)


def attend_back(rank, slopes, mine, other, grads, outs, totals, seg_col, seg_row, start, pairs):
    half = mine.shape[0]
    length = 2 * half
    joined = pl.BlockSpec((half, 6 * HEAD_DIM), lambda p, c, s: (0, p + start))
    mixed = pl.BlockSpec((half, 2 * HEAD_DIM), lambda p, c, s: (0, p + start))
    return pl.pallas_call(
        attend_back_kernel,
        grid_spec=pltpu.PrefetchScalarGridSpec(
            num_scalar_prefetch=2,
            grid=(pairs,),
            in_specs=[
                joined,
                joined,
                mixed,
                mixed,
                mixed,
                mixed,
                pl.BlockSpec((1, 2, half), lambda p, c, s: (p + start, 0, 0)),
                pl.BlockSpec((1, 2, half), lambda p, c, s: (p + start, 0, 0)),
                pl.BlockSpec((length, 1), lambda p, c, s: (0, 0)),
                pl.BlockSpec((1, length), lambda p, c, s: (0, 0)),
            ],
            out_specs=[
                pl.BlockSpec((2, half, 6 * HEAD_DIM), lambda p, c, s: (0, 0, p)),
                pl.BlockSpec((1, 1, 4 * HEAD_DIM), lambda p, c, s: (p, 0, 0)),
            ],
            scratch_shapes=[
                pltpu.VMEM((length, length), jnp.bfloat16),
                pltpu.VMEM((length, length), jnp.bfloat16),
            ],
        ),
        out_shape=[
            jax.ShapeDtypeStruct((2, half, pairs * 6 * HEAD_DIM), jnp.bfloat16),
            jax.ShapeDtypeStruct((pairs, 1, 4 * HEAD_DIM), jnp.float32),
        ],
        compiler_params=pltpu.CompilerParams(vmem_limit_bytes=20 * 2**20),
        cost_estimate=free(),
        name="attend_backward",
    )(rank, slopes[2 * start :], mine, other, *grads, *outs, *totals, seg_col, seg_row)


def free():
    return pl.CostEstimate(flops=1000, bytes_accessed=1000, transcendentals=0)


def gelu_parts(v):
    rate, bend = 0.7978845608028654, 0.044715
    square = v * v
    t = 0.5 + 0.5 * jnp.tanh(v * (rate + (rate * bend) * square))
    turn = v * (2.0 * rate + (6.0 * rate * bend) * square)
    return v * t, t * (1.0 + turn * (1.0 - t))


def up_kernel(rows_ref, weight_ref, bias_ref, act_ref, slope_ref):
    rows = rows_ref[...]
    for at in range(0, act_ref.shape[1], STRIP):
        strip = slice(at, at + STRIP)
        act, slope = gelu_parts(nn(rows, weight_ref[:, strip]) + bias_ref[:, strip])
        act_ref[:, strip] = act.astype(act_ref.dtype)
        slope_ref[:, strip] = slope.astype(slope_ref.dtype)


def pull_kernel(rows_ref, weight_ref, slope_ref, out_ref, sum_ref):
    rows = rows_ref[...]

    @pl.when(pl.program_id(0) == 0)
    def _():
        sum_ref[...] = jnp.zeros_like(sum_ref)

    for at in range(0, out_ref.shape[1], STRIP):
        strip = slice(at, at + STRIP)
        value = nt(rows, weight_ref[strip, :]) * slope_ref[:, strip].astype(jnp.float32)
        grads = value.astype(jnp.bfloat16)
        out_ref[:, strip] = grads
        sum_ref[:, strip] += jnp.sum(grads.astype(jnp.float32), axis=0, keepdims=True)


def units_call(kernel, name, rows, weight, third, wide, outs, tile=256):
    by_rows = pl.BlockSpec((tile, wide), lambda i: (i, 0))
    whole = pl.BlockSpec((1, wide), lambda i: (0, 0))
    specs = {rows.shape[0]: by_rows, 1: whole}
    return pl.pallas_call(
        kernel,
        grid=(rows.shape[0] // tile,),
        in_specs=[
            pl.BlockSpec((tile, rows.shape[1]), lambda i: (i, 0)),
            pl.BlockSpec(weight.shape, lambda i: (0, 0)),
            specs[third.shape[0]],
        ],
        out_specs=[specs[out.shape[0]] for out in outs],
        out_shape=outs,
        compiler_params=pltpu.CompilerParams(vmem_limit_bytes=28 * 2**20),
        cost_estimate=free(),
        name=name,
    )(rows, weight, third)


def outer_kernel(core_ref, mine_ref, other_ref, right_mine, right_other, kept_ref, send_ref, turned):
    half = mine_ref.shape[0]
    count = kept_ref.shape[0]
    size = kept_ref.shape[1]

    @pl.when(pl.program_id(0) == 0)
    def _():
        for part, ref in enumerate((mine_ref, other_ref)):
            value = ref[...].T
            for block in range(2 * count):
                to = ((block % 2) * count + block // 2) * size
                turned[to : to + size, part * half : (part + 1) * half] = value[
                    block * size : (block + 1) * size
                ]

    value = nn(turned[:, :half], right_mine[...]) + nn(turned[:, half:], right_other[...])
    value = value.astype(kept_ref.dtype).reshape(2, count, size, value.shape[1])

    @pl.when(core_ref[0] == 0)
    def _():
        kept_ref[...] = value[0]
        send_ref[...] = value[1]

    @pl.when(core_ref[0] != 0)
    def _():
        kept_ref[...] = value[1]
        send_ref[...] = value[0]


def outer(core, lefts, rights):
    half, deep = lefts[0].shape
    if len(rights) == 1:
        rights, below = rights * 2, 1
    else:
        below = 0
    wide = rights[0].shape[1]
    tile = next(t for t in (512, 384, 256, 128) if wide % t == 0)
    out = pl.BlockSpec((8, deep // 16, tile), lambda n, c: (0, 0, n))
    return pl.pallas_call(
        outer_kernel,
        grid_spec=pltpu.PrefetchScalarGridSpec(
            num_scalar_prefetch=1,
            grid=(wide // tile,),
            in_specs=[
                pl.BlockSpec((half, deep), lambda n, c: (0, 0)),
                pl.BlockSpec((half, deep), lambda n, c: (0, 0)),
                pl.BlockSpec((half, tile), lambda n, c: (0, n)),
                pl.BlockSpec((half, tile), lambda n, c: (below, n)),
            ],
            out_specs=[out, out],
            scratch_shapes=[pltpu.VMEM((deep, 2 * half), jnp.bfloat16)],
        ),
        out_shape=[jax.ShapeDtypeStruct((8, deep // 16, wide), jnp.bfloat16)] * 2,
        compiler_params=pltpu.CompilerParams(vmem_limit_bytes=18 * 2**20),
        cost_estimate=free(),
        name="matmul_outer",
    )(core, *lefts, *rights)


def rows_call(body, name, operands, vectors, outs, sums=0, tile=128):
    rows, wide = operands[0].shape
    by_rows = pl.BlockSpec((tile, wide), lambda i: (i, 0))
    whole = pl.BlockSpec((1, wide), lambda i: (0, 0))
    shapes = [jax.ShapeDtypeStruct((rows, wide), kind) for kind in outs]
    shapes += [jax.ShapeDtypeStruct((1, wide), jnp.float32)] * sums
    count = len(operands) + len(vectors)

    def kernel(*refs):
        values = [ref[...].astype(jnp.float32) for ref in refs[:count]]
        results, totals = body(*values)
        for ref, value in zip(refs[count:], results):
            ref[...] = value.astype(ref.dtype)
        for ref, value in zip(refs[count + len(outs) :], totals):
            part = jnp.sum(value, axis=0, keepdims=True)
            ref[...] = jnp.where(pl.program_id(0) == 0, part, ref[...] + part)

    return pl.pallas_call(
        kernel,
        grid=(rows // tile,),
        in_specs=[by_rows] * len(operands) + [whole] * len(vectors),
        out_specs=[by_rows] * len(outs) + [whole] * sums,
        out_shape=shapes,
        compiler_params=pltpu.CompilerParams(vmem_limit_bytes=16 * 2**20),
        cost_estimate=free(),
        name=name,
    )(*operands, *[v.reshape(1, wide) for v in vectors])


def first_norm(source, gain, shift):
    return (layer_norm(source, gain, shift),), ()


def join_norm(source, mine, came, bias, gain, shift):
    resid = source + mine + came + bias
    return (resid, layer_norm(resid, gain, shift)), ()


def join_out(resid, mine, came, bias):
    return (resid + mine + came + bias,), ()


def norm_two_back(resid, mine, came, seed, gain):
    grads = mine + came
    hat, inverse = norm_parts(resid)
    scaled = grads * gain
    out = seed + inverse * (
        scaled
        - jnp.mean(scaled, axis=-1, keepdims=True)
        - hat * jnp.mean(scaled * hat, axis=-1, keepdims=True)
    )
    return (out,), (grads * hat, grads, out, seed)


def norm_one_back(source, mine, came, resid_grad, gain):
    grads = mine + came
    hat, inverse = norm_parts(source)
    scaled = grads * gain
    out = resid_grad + inverse * (
        scaled
        - jnp.mean(scaled, axis=-1, keepdims=True)
        - hat * jnp.mean(scaled * hat, axis=-1, keepdims=True)
    )
    return (out,), (grads * hat, grads)


def norm_parts(values):
    row_mean = jnp.mean(values, axis=-1, keepdims=True)
    centered = values - row_mean
    row_var = jnp.mean(centered * centered, axis=-1, keepdims=True)
    inverse = lax.rsqrt(row_var + norm_eps)
    return centered * inverse, inverse


def fold_kernel(widths, came, which_ref, *refs):
    count = len(widths)
    step = 2 if came else 1
    ins, (kept_ref, send_ref) = refs[:-2], refs[-2:]
    for out_ref, side in ((kept_ref, 0), (send_ref, 1)):
        at = 0
        for number, wide in enumerate(widths):
            first = (side * count + number) * step
            value = ins[first][...]
            if came:
                value = value.astype(jnp.float32) + ins[first + 1][...].astype(jnp.float32)
            out_ref[:, :, at : at + wide] = value.astype(out_ref.dtype)
            at += wide


def fold(which, *terms):
    widths = [kept.shape[2] for kept, _ in terms]
    blocks, size = terms[0][0].shape[:2]
    came = terms[0][1] is not None
    specs, operands = [], []
    for side in range(2):
        for (kept, other), wide in zip(terms, widths):

            def at(i, w, side=side):
                return (2 * i + (w[0] if side == 0 else 1 - w[0]), 0, 0)

            for value in (kept, other) if came else (kept,):
                specs.append(pl.BlockSpec((1, size, wide), at))
                operands.append(value)
    out = pl.BlockSpec((1, size, sum(widths)), lambda i, w: (i, 0, 0))
    return pl.pallas_call(
        partial(fold_kernel, widths, came),
        grid_spec=pltpu.PrefetchScalarGridSpec(
            num_scalar_prefetch=1,
            grid=(blocks // 2,),
            in_specs=specs,
            out_specs=[out, out],
        ),
        out_shape=[jax.ShapeDtypeStruct((blocks // 2, size, sum(widths)), jnp.bfloat16)] * 2,
        compiler_params=pltpu.CompilerParams(vmem_limit_bytes=16 * 2**20),
        cost_estimate=free(),
        name="fold_halves",
    )(which.astype(jnp.int32).reshape(1), *operands)


def sum_everywhere(value):
    value = value + cross(value)
    for bit in (1, 2, 4, 8):
        value = value + flip(value, bit)
    return value


def chip_body(
    tokens,
    segments,
    w_qkv,
    b_qv,
    w_out,
    b_out,
    w_up,
    b_up,
    w_down,
    b_down,
    gain_one,
    shift_one,
    gain_two,
    shift_two,
    cotangent,
):
    f32, bf16 = jnp.float32, jnp.bfloat16
    place = lax.axis_index("dp")
    rank = lax.axis_index("tensor")
    core, y_at, z_low, z_high = place % 2, (place // 2) % 2, (place // 4) % 2, place // 8
    core_s = core.astype(jnp.int32).reshape(1)
    rank_s = rank.astype(jnp.int32).reshape(1)
    half, width = tokens.shape
    length = segments.shape[1]
    heads = w_qkv.shape[1] // (3 * HEAD_DIM)
    units = w_up.shape[1]
    seg_col = segments.reshape(length, 1)
    head_index = rank * heads + lax.iota(jnp.int32, heads)
    slopes = 2.0 ** (-8.0 * (head_index + 1).astype(f32) / HEADS)

    (normed,) = rows_call(first_norm, "first_norm", [tokens], [gain_one, shift_one], [bf16])
    normed_came = cross(normed)
    pair = b_qv.astype(f32).reshape(heads, 2, HEAD_DIM)
    bias = jnp.stack([pair[:, 0], jnp.zeros_like(pair[:, 0]), pair[:, 1]], axis=1).reshape(-1)

    def project(rows):
        return (jnp.dot(rows, w_qkv, preferred_element_type=f32) + bias).astype(bf16)

    seed_came = cross(cotangent)
    joined = [project(normed)]
    joined[0], normed_came = barrier(joined[0], normed_came)
    joined.append(project(normed_came))
    attend_args = (rank_s, slopes, *joined, seg_col, segments)
    mixed_other, totals_other = attend(*attend_args, 1)
    sent = jnp.dot(mixed_other, w_out, preferred_element_type=f32).astype(bf16)
    came = cross(sent)
    sent, *attend_args = barrier(sent, *attend_args)
    mixed_mine, totals_mine = attend(*attend_args, 0)
    mixed, totals = [mixed_mine, mixed_other], [totals_mine, totals_other]
    mine = jnp.dot(mixed_mine, w_out, preferred_element_type=f32).astype(bf16)
    mine, came, seed_came = barrier(mine, came, seed_came)
    resid, normed_two = rows_call(
        join_norm, "join_norm", [tokens, mine, came], [b_out, gain_two, shift_two], [f32, bf16]
    )
    two_came = cross(normed_two)
    wide = jax.ShapeDtypeStruct((half, units), bf16)
    b_up_f = b_up.astype(f32).reshape(1, units)

    def lift(rows):
        return units_call(up_kernel, "matmul_up", rows, w_up, b_up_f, units, [wide] * 2)

    act_mine, slope_mine = lift(normed_two)

    sums = jax.ShapeDtypeStruct((1, units), f32)

    def pull(rows, slope):
        return units_call(pull_kernel, "matmul_pull", rows, w_down, slope, units, [wide, sums])

    grad_mine, sum_mine = pull(cotangent, slope_mine)
    down_mine = jnp.dot(act_mine, w_down, preferred_element_type=f32).astype(bf16)
    two_came, down_mine, grad_mine = barrier(two_came, down_mine, grad_mine)
    act_other, slope_other = lift(two_came)
    grad_other, sum_other = pull(seed_came, slope_other)
    grad_b_up = (sum_mine + sum_other)[0]
    sent = contract_cols(grad_other, w_up).astype(bf16)
    came = cross(sent)
    sent, act_mine, act_other, grad_mine, grad_other = barrier(
        sent, act_mine, act_other, grad_mine, grad_other
    )
    down_kept, down_send = outer(core_s, [cotangent, seed_came], [act_mine, act_other])
    up_kept, up_send = outer(core_s, [normed_two, two_came], [grad_mine, grad_other])
    mine = contract_cols(grad_mine, w_up).astype(bf16)
    came, mine, up_send, down_send = barrier(came, mine, up_send, down_send)
    down_came = flip(down_send, 1)
    up_came = flip(up_send, 1)
    branch, grad_gain_two, grad_shift_two, sum_resid, sum_seed = rows_call(
        norm_two_back, "norm_two_back", [resid, mine, came, cotangent], [gain_two], [bf16], 4
    )
    branch_came = cross(branch)
    branch, down_came, up_came = barrier(branch, down_came, up_came)
    ff_kept, ff_send = fold(y_at, (down_kept, down_came), (up_kept, up_came))
    down_sent = jnp.dot(act_other, w_down, preferred_element_type=f32).astype(bf16)
    ff_came = flip(ff_send, 2)
    ff_send, branch_b = barrier(ff_send, branch)
    grad_mixed = [contract_cols(branch_b, w_out).astype(bf16)]
    grad_mixed[0], branch_came, down_sent = barrier(grad_mixed[0], branch_came, down_sent)
    grad_mixed.append(contract_cols(branch_came, w_out).astype(bf16))

    grad_mixed[1], down_sent = barrier(grad_mixed[1], down_sent)
    out_came = cross(down_sent)
    outs = list(mixed)
    pairs = heads // 4
    back_one, sums_one = attend_back(
        rank_s, slopes, *joined, grad_mixed, outs, totals, seg_col, segments, 0, pairs
    )
    back_one, branch_came, mixed[0] = barrier(
        back_one.reshape(length, -1), branch_came, mixed[0]
    )
    one_kept, one_send = outer(core_s, [normed, normed_came], [back_one])
    one_came = flip(one_send, 1)
    proj_kept, proj_send = outer(core_s, [branch, branch_came], mixed)
    proj_came = flip(proj_send, 1)
    proj_send, ff_came = barrier(proj_send, ff_came)
    ff_kept, ff_send = fold(z_low, (ff_kept, ff_came))
    ff_came = flip(ff_send, 4)
    a_kept, a_send = fold(y_at, (one_kept, one_came), (proj_kept, proj_came))
    a_came = flip(a_send, 2)
    joined[1], a_send, ff_send = barrier(joined[1], a_send, ff_send)
    back_two, sums_two = attend_back(
        rank_s, slopes, *joined, grad_mixed, outs, totals, seg_col, segments, pairs, pairs
    )
    back_two = back_two.reshape(length, -1)
    back_two, a_came, out_came = barrier(back_two, a_came, out_came)
    cut = back_one.shape[1]

    def to_rows(rows):
        return (
            contract_cols(back_one[rows], w_qkv[:, :cut])
            + contract_cols(back_two[rows], w_qkv[:, cut:])
        ).astype(bf16)

    sent = to_rows(slice(half, None))
    came = cross(sent)
    back_two, sent = barrier(back_two, sent)
    two_kept, two_send = outer(core_s, [normed, normed_came], [back_two])
    b_came = flip(two_send, 1)
    two_send, ff_came, a_came = barrier(two_send, ff_came, a_came)
    a_kept, a_send = fold(z_low, (a_kept, a_came))
    a_came = flip(a_send, 4)
    ff_kept, ff_send = fold(z_high, (ff_kept, ff_came))
    ff_came = flip(ff_send, 8)
    ff_send, b_came = barrier(ff_send, b_came)
    b_kept, b_send = fold(y_at, (two_kept, b_came))
    b_came = flip(b_send, 2)
    mine = to_rows(slice(0, half))
    mine, b_came = barrier(mine, b_came)
    b_kept, b_send = fold(z_low, (b_kept, b_came))
    b_came = flip(b_send, 4)
    b_send, a_came = barrier(b_send, a_came)
    t_kept, t_send = fold(z_high, (a_kept, a_came), (b_kept, b_came))
    t_came = flip(t_send, 8)
    t_send, came = barrier(t_send, came)
    input_grad, grad_gain_one, grad_shift_one = rows_call(
        norm_one_back, "norm_one_back", [tokens, mine, came, branch], [gain_one], [bf16], 2
    )
    grad_gain_one, down_mine = barrier(grad_gain_one, down_mine)
    (layer_out,) = rows_call(join_out, "join_out", [resid, down_mine, out_came], [b_down], [bf16])

    def last(kept, came):
        return (kept.astype(f32) + came.astype(f32))[0]

    sum_ff = last(ff_kept, ff_came)
    sum_down, sum_up = sum_ff[:, :units].T, sum_ff[:, units:]
    sum_rest = last(t_kept, t_came)
    split = cut + w_out.shape[0]
    sum_qkv = jnp.concatenate([sum_rest[:, :cut], sum_rest[:, split:]], axis=1)
    sum_out = sum_rest[:, cut:split].T
    qv_sums = jnp.concatenate([sums_one.reshape(-1), sums_two.reshape(-1)])
    small = sum_everywhere(
        jnp.concatenate(
            [
                sum_resid[0],
                grad_gain_two[0],
                grad_shift_two[0],
                sum_seed[0],
                grad_gain_one[0],
                grad_shift_one[0],
                spread_slots(grad_b_up, rank, 2),
                spread_slots(qv_sums, rank, 2),
            ]
        )
    )
    up_width = grad_b_up.shape[0]
    qv_width = b_qv.shape[0]
    up_from, qv_from = 6 * width, 6 * width + 2 * up_width
    sum_b_up = lax.dynamic_slice_in_dim(small, up_from + rank * up_width, up_width)
    sum_b_qv = lax.dynamic_slice_in_dim(small, qv_from + rank * qv_width, qv_width)
    rows = [small[i * width : (i + 1) * width] for i in range(6)]
    return (
        layer_out,
        input_grad,
        sum_qkv,
        sum_b_qv,
        sum_out,
        rows[0],
        sum_up,
        sum_b_up,
        sum_down,
        rows[3],
        rows[4],
        rows[5],
        rows[1],
        rows[2],
    )


def solution(mesh):
    in_specs = (
        P(("dp", "tensor"), None),
        P("dp", None),
        P(None, "tensor"),
        P("tensor"),
        P("tensor", None),
        P(),
        P(None, "tensor"),
        P("tensor"),
        P("tensor", None),
        P(),
        P(),
        P(),
        P(),
        P(),
        P(("dp", "tensor"), None),
    )
    out_specs = (
        P(("dp", "tensor"), None),
        P(("dp", "tensor"), None),
        P("dp", "tensor"),
        P("tensor"),
        P("tensor", "dp"),
        P(),
        P("dp", "tensor"),
        P("tensor"),
        P("tensor", "dp"),
        P(),
        P(),
        P(),
        P(),
        P(),
    )
    pairs = mesh.shape["tensor"] == 2 and mesh.shape["dp"] == 16
    plan = chip_body if pairs else body
    return jax.shard_map(plan, mesh=mesh, in_specs=in_specs, out_specs=out_specs, check_vma=False)
```
